256 devices in a mesh: hid: 16 (over x, y), ffn: 16 (over z, core).
Axes of the slice: x: 4, y: 4, z: 8, core: 2. Of those that a mesh axis runs over, the one named last changes fastest.
Arguments:
- activations: bfloat16 [1024, 10240], P('ffn', 'hid'), may hold values from -12 to 12
- ln_gain: float32 [10240], P('hid'), may hold values from 0.1 to 1.9
- segments: int32 [1024], replicated, may hold values from 0 to 3, never falling along the last dimension, each value on 1 to 512 neighbouring positions
- w_query: bfloat16 [10240, 12288], P('hid', 'ffn'), may hold values from -0.0625 to 0.0625
- w_key_value: bfloat16 [10240, 512], P('hid'), may hold values from -0.0625 to 0.0625
- w_gate: bfloat16 [10240, 36864], P('hid', 'ffn'), may hold values from -0.0625 to 0.0625
- w_up: bfloat16 [10240, 36864], P('hid', 'ffn'), may hold values from -0.0625 to 0.0625
- w_out: bfloat16 [12288, 10240], P('ffn', 'hid'), may hold values from -0.0546875 to 0.0546875
- w_down: bfloat16 [36864, 10240], P('ffn', 'hid'), may hold values from -0.03125 to 0.03125
Outputs:
- block_out: bfloat16 [1024, 10240], P('ffn', 'hid')
The draws below stay inside these ranges and needn't reach their ends.
Inputs may be any that keep to these rules, and one draw needn't show every extreme that they name: `segments`: document numbers never fall along the tokens; each document has 1 to 512 tokens, one exactly 512.
All inputs are finite; a program needn't handle non-finite values.
Results may differ from the reference program's by a relative error of at most 0.015.
Values may be sent and summed in bfloat16 or wider, within the bound.
A program may use at most 128 MiB of HBM per device.

```python
import math
import jax
import jax.numpy as jnp
import numpy as np
from jax import lax

D = 10240
HEADS = 48
HEAD = 256
FF = 36864
TOKENS = 1024


def draw_activations(key, part):
    key = jax.random.fold_in(key, 11)
    row_key, noise_key = jax.random.split(key)
    row_level = jax.random.uniform(row_key, (TOKENS, 1), jnp.float32, -1.0, 1.0)
    ramp = jnp.arange(D).astype(jnp.float32) / D
    feature_scale = 1.0 + 3.0 * ramp
    noise = jnp.clip(jax.random.normal(noise_key, (TOKENS, D), jnp.float32), -4.0, 4.0)
    return (row_level * feature_scale[None, :] + noise).astype(jnp.bfloat16)


def block_scale(key, extent, cuts, smallest, largest):
    gain = 1.0
    for dim, blocks in cuts:
        heights = jax.random.uniform(jax.random.fold_in(jax.random.fold_in(key, 6), dim), (blocks,), jnp.float32, smallest / len(cuts), largest / len(cuts))
        gain = gain * jnp.repeat(jnp.exp(heights), extent[dim] // blocks).reshape((-1,) + (1,) * (len(extent) - 1 - dim))
    return gain


def profile(count, total, limit, slope):
    weights = [(1 << 20) // math.isqrt(rank ** slope) + 1 for rank in range(2, count + 1)]
    surplus, counts = total - limit - (count - 1), [1] * (count - 1)
    while surplus > 0:
        movable = [i for i in range(count - 1) if counts[i] < limit]
        mass, budget = sum([weights[i] for i in movable]), surplus
        for i in movable:
            more = min(limit - counts[i], max(1, budget * weights[i] // mass), surplus)
            counts[i] = counts[i] + more
            surplus = surplus - more
    return np.array([limit] + counts)


def uneven_parts(key, count, total, bound, skew):
    if count == 2:
        one = jax.random.randint(key, (), max(1, total - bound), min(bound, total - 1) + 1)
        return jnp.stack([one, total - one])
    lengths = jnp.asarray(profile(count, total, bound, skew), jnp.int32)
    couples = (count - 1) // 2
    source_of, sink = lengths[1:1 + 2 * couples:2], lengths[2:2 + 2 * couples:2]
    margin = jnp.minimum(source_of - 1, bound - sink)
    shifted = jax.random.randint(jax.random.fold_in(key, 1), (couples,), 0, 1 << 20) % (margin + 1)
    lengths = lengths.at[1:1 + 2 * couples:2].set(source_of - shifted).at[2:2 + 2 * couples:2].set(sink + shifted)
    return lengths[jax.random.permutation(jax.random.fold_in(key, 2), count)]


def centred(stream_key, dims, scale, most, pieces=(), kind=jnp.bfloat16):
    result = jax.random.normal(stream_key, dims, jnp.float32) * scale
    if len(pieces) > 0:
        result = block_scale(stream_key, dims, pieces, -0.22, 0.18) * result
    return jnp.clip(result, min=-most, max=most).astype(kind)


def setup_inputs(seed: int = 0) -> dict:
    streams_of = jax.random.split(jax.random.key(seed), 10)
    return {
        "activations": draw_activations(jax.random.fold_in(streams_of[9], 71), 0),
        "ln_gain": jnp.clip(1.0 + 0.18 * jax.random.normal(streams_of[1], (D,), jnp.float32), 0.1, 1.9),
        "segments": jnp.searchsorted(jnp.cumsum(uneven_parts(streams_of[2], 4, TOKENS, TOKENS // 2, 0)), jnp.arange(TOKENS), side="right").astype(jnp.int32),
        "w_query": centred(streams_of[3], (D, HEADS * HEAD), D ** -0.5, 0.0625, ((0, 16), (1, 16))),
        "w_key_value": centred(streams_of[4], (D, 2 * HEAD), D ** -0.5, 0.0625, ((0, 16),)),
        "w_gate": centred(streams_of[5], (D, FF), D ** -0.5, 0.0625, ((0, 16), (1, 16))),
        "w_up": centred(streams_of[6], (D, FF), D ** -0.5, 0.0625, ((0, 16), (1, 16))),
        "w_out": centred(streams_of[7], (HEADS * HEAD, D), (HEADS * HEAD) ** -0.5, 0.0546875, ((0, 16), (1, 16))),
        "w_down": centred(streams_of[8], (FF, D), FF ** -0.5, 0.03125, ((0, 16), (1, 16))),
    }


def rotate(vector, positions):
    half_width = vector.shape[-1] // 2
    frequency = 10000.0 ** (-jnp.arange(half_width, dtype=jnp.float32) / half_width)
    angles = positions[..., None] * frequency
    cosine = jnp.cos(angles)
    sine = jnp.sin(angles)
    first_half = vector[..., :half_width]
    second_half = vector[..., half_width:]
    return jnp.concatenate([first_half * cosine - second_half * sine, first_half * sine + second_half * cosine], -1)

def reference(activations, ln_gain, segments, w_query, w_key_value, w_gate, w_up, w_out, w_down):
    values_f = activations.astype(jnp.float32)
    row_mean = lax.optimization_barrier(jnp.mean(values_f, 1, keepdims=True))
    centered = values_f - row_mean
    variance = lax.optimization_barrier(jnp.mean(centered * centered, 1, keepdims=True))
    normed = (centered * lax.rsqrt(variance + 1e-06) * ln_gain.astype(jnp.float32)).astype(jnp.bfloat16)
    positions = jnp.arange(TOKENS).astype(jnp.float32)
    query_sum = jnp.dot(normed, w_query, preferred_element_type=jnp.float32).reshape(TOKENS, HEADS, HEAD)
    query = rotate(query_sum, positions[:, None]).astype(jnp.bfloat16)
    pairs = jnp.dot(normed, w_key_value, preferred_element_type=jnp.float32)
    keys = rotate(pairs[:, :HEAD], positions).astype(jnp.bfloat16)
    values = pairs[:, HEAD:].astype(jnp.bfloat16)
    scores = jnp.einsum('rhd,kd->rhk', query.astype(jnp.float32), keys.astype(jnp.float32)) * HEAD ** (-0.5)
    allowed = (positions[None, :] <= positions[:, None]) & (segments[None, :] == segments[:, None])
    expos = jnp.where(allowed[:, None, :], jnp.exp(scores), jnp.float32(0.0))
    probs = (expos / lax.optimization_barrier(jnp.sum(expos, -1, keepdims=True))).astype(jnp.bfloat16)
    attention = jnp.einsum('rhk,kd->rhd', probs.astype(jnp.float32), values.astype(jnp.float32))
    attention = attention.astype(jnp.bfloat16).reshape(TOKENS, HEADS * HEAD)
    gate = jnp.dot(normed, w_gate, preferred_element_type=jnp.float32)
    up_sum = jnp.dot(normed, w_up, preferred_element_type=jnp.float32)
    hidden = (jax.nn.silu(gate) * up_sum).astype(jnp.bfloat16)
    total = values_f + jnp.dot(attention, w_out, preferred_element_type=jnp.float32)
    total = total + jnp.dot(hidden, w_down, preferred_element_type=jnp.float32)
    return total.astype(jnp.bfloat16)
```

```python
import jax
import jax.numpy as jnp
import numpy as np
from jax import lax
from jax.experimental import pallas as pl
from jax.experimental.pallas import tpu as pltpu
from jax.sharding import PartitionSpec as P

D = 10240
HEAD = 256
TOKENS = 1024
EPSILON = 1e-06

SIDE = 4
RING = 8
GROUP = SIDE * SIDE
ROWS = TOKENS // GROUP
FEATS = D // GROUP
WIDE = 384
STEPS = 7
UNITS = 8
HALF = ROWS // 2
QUARTER = ROWS // 4
F32 = jnp.float32
BF16 = jnp.bfloat16


def tables():
    half = HEAD // 2
    frequency = np.float32(10000.0) ** (-np.arange(half, dtype=np.float32) / np.float32(half))
    angles = np.arange(TOKENS, dtype=np.float32)[:, None] * frequency[None, :].astype(np.float32)
    wide = angles.astype(np.float64)
    return np.stack([np.cos(wide), np.sin(wide)]).astype(np.float32)


def block_kernel(
    act,
    gain,
    seg,
    table,
    w_query,
    w_pairs,
    w_gate,
    w_up,
    w_out,
    w_down,
    out,
    w_in,
    w_back,
    w_kv,
    turn,
    stat,
    stat_in,
    rows_all,
    pair_part,
    pair_in,
    pair_sum,
    pair_all,
    kv_all,
    part,
    land1,
    land2,
    mixed,
    total,
    sib_out,
    sib_in,
    ring_out,
    ring_half,
    ring_in,
    w_sem,
    wb_sem,
    m_sem,
    small_s,
    small_r,
    zx_s,
    zx_r,
    zk_s,
    zk_r,
    rs_s,
    rs_r,
    ag_s,
    ag_r,
    zr_s,
    zr_r,
):
    hid = lax.axis_index("hid")
    ffn = lax.axis_index("ffn")
    x, y = hid // SIDE, hid % SIDE
    z, core = ffn // 2, ffn % 2

    def mod4(v):
        return (v + SIDE) % SIDE

    def mod8(v):
        return (v + RING) % RING

    def dev_x(d):
        return (mod4(x + d) * SIDE + y, ffn)

    def dev_y(d):
        return (x * SIDE + mod4(y + d), ffn)

    def dev_z(d):
        return (hid, mod8(z + d) * 2 + core)

    sibling = (hid, z * 2 + 1 - core)
    dirs = (1, -1)
    orders = ((x, y, dev_x, dev_y), (y, x, dev_y, dev_x))

    def remote(src, dst, ssem, rsem, dev):
        return pltpu.make_async_remote_copy(
            src_ref=src,
            dst_ref=dst,
            send_sem=ssem,
            recv_sem=rsem,
            device_id=dev,
            device_id_type=pl.DeviceIdType.MESH,
        )

    def w_copy(s, o):
        if s == 0:
            src = w_query.at[:, pl.ds(o * WIDE, WIDE)]
        else:
            src = (w_gate, w_up)[o].at[:, pl.ds((s - 1) * WIDE, WIDE)]
        return pltpu.make_async_copy(src, w_in.at[s, o], w_sem.at[s, o])

    def wb_copy(u):
        if u < 2:
            src = w_out.at[pl.ds(u * WIDE, WIDE)]
        else:
            src = w_down.at[pl.ds((u - 2) * WIDE, WIDE)]
        return pltpu.make_async_copy(src, w_back.at[u], wb_sem.at[u])

    def turn_copy(k, i):
        first = (hid if k == 0 else ffn) * ROWS
        return pltpu.make_async_copy(
            table.at[i, pl.ds(first, ROWS)], turn.at[k, i], m_sem.at[1 + 2 * k + i]
        )

    kv_copy = pltpu.make_async_copy(w_pairs, w_kv, m_sem.at[0])
    kv_copy.start()
    for k in range(2):
        for i in range(2):
            turn_copy(k, i).start()
    for s in range(STEPS):
        for o in range(2):
            w_copy(s, o).start()
    for u in range(UNITS):
        wb_copy(u).start()

    barrier = pltpu.get_barrier_semaphore()
    partners = [dev_x(d) for d in (1, 2, 3)] + [dev_y(d) for d in (1, 2, 3)]
    partners += [dev_z(1), dev_z(-1), sibling]
    for dev in partners:
        pl.semaphore_signal(barrier, inc=1, device_id=dev, device_id_type=pl.DeviceIdType.MESH)
    pl.semaphore_wait(barrier, len(partners))

    def stat_copy(a, d):
        return remote(
            stat.at[a], stat_in.at[a, d - 1], small_s.at[a, d - 1], small_r.at[a, d - 1],
            (dev_x, dev_y)[a](d),
        )

    def pair_copy(k, d):
        if k == 0:
            src, dst, dev = pair_part.at[mod4(x + d)], pair_in.at[0, d - 1], dev_x(d)
        elif k == 1:
            src, dst, dev = pair_sum, pair_in.at[1, d - 1], dev_y(d)
        else:
            src, dst, dev = pair_all.at[x], pair_all.at[x], dev_x(d)
        return remote(src, dst, small_s.at[2 + k, d - 1], small_r.at[2 + k, d - 1], dev)

    def each(fn, k, what):
        for d in (1, 2, 3):
            getattr(fn(k, d), what)()

    def z_copy(buf, sems, j, i):
        d = dirs[i]
        block = mod8(z - (j - 1) * d) * 2 + core
        ref = buf.at[block] if j < 4 else buf.at[block, pl.ds(i * HALF, HALF)]
        return remote(ref, ref, sems[0].at[j - 1, i], sems[1].at[j - 1, i], dev_z(d))

    def sib_copy(buf, sems, off):
        ref = buf.at[mod8(z + off) * 2 + core]
        row = 4 + (off + 3) // 2
        col = (off + 3) % 2
        return remote(ref, ref, sems[0].at[row, col], sems[1].at[row, col], sibling)

    def z_start(buf, sems):
        for i in range(2):
            z_copy(buf, sems, 1, i).start()
        sib_copy(buf, sems, 0).start()

    def z_step(buf, sems, j):
        if j < 4:
            for i in range(2):
                z_copy(buf, sems, j, i).wait()
                z_copy(buf, sems, j + 1, i).start()
                sib_copy(buf, sems, -j * dirs[i]).start()
        else:
            for i in range(2):
                z_copy(buf, sems, j, i).wait()
            sib_copy(buf, sems, 4).start()
            for off in (0, 1, -1, 2, -2, 3, -3, 4):
                sib_copy(buf, sems, off).wait()

    values = act[...].astype(F32)
    mean = jnp.mean(values, 1, keepdims=True)
    square = jnp.sum((values - mean) ** 2, 1, keepdims=True)
    lane = lax.broadcasted_iota(jnp.int32, (ROWS, 128), 1)
    for a, count in ((0, FEATS), (1, FEATS * SIDE)):
        stat[a] = jnp.where(lane < 64, mean, square)
        each(stat_copy, a, "start")
        if a == 0:
            total[...] = jnp.zeros_like(total)
        each(stat_copy, a, "wait")
        means = [mean] + [stat_in[a, d, :, 0:1] for d in range(3)]
        squares = [square] + [stat_in[a, d, :, 64:65] for d in range(3)]
        mean = (means[0] + means[1] + means[2] + means[3]) * 0.25
        square = squares[0] + squares[1] + squares[2] + squares[3]
        for one in means:
            square += count * (one - mean) ** 2
    scale = lax.rsqrt(square * (1.0 / D) + EPSILON)
    values = act[...].astype(F32)
    normed = ((values - mean) * scale * gain[...]).astype(BF16)
    rows_all[ffn] = normed
    zx = (zx_s, zx_r)
    zk = (zk_s, zk_r)
    z_start(rows_all, zx)

    kv_copy.wait()
    pairs = jnp.dot(normed, w_kv[...], preferred_element_type=F32).astype(BF16)
    for q in range(4):
        pair_part[q] = pairs[:, q * 128 : (q + 1) * 128]
    each(pair_copy, 0, "start")
    z_step(rows_all, zx, 1)
    each(pair_copy, 0, "wait")
    pair_sum[...] = (
        pair_part[x].astype(F32)
        + pair_in[0, 0].astype(F32)
        + pair_in[0, 1].astype(F32)
        + pair_in[0, 2].astype(F32)
    ).astype(BF16)
    each(pair_copy, 1, "start")
    z_step(rows_all, zx, 2)
    each(pair_copy, 1, "wait")
    pair_all[x] = (
        pair_sum[...].astype(F32)
        + pair_in[1, 0].astype(F32)
        + pair_in[1, 1].astype(F32)
        + pair_in[1, 2].astype(F32)
    ).astype(BF16)
    each(pair_copy, 2, "start")
    z_step(rows_all, zx, 3)
    each(pair_copy, 2, "wait")
    for k in range(2):
        for i in range(2):
            turn_copy(k, i).wait()
    first, second = pair_all[0].astype(F32), pair_all[1].astype(F32)
    kv_all[ffn, :, 0:128] = (first * turn[1, 0] - second * turn[1, 1]).astype(BF16)
    kv_all[ffn, :, 128:256] = (first * turn[1, 1] + second * turn[1, 0]).astype(BF16)
    kv_all[ffn, :, 256:384] = pair_all[2]
    kv_all[ffn, :, 384:512] = pair_all[3]
    z_step(rows_all, zx, 4)

    for s in range(STEPS):
        for o in range(2):
            w_copy(s, o).wait()
    for u in range(UNITS):
        wb_copy(u).wait()

    def first_ref(s, o, i, m):
        p1 = orders[o][0]
        d = dirs[i]
        if m == 0:
            return part.at[s, o, mod4(p1 + 2), pl.ds(2 * i, 2)]
        if m == 1:
            return part.at[s, o, mod4(p1 + d), pl.ds(2 * (1 - i), 2)]
        return part.at[s, o, mod4(p1 + d), pl.ds(2 * i, 2)]

    def first_copy(s, o, i, m):
        at = o * 12 + i * 3 + m
        return remote(
            first_ref(s, o, i, m), land1.at[s, o, i, m], rs_s.at[s, at], rs_r.at[s, at],
            orders[o][2](dirs[i]),
        )

    def second_ref(s, o, i, m):
        p1, p2 = orders[o][0], orders[o][1]
        d = dirs[i]
        if m == 0:
            return part.at[s, o, p1, mod4(p2 + 2), pl.ds(i * HALF, HALF)]
        if m == 1:
            return part.at[s, o, p1, mod4(p2 + d), pl.ds((1 - i) * HALF, HALF)]
        return part.at[s, o, p1, mod4(p2 + d), pl.ds(i * HALF, HALF)]

    def second_copy(s, o, i, m):
        at = o * 12 + 6 + i * 3 + m
        return remote(
            second_ref(s, o, i, m), land2.at[s, o, i, m], rs_s.at[s, at], rs_r.at[s, at],
            orders[o][3](dirs[i]),
        )

    both = [(o, i) for o in range(2) for i in range(2)]

    def phase0(s):
        for o in range(2):

            def tile(t, carry):
                rows = rows_all[pl.ds(t * SIDE, SIDE)].reshape(SIDE * ROWS, FEATS)
                res = jnp.dot(rows, w_in[s, o], preferred_element_type=F32).astype(BF16)
                res = res.reshape(SIDE, ROWS, WIDE)
                if o == 0:
                    part[s, 0, t] = res
                else:
                    part[s, 1, :, t] = res
                return carry

            lax.fori_loop(0, SIDE, tile, 0)
            for i in range(2):
                first_copy(s, o, i, 0).start()
            for i in range(2):
                first_copy(s, o, i, 1).start()

    def add_into(ref, land):
        ref[...] = (ref[...].astype(F32) + land[...].astype(F32)).astype(BF16)

    def phase1(s):
        for o, i in both:
            first_copy(s, o, i, 0).wait()
            add_into(first_ref(s, o, i, 2), land1.at[s, o, i, 0])
            first_copy(s, o, i, 2).start()

    def phase2(s):
        for o in range(2):
            p1 = orders[o][0]
            for i in range(2):
                first_copy(s, o, i, 1).wait()
                first_copy(s, o, i, 2).wait()
            for i in range(2):
                ref = part.at[s, o, p1, pl.ds(2 * i, 2)]
                ref[...] = (
                    ref[...].astype(F32)
                    + land1[s, o, i, 2].astype(F32)
                    + land1[s, o, 1 - i, 1].astype(F32)
                ).astype(BF16)
            for i in range(2):
                second_copy(s, o, i, 0).start()
                second_copy(s, o, i, 1).start()

    def phase3(s):
        for o, i in both:
            second_copy(s, o, i, 0).wait()
            add_into(second_ref(s, o, i, 2), land2.at[s, o, i, 0])
            second_copy(s, o, i, 2).start()

    def attend(left, right):
        seg_row = seg[...].astype(F32)
        key_at = lax.broadcasted_iota(jnp.int32, (ROWS, TOKENS), 1)
        row_at = lax.broadcasted_iota(jnp.int32, (ROWS, TOKENS), 0) + hid * ROWS
        own = jnp.sum(jnp.where(key_at == row_at, seg_row, 0.0), 1, keepdims=True)
        allowed = (key_at <= row_at) & (seg_row == own)
        keys = kv_all[:, :, 0:HEAD].reshape(TOKENS, HEAD)
        vals = kv_all[:, :, HEAD : 2 * HEAD].reshape(TOKENS, HEAD)
        cosine, sine = turn[0, 0], turn[0, 1]
        groups = [v[:, k * 128 : (k + 1) * 128] for v in (left, right) for k in range(3)]
        pieces = []
        for h in range(3):
            a, b = groups[2 * h], groups[2 * h + 1]
            query = jnp.concatenate([a * cosine - b * sine, a * sine + b * cosine], 1).astype(BF16)
            scores = lax.dot_general(
                query, keys, (((1,), (1,)), ((), ())), preferred_element_type=F32
            ) * (HEAD**-0.5)
            expos = jnp.where(allowed, jnp.exp(scores), 0.0)
            probs = (expos / jnp.sum(expos, 1, keepdims=True)).astype(BF16)
            res = jnp.dot(probs, vals, preferred_element_type=F32).astype(BF16)
            pieces += [res[:, 0:128], res[:, 128:256]]
        return jnp.concatenate(pieces[:3], 1), jnp.concatenate(pieces[3:], 1)

    def put(u, block):
        mixed[u, 0, y, x] = block[0:HALF]
        mixed[u, 1, x, y] = block[HALF:ROWS]

    def gather_copy(u, o, k, i):
        p1, p2, dev1, dev2 = orders[o]
        d = dirs[i]
        if k == 0:
            ref, dev = mixed.at[u, o, p2, p1], dev1(d)
        elif k == 1:
            ref, dev = mixed.at[u, o, p2, mod4(p1 - d), pl.ds(i * QUARTER, QUARTER)], dev1(d)
        elif k == 2:
            ref, dev = mixed.at[u, o, p2], dev2(d)
        else:
            ref, dev = mixed.at[u, o, mod4(p2 - d), pl.ds(2 * i, 2)], dev2(d)
        at = o * 8 + k * 2 + i
        return remote(ref, ref, ag_s.at[u, at], ag_r.at[u, at], dev)

    def phase4(s):
        sums = []
        for o in range(2):
            p1, p2 = orders[o][0], orders[o][1]
            for i in range(2):
                second_copy(s, o, i, 1).wait()
                second_copy(s, o, i, 2).wait()
            sums.append(
                jnp.concatenate(
                    [
                        part[s, o, p1, p2, i * HALF : (i + 1) * HALF].astype(F32)
                        + land2[s, o, i, 2].astype(F32)
                        + land2[s, o, 1 - i, 1].astype(F32)
                        for i in range(2)
                    ],
                    0,
                )
            )

        @pl.when(s == 0)
        def _():
            left, right = attend(*sums)
            put(0, left)
            put(1, right)
            for u in range(2):
                for o, i in both:
                    gather_copy(u, o, 0, i).start()

        @pl.when(s > 0)
        def _():
            gate, up = sums
            put(s + 1, (gate / (1.0 + jnp.exp(-gate)) * up).astype(BF16))
            for o, i in both:
                gather_copy(s + 1, o, 0, i).start()

    def phase5(u):
        for o, i in both:
            gather_copy(u, o, 0, i).wait()
            gather_copy(u, o, 1, i).start()

    def phase6(u):
        for o in range(2):
            for i in range(2):
                gather_copy(u, o, 1, i).wait()
            for i in range(2):
                gather_copy(u, o, 2, i).start()

    def phase7(u):
        for o, i in both:
            gather_copy(u, o, 2, i).wait()
            gather_copy(u, o, 3, i).start()

    def phase8(u):
        for o in range(2):
            for i in range(2):
                gather_copy(u, o, 3, i).wait()
            for p in range(2):
                rows = mixed[u, o, 2 * p : 2 * p + 2].reshape(2 * SIDE * HALF, WIDE)
                total[o, p * 256 : (p + 1) * 256] += jnp.dot(
                    rows, w_back[u], preferred_element_type=F32
                )

    def slot(t, carry):
        for k, fn in enumerate((phase0, phase1, phase2, phase3)):
            s = t - k
            pl.when((s >= 0) & (s < STEPS))(lambda fn=fn, s=s: fn(s))

        @pl.when(t == 0)
        def _():
            z_start(kv_all, zk)

        for j in range(1, 5):
            pl.when(t == j)(lambda j=j: z_step(kv_all, zk, j))

        s4 = t - 4
        pl.when((s4 >= 0) & (s4 < STEPS))(lambda: phase4(s4))

        for k, fn in ((5, phase5), (6, phase6), (7, phase7), (8, phase8)):
            s = t - k

            @pl.when((s >= 0) & (s < STEPS))
            def _(fn=fn, s=s):
                def unit(u, c):
                    fn(u)
                    return c

                lax.fori_loop(jnp.where(s == 0, 0, s + 1), s + 2, unit, 0)

        return carry

    lax.fori_loop(0, STEPS + 8, slot, 0)

    offsets = (4, 3, -3, 2, -2, 1, -1, 0)

    def block_rows(block):
        bx, by = block // SIDE, block % SIDE
        one = total[0, pl.ds(pl.multiple_of((by * SIDE + bx) * HALF, HALF), HALF)]
        two = total[1, pl.ds(pl.multiple_of(block * HALF, HALF), HALF)]
        return jnp.concatenate([one, two], 0)

    def sib_sum(k):
        at = mod8(z + offsets[k])
        return remote(sib_out.at[at], sib_in.at[at], zr_s.at[k], zr_r.at[k], sibling)

    for k in range(RING):
        at = mod8(z + offsets[k])
        sib_out[at] = block_rows(at * 2 + 1 - core).astype(BF16)
        sib_sum(k).start()

    def chip_sum(k):
        at = mod8(z + offsets[k])
        sib_sum(k).wait()
        return block_rows(at * 2 + core) + sib_in[at].astype(F32)

    def half_copy(i):
        return remote(
            ring_out.at[0, i, pl.ds(0, HALF)], ring_half.at[i], zr_s.at[8 + i], zr_r.at[8 + i],
            dev_z(dirs[i]),
        )

    def full_copy(j, i):
        at = 10 + 2 * j + i
        return remote(
            ring_out.at[1 + j, i], ring_in.at[j, i], zr_s.at[at], zr_r.at[at], dev_z(dirs[i])
        )

    far = chip_sum(0)
    for i in range(2):
        ring_out[0, i, 0:HALF] = far[i * HALF : (i + 1) * HALF].astype(BF16)
        half_copy(i).start()
    for i in range(2):
        here = chip_sum(1 + i)
        half_copy(i).wait()
        come = ring_half[i].astype(F32)
        pad = jnp.zeros((HALF, FEATS), F32)
        come = jnp.concatenate([come, pad] if i == 0 else [pad, come], 0)
        ring_out[1, i] = (here + come).astype(BF16)
        full_copy(0, i).start()
    for j in (1, 2):
        for i in range(2):
            here = chip_sum(1 + 2 * j + i)
            full_copy(j - 1, i).wait()
            ring_out[1 + j, i] = (here + ring_in[j - 1, i].astype(F32)).astype(BF16)
            full_copy(j, i).start()
    here = chip_sum(7) + act[...].astype(F32)
    for i in range(2):
        full_copy(2, i).wait()
        here += ring_in[2, i].astype(F32)
    out[...] = here.astype(BF16)


def per_device(activations, ln_gain, segments, w_query, w_key_value, w_gate, w_up, w_out, w_down):
    vmem = pl.BlockSpec(memory_space=pltpu.VMEM)
    anywhere = pl.BlockSpec(memory_space=pl.ANY)
    dma = pltpu.SemaphoreType.DMA
    scratch = [
        pltpu.VMEM((STEPS, 2, FEATS, WIDE), BF16),
        pltpu.VMEM((UNITS, WIDE, FEATS), BF16),
        pltpu.VMEM((FEATS, 512), BF16),
        pltpu.VMEM((2, 2, ROWS, 128), F32),
        pltpu.VMEM((2, ROWS, 128), F32),
        pltpu.VMEM((2, 3, ROWS, 128), F32),
        pltpu.VMEM((GROUP, ROWS, FEATS), BF16),
        pltpu.VMEM((4, ROWS, 128), BF16),
        pltpu.VMEM((2, 3, ROWS, 128), BF16),
        pltpu.VMEM((ROWS, 128), BF16),
        pltpu.VMEM((4, ROWS, 128), BF16),
        pltpu.VMEM((GROUP, ROWS, 512), BF16),
        pltpu.VMEM((STEPS, 2, SIDE, SIDE, ROWS, WIDE), BF16),
        pltpu.VMEM((STEPS, 2, 2, 3, 2, ROWS, WIDE), BF16),
        pltpu.VMEM((STEPS, 2, 2, 3, HALF, WIDE), BF16),
        pltpu.VMEM((UNITS, 2, SIDE, SIDE, HALF, WIDE), BF16),
        pltpu.VMEM((2, GROUP * HALF, FEATS), F32),
        pltpu.VMEM((RING, ROWS, FEATS), BF16),
        pltpu.VMEM((RING, ROWS, FEATS), BF16),
        pltpu.VMEM((4, 2, ROWS, FEATS), BF16),
        pltpu.VMEM((2, HALF, FEATS), BF16),
        pltpu.VMEM((3, 2, ROWS, FEATS), BF16),
        dma((STEPS, 2)),
        dma((UNITS,)),
        dma((5,)),
        dma((5, 3)),
        dma((5, 3)),
        dma((8, 2)),
        dma((8, 2)),
        dma((8, 2)),
        dma((8, 2)),
        dma((STEPS, 24)),
        dma((STEPS, 24)),
        dma((UNITS, 16)),
        dma((UNITS, 16)),
        dma((16,)),
        dma((16,)),
    ]
    return pl.pallas_call(
        block_kernel,
        out_shape=jax.ShapeDtypeStruct((ROWS, FEATS), BF16),
        in_specs=[vmem, vmem, vmem] + [anywhere] * 7,
        out_specs=vmem,
        scratch_shapes=scratch,
        compiler_params=pltpu.CompilerParams(
            collective_id=0, has_side_effects=True, vmem_limit_bytes=60 * 1024 * 1024
        ),
    )(
        activations,
        ln_gain.reshape(1, FEATS),
        segments.reshape(1, TOKENS),
        jnp.asarray(tables()),
        w_query,
        w_key_value,
        w_gate,
        w_up,
        w_out,
        w_down,
    )


def solution(mesh):
    placed = (
        P("ffn", "hid"),
        P("hid"),
        P(),
        P("hid", "ffn"),
        P("hid", None),
        P("hid", "ffn"),
        P("hid", "ffn"),
        P("ffn", "hid"),
        P("ffn", "hid"),
    )
    return jax.shard_map(
        per_device, mesh=mesh, in_specs=placed, out_specs=P("ffn", "hid"), check_vma=False
    )
```

```python
import jax
import jax.numpy as jnp
import numpy as np
from jax import lax
from jax.experimental import pallas as pl
from jax.experimental.pallas import tpu as pltpu
from jax.sharding import PartitionSpec as P

D = 10240
HEAD = 256
TOKENS = 1024
EPSILON = 1e-06

SIDE = 4
RING = 8
GROUP = SIDE * SIDE
ROWS = TOKENS // GROUP
FEATS = D // GROUP
WIDE = 384
STEPS = 7
UNITS = 8
HALF = ROWS // 2
QUARTER = ROWS // 4
F32 = jnp.float32
BF16 = jnp.bfloat16


def tables():
    half = HEAD // 2
    frequency = np.float32(10000.0) ** (-np.arange(half, dtype=np.float32) / np.float32(half))
    angles = np.arange(TOKENS, dtype=np.float32)[:, None] * frequency[None, :].astype(np.float32)
    wide = angles.astype(np.float64)
    return np.stack([np.cos(wide), np.sin(wide)]).astype(np.float32)


def block_kernel(
    act,
    gain,
    seg,
    table,
    w_query,
    w_pairs,
    w_gate,
    w_up,
    w_out,
    w_down,
    out,
    w_in,
    w_back,
    w_kv,
    turn,
    stat,
    stat_in,
    rows_all,
    pair_part,
    pair_in,
    pair_sum,
    pair_all,
    kv_all,
    part,
    land1,
    last1,
    land2,
    last2,
    mixed,
    total,
    sib_out,
    sib_in,
    ring_out,
    ring_half,
    ring_in,
    w_sem,
    wb_sem,
    m_sem,
    small_s,
    small_r,
    zx_s,
    zx_r,
    zk_s,
    zk_r,
    rs_s,
    rs_r,
    ag_s,
    ag_r,
    zr_s,
    zr_r,
):
    hid = lax.axis_index("hid")
    ffn = lax.axis_index("ffn")
    x, y = hid // SIDE, hid % SIDE
    z, core = ffn // 2, ffn % 2

    def mod4(v):
        return (v + SIDE) % SIDE

    def mod8(v):
        return (v + RING) % RING

    ids_x = {d: mod4(x + d) * SIDE + y for d in (1, 2, 3)}
    ids_y = {d: x * SIDE + mod4(y + d) for d in (1, 2, 3)}
    ids_z = {d: mod8(z + d) * 2 + core for d in (1, -1)}

    def dev_x(d):
        return (ids_x[d % SIDE], ffn)

    def dev_y(d):
        return (ids_y[d % SIDE], ffn)

    def dev_z(d):
        return (hid, ids_z[d])

    sibling = (hid, z * 2 + 1 - core)
    dirs = (1, -1)
    devs = ((dev_x, dev_y), (dev_y, dev_x))

    barrier = pltpu.get_barrier_semaphore()
    partners = [dev_x(d) for d in (1, 2, 3)] + [dev_y(d) for d in (1, 2, 3)]
    partners += [dev_z(1), dev_z(-1), sibling]
    for dev in partners:
        pl.semaphore_signal(barrier, inc=1, device_id=dev, device_id_type=pl.DeviceIdType.MESH)

    def remote(src, dst, ssem, rsem, dev):
        return pltpu.make_async_remote_copy(
            src_ref=src,
            dst_ref=dst,
            send_sem=ssem,
            recv_sem=rsem,
            device_id=dev,
            device_id_type=pl.DeviceIdType.MESH,
        )

    def w_copy(s, o):
        if s == 0:
            src = w_query.at[:, pl.ds(o * WIDE, WIDE)]
        else:
            src = (w_gate, w_up)[o].at[:, pl.ds((s - 1) * WIDE, WIDE)]
        return pltpu.make_async_copy(src, w_in.at[s, :, pl.ds(o * WIDE, WIDE)], w_sem.at[s, o])

    def wb_copy(u):
        if u < 2:
            src = w_out.at[pl.ds(u * WIDE, WIDE)]
        else:
            src = w_down.at[pl.ds((u - 2) * WIDE, WIDE)]
        return pltpu.make_async_copy(src, w_back.at[u], wb_sem.at[u])

    def turn_copy(k, i):
        first = (hid if k == 0 else ffn) * ROWS
        return pltpu.make_async_copy(
            table.at[i, pl.ds(first, ROWS)], turn.at[k, i], m_sem.at[1 + 2 * k + i]
        )

    kv_copy = pltpu.make_async_copy(w_pairs, w_kv, m_sem.at[0])
    kv_copy.start()
    for k in range(2):
        for i in range(2):
            turn_copy(k, i).start()
    for s in range(STEPS):
        for o in range(2):
            w_copy(s, o).start()
    for u in range(UNITS):
        wb_copy(u).start()

    pl.semaphore_wait(barrier, len(partners))

    def stat_copy(a, d):
        return remote(
            stat.at[a], stat_in.at[a, d - 1], small_s.at[a, d - 1], small_r.at[a, d - 1],
            (dev_x, dev_y)[a](d),
        )

    def pair_copy(k, d):
        if k == 0:
            src, dst, dev = pair_part.at[mod4(x + d)], pair_in.at[0, d - 1], dev_x(d)
        elif k == 1:
            src, dst, dev = pair_sum, pair_in.at[1, d - 1], dev_y(d)
        else:
            src, dst, dev = pair_all.at[x], pair_all.at[x], dev_x(d)
        return remote(src, dst, small_s.at[2 + k, d - 1], small_r.at[2 + k, d - 1], dev)

    def each(fn, k, what):
        for d in (1, 2, 3):
            getattr(fn(k, d), what)()

    def z_copy(buf, sems, j, i):
        d = dirs[i]
        block = mod8(z - (j - 1) * d) * 2 + core
        ref = buf.at[block] if j < 4 else buf.at[block, pl.ds(i * HALF, HALF)]
        return remote(ref, ref, sems[0].at[j - 1, i], sems[1].at[j - 1, i], dev_z(d))

    def sib_copy(buf, sems, off):
        ref = buf.at[mod8(z + off) * 2 + core]
        row = 4 + (off + 3) // 2
        col = (off + 3) % 2
        return remote(ref, ref, sems[0].at[row, col], sems[1].at[row, col], sibling)

    def z_start(buf, sems):
        for i in range(2):
            z_copy(buf, sems, 1, i).start()
        sib_copy(buf, sems, 0).start()

    def z_step(buf, sems, j):
        if j < 4:
            for i in range(2):
                z_copy(buf, sems, j, i).wait()
                z_copy(buf, sems, j + 1, i).start()
                sib_copy(buf, sems, -j * dirs[i]).start()
        else:
            for i in range(2):
                z_copy(buf, sems, j, i).wait()
            sib_copy(buf, sems, 4).start()
            for off in (0, 1, -1, 2, -2, 3, -3, 4):
                sib_copy(buf, sems, off).wait()

    values = act[...].astype(F32)
    mean = jnp.mean(values, 1, keepdims=True)
    square = jnp.sum((values - mean) ** 2, 1, keepdims=True)
    lane = lax.broadcasted_iota(jnp.int32, (ROWS, 128), 1)
    for a, count in ((0, FEATS), (1, FEATS * SIDE)):
        stat[a] = jnp.where(lane < 64, mean, square)
        each(stat_copy, a, "start")
        if a == 0:
            total[...] = jnp.zeros_like(total)
        each(stat_copy, a, "wait")
        means = [mean] + [stat_in[a, d, :, 0:1] for d in range(3)]
        squares = [square] + [stat_in[a, d, :, 64:65] for d in range(3)]
        mean = (means[0] + means[1] + means[2] + means[3]) * 0.25
        square = squares[0] + squares[1] + squares[2] + squares[3]
        for one in means:
            square += count * (one - mean) ** 2
    scale = lax.rsqrt(square * (1.0 / D) + EPSILON)
    values = act[...].astype(F32)
    normed = ((values - mean) * scale * gain[...].reshape(1, FEATS)).astype(BF16)
    rows_all[ffn] = normed
    zx = (zx_s, zx_r)
    zk = (zk_s, zk_r)
    z_start(rows_all, zx)

    kv_copy.wait()
    pairs = jnp.dot(normed, w_kv[...], preferred_element_type=F32).astype(BF16)
    for q in range(4):
        pair_part[q] = pairs[:, q * 128 : (q + 1) * 128]
    each(pair_copy, 0, "start")
    z_step(rows_all, zx, 1)
    each(pair_copy, 0, "wait")
    pair_sum[...] = (
        pair_part[x].astype(F32)
        + pair_in[0, 0].astype(F32)
        + pair_in[0, 1].astype(F32)
        + pair_in[0, 2].astype(F32)
    ).astype(BF16)
    each(pair_copy, 1, "start")
    z_step(rows_all, zx, 2)
    each(pair_copy, 1, "wait")
    pair_all[x] = (
        pair_sum[...].astype(F32)
        + pair_in[1, 0].astype(F32)
        + pair_in[1, 1].astype(F32)
        + pair_in[1, 2].astype(F32)
    ).astype(BF16)
    each(pair_copy, 2, "start")
    z_step(rows_all, zx, 3)
    each(pair_copy, 2, "wait")
    for k in range(2):
        for i in range(2):
            turn_copy(k, i).wait()
    first, second = pair_all[0].astype(F32), pair_all[1].astype(F32)
    kv_all[ffn, :, 0:128] = (first * turn[1, 0] - second * turn[1, 1]).astype(BF16)
    kv_all[ffn, :, 128:256] = (first * turn[1, 1] + second * turn[1, 0]).astype(BF16)
    kv_all[ffn, :, 256:384] = pair_all[2]
    kv_all[ffn, :, 384:512] = pair_all[3]
    z_step(rows_all, zx, 4)

    for s in range(STEPS):
        for o in range(2):
            w_copy(s, o).wait()
    for u in range(UNITS):
        wb_copy(u).wait()

    far1 = ((12, 8), (20, 8))
    near1 = ((8, 4), (28, 4))
    far2 = ((3, 2), (5, 2))
    near2 = ((2, 1), (7, 1))

    def rs_copy(s, o, k, i):
        first, size = (far1, near1, far2, near2)[k][i]
        at = o * 8 + k * 2 + i
        return remote(
            part.at[s, o, pl.ds(first, size)],
            (land1, last1, land2, last2)[k].at[s, o, i],
            rs_s.at[s, at],
            rs_r.at[s, at],
            devs[o][k // 2](dirs[i]),
        )

    both = [(o, i) for o in range(2) for i in range(2)]
    rel_y = [mod4(k - y) for k in range(SIDE)]

    def phase0(s):
        def tile(t, carry):
            rows = rows_all[pl.ds(t * SIDE, SIDE)].reshape(SIDE * ROWS, FEATS)
            res = jnp.dot(rows, w_in[s], preferred_element_type=F32).astype(BF16)
            rel_x = mod4(t - x)
            for k in range(SIDE):
                block = res[k * ROWS : (k + 1) * ROWS].reshape(2, HALF, 2 * WIDE)
                part[s, 0, pl.ds((rel_x * SIDE + rel_y[k]) * 2, 2)] = block[:, :, :WIDE]
                part[s, 1, pl.ds((rel_y[k] * SIDE + rel_x) * 2, 2)] = block[:, :, WIDE:]
            return carry

        lax.fori_loop(0, SIDE, tile, 0)
        for o, i in both:
            rs_copy(s, o, 0, i).start()

    def add_into(ref, *lands):
        res = ref[...].astype(F32)
        for land in lands:
            res += land[...].astype(F32)
        ref[...] = res.astype(BF16)

    def phase1(s):
        for o, i in both:
            rs_copy(s, o, 0, i).wait()
            first, size = near1[i]
            add_into(part.at[s, o, pl.ds(first, size)], land1.at[s, o, i, pl.ds(4 - 4 * i, 4)])
            rs_copy(s, o, 1, i).start()

    def phase2(s):
        for o in range(2):
            for i in range(2):
                rs_copy(s, o, 1, i).wait()
            for i in range(2):
                add_into(
                    part.at[s, o, pl.ds(4 * i, 4)],
                    last1.at[s, o, i],
                    land1.at[s, o, 1 - i, pl.ds(4 - 4 * i, 4)],
                )
            for i in range(2):
                rs_copy(s, o, 2, i).start()

    def phase3(s):
        for o, i in both:
            rs_copy(s, o, 2, i).wait()
            first, size = near2[i]
            add_into(part.at[s, o, pl.ds(first, size)], land2.at[s, o, i, pl.ds(1 - i, 1)])
            rs_copy(s, o, 3, i).start()

    def attend(left, right):
        seg_row = seg[...].astype(F32)
        key_at = lax.broadcasted_iota(jnp.int32, (ROWS, TOKENS), 1)
        row_at = lax.broadcasted_iota(jnp.int32, (ROWS, TOKENS), 0) + hid * ROWS
        own = jnp.sum(jnp.where(key_at == row_at, seg_row, 0.0), 1, keepdims=True)
        allowed = (key_at <= row_at) & (seg_row == own)
        keys = kv_all[:, :, 0:HEAD].reshape(TOKENS, HEAD)
        vals = kv_all[:, :, HEAD : 2 * HEAD].reshape(TOKENS, HEAD)
        cosine, sine = turn[0, 0] * HEAD**-0.5, turn[0, 1] * HEAD**-0.5
        groups = [v[:, k * 128 : (k + 1) * 128] for v in (left, right) for k in range(3)]
        pieces = []
        for h in range(3):
            a, b = groups[2 * h], groups[2 * h + 1]
            query = jnp.concatenate([a * cosine - b * sine, a * sine + b * cosine], 1).astype(BF16)
            scores = lax.dot_general(
                query, keys, (((1,), (1,)), ((), ())), preferred_element_type=F32
            )
            expos = jnp.where(allowed, jnp.exp(scores), 0.0)
            probs = (expos / jnp.sum(expos, 1, keepdims=True)).astype(BF16)
            res = jnp.dot(probs, vals, preferred_element_type=F32).astype(BF16)
            pieces += [res[:, 0:128], res[:, 128:256]]
        return jnp.concatenate(pieces[:3], 1), jnp.concatenate(pieces[3:], 1)

    def put(u, block):
        mixed[u, 0, 0, 0] = block[0:HALF]
        mixed[u, 1, 0, 0] = block[HALF:ROWS]

    def gather_copy(u, o, k, i):
        d = dirs[i]
        away, near = (3, 1)[i], (3, 1)[i]
        dev = devs[o][k // 2](d)
        if k == 0:
            src, dst = mixed.at[u, o, 0, 0], mixed.at[u, o, 0, away]
        elif k == 1:
            rows = pl.ds(i * QUARTER, QUARTER)
            src, dst = mixed.at[u, o, 0, near, rows], mixed.at[u, o, 0, 2, rows]
        elif k == 2:
            src, dst = mixed.at[u, o, 0], mixed.at[u, o, away]
        else:
            cut = pl.ds(2 * i, 2)
            src, dst = mixed.at[u, o, near, cut], mixed.at[u, o, 2, cut]
        at = o * 8 + k * 2 + i
        return remote(src, dst, ag_s.at[u, at], ag_r.at[u, at], dev)

    def phase4(s):
        sums = []
        for o in range(2):
            for i in range(2):
                rs_copy(s, o, 3, i).wait()
            sums.append(
                jnp.concatenate(
                    [
                        part[s, o, i].astype(F32)
                        + last2[s, o, i, 0].astype(F32)
                        + land2[s, o, 1 - i, 1 - i].astype(F32)
                        for i in range(2)
                    ],
                    0,
                )
            )

        @pl.when(s == 0)
        def _():
            left, right = attend(*sums)
            put(0, left)
            put(1, right)
            for u in range(2):
                for o, i in both:
                    gather_copy(u, o, 0, i).start()

        @pl.when(s > 0)
        def _():
            gate, up = sums
            put(s + 1, (gate / (1.0 + jnp.exp(-gate)) * up).astype(BF16))
            for o, i in both:
                gather_copy(s + 1, o, 0, i).start()

    def phase5(u):
        for o, i in both:
            gather_copy(u, o, 0, i).wait()
            gather_copy(u, o, 1, i).start()

    def phase6(u):
        for o in range(2):
            for i in range(2):
                gather_copy(u, o, 1, i).wait()
            for i in range(2):
                gather_copy(u, o, 2, i).start()

    def phase7(u):
        for o, i in both:
            gather_copy(u, o, 2, i).wait()
            gather_copy(u, o, 3, i).start()

    def phase8(u):
        for o in range(2):
            for i in range(2):
                gather_copy(u, o, 3, i).wait()
            for p in range(2):
                rows = mixed[u, o, 2 * p : 2 * p + 2].reshape(2 * SIDE * HALF, WIDE)
                total[o, p * 256 : (p + 1) * 256] += jnp.dot(
                    rows, w_back[u], preferred_element_type=F32
                )

    def slot(t, carry):
        for k, fn in enumerate((phase0, phase1, phase2, phase3)):
            s = t - k
            pl.when((s >= 0) & (s < STEPS))(lambda fn=fn, s=s: fn(s))

        @pl.when(t == 0)
        def _():
            z_start(kv_all, zk)

        for j in range(1, 5):
            pl.when(t == j)(lambda j=j: z_step(kv_all, zk, j))

        s4 = t - 4
        pl.when((s4 >= 0) & (s4 < STEPS))(lambda: phase4(s4))

        for k, fn in ((5, phase5), (6, phase6), (7, phase7), (8, phase8)):
            s = t - k

            @pl.when((s >= 0) & (s < STEPS))
            def _(fn=fn, s=s):
                def unit(u, c):
                    fn(u)
                    return c

                lax.fori_loop(jnp.where(s == 0, 0, s + 1), s + 2, unit, 0)

        return carry

    lax.fori_loop(0, STEPS + 8, slot, 0)

    offsets = (4, 3, -3, 2, -2, 1, -1, 0)

    def block_rows(block):
        bx, by = mod4(block // SIDE - x), mod4(block % SIDE - y)
        one = total[0, pl.ds(pl.multiple_of((by * SIDE + bx) * HALF, HALF), HALF)]
        two = total[1, pl.ds(pl.multiple_of((bx * SIDE + by) * HALF, HALF), HALF)]
        return jnp.concatenate([one, two], 0)

    def sib_sum(k):
        at = mod8(z + offsets[k])
        return remote(sib_out.at[at], sib_in.at[at], zr_s.at[k], zr_r.at[k], sibling)

    for k in range(RING):
        at = mod8(z + offsets[k])
        sib_out[at] = block_rows(at * 2 + 1 - core).astype(BF16)
        sib_sum(k).start()

    def chip_sum(k):
        at = mod8(z + offsets[k])
        sib_sum(k).wait()
        return block_rows(at * 2 + core) + sib_in[at].astype(F32)

    def half_copy(i):
        return remote(
            ring_out.at[0, i, pl.ds(0, HALF)], ring_half.at[i], zr_s.at[8 + i], zr_r.at[8 + i],
            dev_z(dirs[i]),
        )

    def full_copy(j, i):
        at = 10 + 2 * j + i
        return remote(
            ring_out.at[1 + j, i], ring_in.at[j, i], zr_s.at[at], zr_r.at[at], dev_z(dirs[i])
        )

    far = chip_sum(0)
    for i in range(2):
        ring_out[0, i, 0:HALF] = far[i * HALF : (i + 1) * HALF].astype(BF16)
        half_copy(i).start()
    for i in range(2):
        here = chip_sum(1 + i)
        half_copy(i).wait()
        come = ring_half[i].astype(F32)
        pad = jnp.zeros((HALF, FEATS), F32)
        come = jnp.concatenate([come, pad] if i == 0 else [pad, come], 0)
        ring_out[1, i] = (here + come).astype(BF16)
        full_copy(0, i).start()
    for j in (1, 2):
        for i in range(2):
            here = chip_sum(1 + 2 * j + i)
            full_copy(j - 1, i).wait()
            ring_out[1 + j, i] = (here + ring_in[j - 1, i].astype(F32)).astype(BF16)
            full_copy(j, i).start()
    here = chip_sum(7) + act[...].astype(F32)
    for i in range(2):
        full_copy(2, i).wait()
        here += ring_in[2, i].astype(F32)
    out[...] = here.astype(BF16)


def per_device(activations, ln_gain, segments, w_query, w_key_value, w_gate, w_up, w_out, w_down):
    vmem = pl.BlockSpec(memory_space=pltpu.VMEM)
    anywhere = pl.BlockSpec(memory_space=pl.ANY)
    dma = pltpu.SemaphoreType.DMA
    scratch = [
        pltpu.VMEM((STEPS, FEATS, 2 * WIDE), BF16),
        pltpu.VMEM((UNITS, WIDE, FEATS), BF16),
        pltpu.VMEM((FEATS, 512), BF16),
        pltpu.VMEM((2, 2, ROWS, 128), F32),
        pltpu.VMEM((2, ROWS, 128), F32),
        pltpu.VMEM((2, 3, ROWS, 128), F32),
        pltpu.VMEM((GROUP, ROWS, FEATS), BF16),
        pltpu.VMEM((4, ROWS, 128), BF16),
        pltpu.VMEM((2, 3, ROWS, 128), BF16),
        pltpu.VMEM((ROWS, 128), BF16),
        pltpu.VMEM((4, ROWS, 128), BF16),
        pltpu.VMEM((GROUP, ROWS, 512), BF16),
        pltpu.VMEM((STEPS, 2, 2 * GROUP, HALF, WIDE), BF16),
        pltpu.VMEM((STEPS, 2, 2, 8, HALF, WIDE), BF16),
        pltpu.VMEM((STEPS, 2, 2, 4, HALF, WIDE), BF16),
        pltpu.VMEM((STEPS, 2, 2, 2, HALF, WIDE), BF16),
        pltpu.VMEM((STEPS, 2, 2, 1, HALF, WIDE), BF16),
        pltpu.VMEM((UNITS, 2, SIDE, SIDE, HALF, WIDE), BF16),
        pltpu.VMEM((2, GROUP * HALF, FEATS), F32),
        pltpu.VMEM((RING, ROWS, FEATS), BF16),
        pltpu.VMEM((RING, ROWS, FEATS), BF16),
        pltpu.VMEM((4, 2, ROWS, FEATS), BF16),
        pltpu.VMEM((2, HALF, FEATS), BF16),
        pltpu.VMEM((3, 2, ROWS, FEATS), BF16),
        dma((STEPS, 2)),
        dma((UNITS,)),
        dma((5,)),
        dma((5, 3)),
        dma((5, 3)),
        dma((8, 2)),
        dma((8, 2)),
        dma((8, 2)),
        dma((8, 2)),
        dma((STEPS, 16)),
        dma((STEPS, 16)),
        dma((UNITS, 16)),
        dma((UNITS, 16)),
        dma((16,)),
        dma((16,)),
    ]
    return pl.pallas_call(
        block_kernel,
        out_shape=jax.ShapeDtypeStruct((ROWS, FEATS), BF16),
        in_specs=[vmem, vmem, vmem] + [anywhere] * 7,
        out_specs=vmem,
        scratch_shapes=scratch,
        compiler_params=pltpu.CompilerParams(
            collective_id=0, has_side_effects=True, vmem_limit_bytes=60 * 1024 * 1024
        ),
    )(
        activations,
        ln_gain,
        segments.reshape(1, TOKENS),
        jnp.asarray(tables()),
        w_query,
        w_key_value,
        w_gate,
        w_up,
        w_out,
        w_down,
    )


def solution(mesh):
    placed = (
        P("ffn", "hid"),
        P("hid"),
        P(),
        P("hid", "ffn"),
        P("hid", None),
        P("hid", "ffn"),
        P("hid", "ffn"),
        P("ffn", "hid"),
        P("ffn", "hid"),
    )
    return jax.shard_map(
        per_device, mesh=mesh, in_specs=placed, out_specs=P("ffn", "hid"), check_vma=False
    )
```

```python
import jax
import jax.numpy as jnp
import numpy as np
from jax import lax
from jax.experimental import pallas as pl
from jax.experimental.pallas import tpu as pltpu
from jax.sharding import PartitionSpec as P

D = 10240
HEAD = 256
TOKENS = 1024
EPSILON = 1e-06

SIDE = 4
RING = 8
GROUP = SIDE * SIDE
ROWS = TOKENS // GROUP
FEATS = D // GROUP
WIDE = 384
STEPS = 7
UNITS = 8
HALF = ROWS // 2
QUARTERS = 4
QUARTER = ROWS // 4
F32 = jnp.float32
BF16 = jnp.bfloat16


def tables():
    half = HEAD // 2
    frequency = np.float32(10000.0) ** (-np.arange(half, dtype=np.float32) / np.float32(half))
    angles = np.arange(TOKENS, dtype=np.float32)[:, None] * frequency[None, :].astype(np.float32)
    wide = angles.astype(np.float64)
    return np.stack([np.cos(wide), np.sin(wide)]).astype(np.float32)


def block_kernel(
    act,
    gain,
    seg,
    table,
    w_query,
    w_pairs,
    w_gate,
    w_up,
    w_out,
    w_down,
    out,
    w_in,
    w_back,
    w_kv,
    turn,
    stat,
    stat_in,
    stat_all,
    raw_all,
    rows_all,
    pair_part,
    pair_in,
    pair_sum,
    pair_all,
    kv_all,
    part,
    land1,
    last1,
    half_sum,
    land2,
    last2,
    mixed,
    total,
    sib_out,
    sib_in,
    ring_out,
    ring_in,
    w_sem,
    wb_sem,
    m_sem,
    small_s,
    small_r,
    zx_s,
    zx_r,
    zt_s,
    zt_r,
    rq_s,
    rq_r,
    zk_s,
    zk_r,
    rs_s,
    rs_r,
    ag_s,
    ag_r,
    zr_s,
    zr_r,
):
    hid = lax.axis_index("hid")
    ffn = lax.axis_index("ffn")
    x, y = hid // SIDE, hid % SIDE
    z, core = ffn // 2, ffn % 2

    def mod4(v):
        return (v + SIDE) % SIDE

    def mod8(v):
        return (v + RING) % RING

    ids_x = {d: mod4(x + d) * SIDE + y for d in (1, 2, 3)}
    ids_y = {d: x * SIDE + mod4(y + d) for d in (1, 2, 3)}
    ids_z = {d: mod8(z + d) * 2 + core for d in (1, -1)}

    def dev_x(d):
        return (ids_x[d % SIDE], ffn)

    def dev_y(d):
        return (ids_y[d % SIDE], ffn)

    def dev_z(d):
        return (hid, ids_z[d])

    sibling = (hid, z * 2 + 1 - core)
    dirs = (1, -1)
    devs = ((dev_x, dev_y), (dev_y, dev_x))

    barrier = pltpu.get_barrier_semaphore()
    partners = [dev_x(d) for d in (1, 2, 3)] + [dev_y(d) for d in (1, 2, 3)]
    partners += [dev_z(1), dev_z(-1), sibling]
    for dev in partners:
        pl.semaphore_signal(barrier, inc=1, device_id=dev, device_id_type=pl.DeviceIdType.MESH)

    def remote(src, dst, ssem, rsem, dev):
        return pltpu.make_async_remote_copy(
            src_ref=src,
            dst_ref=dst,
            send_sem=ssem,
            recv_sem=rsem,
            device_id=dev,
            device_id_type=pl.DeviceIdType.MESH,
        )

    def w_copy(s, o):
        if s == 0:
            src = w_query.at[:, pl.ds(o * WIDE, WIDE)]
        else:
            src = (w_gate, w_up)[o].at[:, pl.ds((s - 1) * WIDE, WIDE)]
        return pltpu.make_async_copy(src, w_in.at[s, :, pl.ds(o * WIDE, WIDE)], w_sem.at[s, o])

    def wb_copy(u):
        if u < 2:
            src = w_out.at[pl.ds(u * WIDE, WIDE)]
        else:
            src = w_down.at[pl.ds((u - 2) * WIDE, WIDE)]
        return pltpu.make_async_copy(src, w_back.at[u], wb_sem.at[u])

    def turn_copies(i):
        copies = [
            pltpu.make_async_copy(
                table.at[i, pl.ds(pl.multiple_of(ffn * ROWS, ROWS), ROWS)],
                turn.at[1, i],
                m_sem.at[1 + 5 * i],
            )
        ]
        for g in range(QUARTERS):
            first = pl.multiple_of(g * (TOKENS // QUARTERS) + hid * QUARTER, QUARTER)
            copies.append(
                pltpu.make_async_copy(
                    table.at[i, pl.ds(first, QUARTER)],
                    turn.at[0, i, pl.ds(g * QUARTER, QUARTER)],
                    m_sem.at[2 + 5 * i + g],
                )
            )
        return copies

    kv_copy = pltpu.make_async_copy(w_pairs, w_kv, m_sem.at[0])
    kv_copy.start()
    for i in range(2):
        for copy in turn_copies(i):
            copy.start()
    for s in range(STEPS):
        for o in range(2):
            w_copy(s, o).start()
    for u in range(UNITS):
        wb_copy(u).start()

    pl.semaphore_wait(barrier, len(partners))

    def stat_copy(a, d):
        return remote(
            stat.at[a], stat_in.at[a, d - 1], small_s.at[a, d - 1], small_r.at[a, d - 1],
            (dev_x, dev_y)[a](d),
        )

    def pair_copy(k, d):
        if k == 0:
            src, dst, dev = pair_part.at[mod4(x + d)], pair_in.at[0, d - 1], dev_x(d)
        elif k == 1:
            src, dst, dev = pair_sum, pair_in.at[1, d - 1], dev_y(d)
        else:
            src, dst, dev = pair_all.at[x], pair_all.at[x], dev_x(d)
        return remote(src, dst, small_s.at[2 + k, d - 1], small_r.at[2 + k, d - 1], dev)

    def each(fn, k, what):
        for d in (1, 2, 3):
            getattr(fn(k, d), what)()

    def z_copy(buf, sems, j, i):
        d = dirs[i]
        block = mod8(z - (j - 1) * d) * 2 + core
        ref = buf.at[block] if j < 4 else buf.at[block, pl.ds(i * HALF, HALF)]
        return remote(ref, ref, sems[0].at[j - 1, i], sems[1].at[j - 1, i], dev_z(d))

    def sib_copy(buf, sems, off):
        ref = buf.at[mod8(z + off) * 2 + core]
        row = 4 + (off + 3) // 2
        col = (off + 3) % 2
        return remote(ref, ref, sems[0].at[row, col], sems[1].at[row, col], sibling)

    def z_start(buf, sems):
        for i in range(2):
            z_copy(buf, sems, 1, i).start()
        sib_copy(buf, sems, 0).start()

    def z_step(buf, sems, j):
        if j < 4:
            for i in range(2):
                z_copy(buf, sems, j, i).wait()
                z_copy(buf, sems, j + 1, i).start()
                sib_copy(buf, sems, -j * dirs[i]).start()
        else:
            for i in range(2):
                z_copy(buf, sems, j, i).wait()
            sib_copy(buf, sems, 4).start()

    def sib_wait(buf, sems, *offs):
        for off in offs:
            sib_copy(buf, sems, off).wait()

    def stat_z(j, i):
        ref = stat_all.at[mod8(z - (j - 1) * dirs[i])]
        return remote(ref, ref, zt_s.at[j, i], zt_r.at[j, i], dev_z(dirs[i]))

    def stat_step(j):
        for i in range(2):
            if (j, i) == (4, 1):
                continue
            stat_z(j, i).wait()
            if j < 3 + (i == 0):
                stat_z(j + 1, i).start()

    def quarter_copy(j, g, o, i):
        at = o * 2 + i
        return remote(
            part.at[0, o, g, pl.ds((6, 10)[i], 4)],
            land1.at[0, o, i, g],
            rq_s.at[j, at],
            rq_r.at[j, at],
            devs[o][0](dirs[i]),
        )

    both = [(o, i) for o in range(2) for i in range(2)]
    rel_x = [mod4(k - x) for k in range(SIDE)]
    rel_y = [mod4(k - y) for k in range(SIDE)]
    places = (
        [rel_x[h // SIDE] * SIDE + rel_y[h % SIDE] for h in range(GROUP)],
        [rel_y[h % SIDE] * SIDE + rel_x[h // SIDE] for h in range(GROUP)],
    )

    def products(s, g):
        rows = rows_all[pl.ds(g * QUARTERS, QUARTERS)].reshape(QUARTERS * ROWS, FEATS)
        res = jnp.dot(rows, w_in[s], preferred_element_type=F32).astype(BF16)
        for h in range(GROUP):
            block = res[h * QUARTER : (h + 1) * QUARTER]
            for o in range(2):
                part[s, o, g, places[o][h]] = block[:, o * WIDE : (o + 1) * WIDE]

    eye = lax.broadcasted_iota(jnp.int32, (ROWS, 128), 0) == lax.broadcasted_iota(
        jnp.int32, (ROWS, 128), 1
    )
    line = lax.broadcasted_iota(jnp.int32, (8, 128), 0)

    def to_row(column):
        return jnp.sum(jnp.where(eye, column, 0.0), 0, keepdims=True)

    def to_column(row):
        return jnp.sum(jnp.where(eye, row, 0.0), 1, keepdims=True)

    def norm(rows, tile):
        mean, scale = to_column(tile[0:1]), to_column(tile[1:2])
        return ((rows.astype(F32) - mean) * scale * gain[...].reshape(1, FEATS)).astype(BF16)

    zx = (zx_s, zx_r)
    zk = (zk_s, zk_r)
    raw_all[ffn] = act[...]
    z_start(raw_all, zx)
    values = act[...].astype(F32)
    mean = jnp.mean(values, 1, keepdims=True)
    square = jnp.sum((values - mean) ** 2, 1, keepdims=True)
    mean, square = to_row(mean), to_row(square)
    for a, count in ((0, FEATS), (1, FEATS * SIDE)):
        stat[a] = jnp.where(line == 0, mean, square)
        each(stat_copy, a, "start")
        if a == 0:
            total[...] = jnp.zeros_like(total)
        else:
            z_step(raw_all, zx, 1)
        each(stat_copy, a, "wait")
        means = [mean] + [stat_in[a, d, 0:1] for d in range(3)]
        squares = [square] + [stat_in[a, d, 1:2] for d in range(3)]
        mean = (means[0] + means[1] + means[2] + means[3]) * 0.25
        square = squares[0] + squares[1] + squares[2] + squares[3]
        for one in means:
            square += count * (one - mean) ** 2
    scale = lax.rsqrt(square * (1.0 / D) + EPSILON)
    stat_all[z, core] = jnp.where(line == 0, mean, scale)
    stat_sib = remote(
        stat_all.at[z, core], stat_all.at[z, core], zt_s.at[0, 0], zt_r.at[0, 0], sibling
    )
    stat_sib.start()
    normed = norm(act[...], stat_all[z, core])
    stat_sib.wait()
    for i in range(2):
        stat_z(1, i).start()
    kv_copy.wait()
    pairs = jnp.dot(normed, w_kv[...], preferred_element_type=F32).astype(BF16)
    for q in range(4):
        pair_part[q] = pairs[:, q * 128 : (q + 1) * 128]
    each(pair_copy, 0, "start")
    for o in range(2):
        w_copy(0, o).wait()

    pair = z // 2
    turned = 1 - 2 * (z % 2)
    order = (pair, mod4(pair - turned), mod4(pair + turned), mod4(pair + 2))

    def first_products(j):
        g = order[j]

        def one(k, carry):
            rows_all[g * 4 + k] = norm(raw_all[g * 4 + k], stat_all[g * 2 + k // 2, k % 2])
            return carry

        lax.fori_loop(0, QUARTERS, one, 0)
        products(0, g)
        for o, i in both:
            quarter_copy(j, g, o, i).start()

    z_step(raw_all, zx, 2)
    stat_step(1)
    sib_wait(raw_all, zx, 0, 1, -1)
    first_products(0)
    each(pair_copy, 0, "wait")
    pair_sum[...] = (
        pair_part[x].astype(F32)
        + pair_in[0, 0].astype(F32)
        + pair_in[0, 1].astype(F32)
        + pair_in[0, 2].astype(F32)
    ).astype(BF16)
    each(pair_copy, 1, "start")
    z_step(raw_all, zx, 3)
    stat_step(2)
    sib_wait(raw_all, zx, 2, -2)
    first_products(1)
    each(pair_copy, 1, "wait")
    pair_all[x] = (
        pair_sum[...].astype(F32)
        + pair_in[1, 0].astype(F32)
        + pair_in[1, 1].astype(F32)
        + pair_in[1, 2].astype(F32)
    ).astype(BF16)
    each(pair_copy, 2, "start")
    z_step(raw_all, zx, 4)
    stat_step(3)
    sib_wait(raw_all, zx, 3, -3)
    first_products(2)
    stat_step(4)
    sib_wait(raw_all, zx, 4)
    first_products(3)
    each(pair_copy, 2, "wait")
    for i in range(2):
        for copy in turn_copies(i):
            copy.wait()
    first, second = pair_all[0].astype(F32), pair_all[1].astype(F32)
    kv_all[ffn, :, 0:128] = (first * turn[1, 0] - second * turn[1, 1]).astype(BF16)
    kv_all[ffn, :, 128:256] = (first * turn[1, 1] + second * turn[1, 0]).astype(BF16)
    kv_all[ffn, :, 256:384] = pair_all[2]
    kv_all[ffn, :, 384:512] = pair_all[3]
    z_start(kv_all, zk)

    for s in range(1, STEPS):
        for o in range(2):
            w_copy(s, o).wait()
    for u in range(UNITS):
        wb_copy(u).wait()

    far1 = ((6, 4), (10, 4))
    near1 = ((4, 2), (14, 2))
    far2 = ((3, 2), (5, 2))
    near2 = ((2, 1), (7, 1))

    def rs_copy(s, o, k, i):
        first, size = (far1, near1, far2, near2)[k][i]
        at = o * 8 + k * 2 + i
        if k < 2:
            src = part.at[s, o, :, pl.ds(first, size)]
        else:
            src = half_sum.at[s, o, pl.ds(first, size)]
        return remote(
            src,
            (land1, last1, land2, last2)[k].at[s, o, i],
            rs_s.at[s, at],
            rs_r.at[s, at],
            devs[o][k // 2](dirs[i]),
        )

    def phase0(s):
        def tile(g, carry):
            products(s, g)
            return carry

        lax.fori_loop(0, QUARTERS, tile, 0)
        for o, i in both:
            rs_copy(s, o, 0, i).start()

    def added(first, *rest):
        res = first.astype(F32)
        for one in rest:
            res += one.astype(F32)
        return res

    def phase1(s):
        @pl.when(s == 0)
        def _():
            for j in range(QUARTERS):
                for o, i in both:
                    quarter_copy(j, order[j], o, i).wait()

        @pl.when(s > 0)
        def _():
            for o, i in both:
                rs_copy(s, o, 0, i).wait()

        for o, i in both:
            first, size = near1[i]
            part[s, o, :, first : first + size] = added(
                part[s, o, :, first : first + size], land1[s, o, i, :, 2 - 2 * i : 4 - 2 * i]
            ).astype(BF16)
            rs_copy(s, o, 1, i).start()

    def phase2(s):
        for o in range(2):
            for i in range(2):
                rs_copy(s, o, 1, i).wait()
            for i in range(2):
                cut = slice(2 - 2 * i, 4 - 2 * i)
                res = added(
                    part[s, o, :, 2 * i : 2 * i + 2],
                    last1[s, o, i],
                    land1[s, o, 1 - i, :, cut],
                ).astype(BF16)
                for b in range(2):
                    for r in range(2):
                        half_sum[s, o, (2 * i + b) * 2 + r] = res[2 * r : 2 * r + 2, b].reshape(
                            HALF, WIDE
                        )
            for i in range(2):
                rs_copy(s, o, 2, i).start()

    def phase3(s):
        for o, i in both:
            rs_copy(s, o, 2, i).wait()
            first = near2[i][0]
            half_sum[s, o, first] = added(half_sum[s, o, first], land2[s, o, i, 1 - i]).astype(BF16)
            rs_copy(s, o, 3, i).start()

    def attend(left, right):
        seg_row = seg[...].astype(F32)
        key_at = lax.broadcasted_iota(jnp.int32, (ROWS, TOKENS), 1)
        row_at = lax.broadcasted_iota(jnp.int32, (ROWS, TOKENS), 0)
        row_at = row_at + (TOKENS // QUARTERS - QUARTER) * (row_at // QUARTER) + hid * QUARTER
        own = jnp.sum(jnp.where(key_at == row_at, seg_row, 0.0), 1, keepdims=True)
        allowed = (key_at <= row_at) & (seg_row == own)
        keys = kv_all[:, :, 0:HEAD].reshape(TOKENS, HEAD)
        vals = kv_all[:, :, HEAD : 2 * HEAD].reshape(TOKENS, HEAD)
        cosine, sine = turn[0, 0] * HEAD**-0.5, turn[0, 1] * HEAD**-0.5
        groups = [v[:, k * 128 : (k + 1) * 128] for v in (left, right) for k in range(3)]
        pieces = []
        for h in range(3):
            a, b = groups[2 * h], groups[2 * h + 1]
            query = jnp.concatenate([a * cosine - b * sine, a * sine + b * cosine], 1).astype(BF16)
            scores = lax.dot_general(
                query, keys, (((1,), (1,)), ((), ())), preferred_element_type=F32
            )
            expos = jnp.where(allowed, jnp.exp(scores), 0.0)
            probs = (expos / jnp.sum(expos, 1, keepdims=True)).astype(BF16)
            res = jnp.dot(probs, vals, preferred_element_type=F32).astype(BF16)
            pieces += [res[:, 0:128], res[:, 128:256]]
        return jnp.concatenate(pieces[:3], 1), jnp.concatenate(pieces[3:], 1)

    def put(u, block):
        mixed[u, 0, 0, 0] = block[0:HALF]
        mixed[u, 1, 0, 0] = block[HALF:ROWS]

    def gather_copy(u, o, k, i):
        d = dirs[i]
        away, near = (3, 1)[i], (3, 1)[i]
        dev = devs[o][k // 2](d)
        if k == 0:
            src, dst = mixed.at[u, o, 0, 0], mixed.at[u, o, 0, away]
        elif k == 1:
            rows = pl.ds(i * QUARTER, QUARTER)
            src, dst = mixed.at[u, o, 0, near, rows], mixed.at[u, o, 0, 2, rows]
        elif k == 2:
            src, dst = mixed.at[u, o, 0], mixed.at[u, o, away]
        else:
            cut = pl.ds(2 * i, 2)
            src, dst = mixed.at[u, o, near, cut], mixed.at[u, o, 2, cut]
        at = o * 8 + k * 2 + i
        return remote(src, dst, ag_s.at[u, at], ag_r.at[u, at], dev)

    def phase4(s):
        sums = []
        for o in range(2):
            for i in range(2):
                rs_copy(s, o, 3, i).wait()
            sums.append(
                jnp.concatenate(
                    [
                        half_sum[s, o, i].astype(F32)
                        + last2[s, o, i, 0].astype(F32)
                        + land2[s, o, 1 - i, 1 - i].astype(F32)
                        for i in range(2)
                    ],
                    0,
                )
            )

        @pl.when(s == 0)
        def _():
            left, right = attend(*sums)
            put(0, left)
            put(1, right)
            for u in range(2):
                for o, i in both:
                    gather_copy(u, o, 0, i).start()

        @pl.when(s > 0)
        def _():
            gate, up = sums
            put(s + 1, (gate / (1.0 + jnp.exp(-gate)) * up).astype(BF16))
            for o, i in both:
                gather_copy(s + 1, o, 0, i).start()

    def phase5(u):
        for o, i in both:
            gather_copy(u, o, 0, i).wait()
            gather_copy(u, o, 1, i).start()

    def phase6(u):
        for o in range(2):
            for i in range(2):
                gather_copy(u, o, 1, i).wait()
            for i in range(2):
                gather_copy(u, o, 2, i).start()

    def phase7(u):
        for o, i in both:
            gather_copy(u, o, 2, i).wait()
            gather_copy(u, o, 3, i).start()

    def phase8(u):
        for o in range(2):
            for i in range(2):
                gather_copy(u, o, 3, i).wait()
            for p in range(2):
                rows = mixed[u, o, 2 * p : 2 * p + 2].reshape(2 * SIDE * HALF, WIDE)
                total[o, p * 256 : (p + 1) * 256] += jnp.dot(
                    rows, w_back[u], preferred_element_type=F32
                )

    def slot(t, carry):
        pl.when(t < STEPS)(lambda: phase0(t))
        for k, fn in ((1, phase1), (2, phase2), (3, phase3)):
            s = t - k
            pl.when((s >= 0) & (s < STEPS))(lambda fn=fn, s=s: fn(s))

        for j in range(1, 5):

            @pl.when(t == j)
            def _(j=j):
                z_step(kv_all, zk, j)
                if j == 4:
                    sib_wait(kv_all, zk, 0, 1, -1, 2, -2, 3, -3, 4)

        s4 = t - 4
        pl.when((s4 >= 0) & (s4 < STEPS))(lambda: phase4(s4))

        for k, fn in ((5, phase5), (6, phase6), (7, phase7), (8, phase8)):
            s = t - k

            @pl.when((s >= 0) & (s < STEPS))
            def _(fn=fn, s=s):
                def unit(u, c):
                    fn(u)
                    return c

                lax.fori_loop(jnp.where(s == 0, 0, s + 1), s + 2, unit, 0)

        return carry

    lax.fori_loop(1, STEPS + 8, slot, 0)

    offsets = (4, 3, -3, 2, -2, 1, -1, 0)

    def half_rows(block, h):
        g = block // SIDE
        o = g // 2
        px = mod4(block % SIDE - x)
        pieces = []
        for k in (2 * h, 2 * h + 1):
            place = jnp.where(o == 0, rel_y[k] * SIDE + px, px * SIDE + rel_y[k])
            first = pl.multiple_of(place * HALF + (g % 2) * QUARTER, QUARTER)
            pieces.append(total[o, pl.ds(first, QUARTER)])
        return jnp.concatenate(pieces, 0)

    def sib_sum(k):
        at = mod8(z + offsets[k])
        return remote(sib_out.at[at], sib_in.at[at], zr_s.at[k], zr_r.at[k], sibling)

    for k in range(RING):
        at = mod8(z + offsets[k])
        for h in range(2):
            sib_out[at, h * HALF : (h + 1) * HALF] = half_rows(at * 2 + 1 - core, h).astype(BF16)
        sib_sum(k).start()

    def chip_sum(k, h):
        at = mod8(z + offsets[k])
        return half_rows(at * 2 + core, h) + sib_in[at, h * HALF : (h + 1) * HALF].astype(F32)

    def ring_copy(j, i, h):
        at = 8 + j * 4 + i * 2 + h
        return remote(
            ring_out.at[j, i, h], ring_in.at[j, i, h], zr_s.at[at], zr_r.at[at], dev_z(dirs[i])
        )

    sib_sum(0).wait()
    for i in range(2):
        ring_out[0, i, i] = chip_sum(0, i).astype(BF16)
        ring_copy(0, i, i).start()
    for j in (1, 2, 3):
        for i in range(2):
            sib_sum(2 * j - 1 + i).wait()
        for turn_of in range(2):
            for i in range(2):
                h = (1 - i, i)[turn_of]
                here = chip_sum(2 * j - 1 + i, h)
                if j > 1 or h == i:
                    ring_copy(j - 1, i, h).wait()
                    here += ring_in[j - 1, i, h].astype(F32)
                ring_out[j, i, h] = here.astype(BF16)
                ring_copy(j, i, h).start()
    sib_sum(7).wait()
    for h in range(2):
        here = chip_sum(7, h) + act[h * HALF : (h + 1) * HALF].astype(F32)
        for i in range(2):
            ring_copy(3, i, h).wait()
            here += ring_in[3, i, h].astype(F32)
        out[h * HALF : (h + 1) * HALF] = here.astype(BF16)


def per_device(activations, ln_gain, segments, w_query, w_key_value, w_gate, w_up, w_out, w_down):
    vmem = pl.BlockSpec(memory_space=pltpu.VMEM)
    anywhere = pl.BlockSpec(memory_space=pl.ANY)
    dma = pltpu.SemaphoreType.DMA
    scratch = [
        pltpu.VMEM((STEPS, FEATS, 2 * WIDE), BF16),
        pltpu.VMEM((UNITS, WIDE, FEATS), BF16),
        pltpu.VMEM((FEATS, 512), BF16),
        pltpu.VMEM((2, 2, ROWS, 128), F32),
        pltpu.VMEM((2, 8, 128), F32),
        pltpu.VMEM((2, 3, 8, 128), F32),
        pltpu.VMEM((RING, 2, 8, 128), F32),
        pltpu.VMEM((GROUP, ROWS, FEATS), BF16),
        pltpu.VMEM((GROUP, ROWS, FEATS), BF16),
        pltpu.VMEM((4, ROWS, 128), BF16),
        pltpu.VMEM((2, 3, ROWS, 128), BF16),
        pltpu.VMEM((ROWS, 128), BF16),
        pltpu.VMEM((4, ROWS, 128), BF16),
        pltpu.VMEM((GROUP, ROWS, 512), BF16),
        pltpu.VMEM((STEPS, 2, QUARTERS, GROUP, QUARTER, WIDE), BF16),
        pltpu.VMEM((STEPS, 2, 2, QUARTERS, 4, QUARTER, WIDE), BF16),
        pltpu.VMEM((STEPS, 2, 2, QUARTERS, 2, QUARTER, WIDE), BF16),
        pltpu.VMEM((STEPS, 2, 2 * SIDE, HALF, WIDE), BF16),
        pltpu.VMEM((STEPS, 2, 2, 2, HALF, WIDE), BF16),
        pltpu.VMEM((STEPS, 2, 2, 1, HALF, WIDE), BF16),
        pltpu.VMEM((UNITS, 2, SIDE, SIDE, HALF, WIDE), BF16),
        pltpu.VMEM((2, GROUP * HALF, FEATS), F32),
        pltpu.VMEM((RING, ROWS, FEATS), BF16),
        pltpu.VMEM((RING, ROWS, FEATS), BF16),
        pltpu.VMEM((4, 2, 2, HALF, FEATS), BF16),
        pltpu.VMEM((4, 2, 2, HALF, FEATS), BF16),
        dma((STEPS, 2)),
        dma((UNITS,)),
        dma((11,)),
        dma((5, 3)),
        dma((5, 3)),
        dma((8, 2)),
        dma((8, 2)),
        dma((5, 2)),
        dma((5, 2)),
        dma((QUARTERS, 4)),
        dma((QUARTERS, 4)),
        dma((8, 2)),
        dma((8, 2)),
        dma((STEPS, 16)),
        dma((STEPS, 16)),
        dma((UNITS, 16)),
        dma((UNITS, 16)),
        dma((24,)),
        dma((24,)),
    ]
    return pl.pallas_call(
        block_kernel,
        out_shape=jax.ShapeDtypeStruct((ROWS, FEATS), BF16),
        in_specs=[vmem, vmem, vmem] + [anywhere] * 7,
        out_specs=vmem,
        scratch_shapes=scratch,
        compiler_params=pltpu.CompilerParams(
            collective_id=0, has_side_effects=True, vmem_limit_bytes=60 * 1024 * 1024
        ),
    )(
        activations,
        ln_gain,
        segments.reshape(1, TOKENS),
        jnp.asarray(tables()),
        w_query,
        w_key_value,
        w_gate,
        w_up,
        w_out,
        w_down,
    )


def solution(mesh):
    placed = (
        P("ffn", "hid"),
        P("hid"),
        P(),
        P("hid", "ffn"),
        P("hid", None),
        P("hid", "ffn"),
        P("hid", "ffn"),
        P("ffn", "hid"),
        P("ffn", "hid"),
    )
    return jax.shard_map(
        per_device, mesh=mesh, in_specs=placed, out_specs=P("ffn", "hid"), check_vma=False
    )
```

```python
import jax
import jax.numpy as jnp
import numpy as np
from jax import lax
from jax.experimental import pallas as pl
from jax.experimental.pallas import tpu as pltpu
from jax.sharding import PartitionSpec as P

D = 10240
HEAD = 256
TOKENS = 1024
EPSILON = 1e-06

SIDE = 4
RING = 8
GROUP = SIDE * SIDE
ROWS = TOKENS // GROUP
FEATS = D // GROUP
WIDE = 384
STEPS = 7
EARLY = 2
UNITS = 8
HALF = ROWS // 2
QUARTERS = 4
QUARTER = ROWS // 4
F32 = jnp.float32
BF16 = jnp.bfloat16


def tables():
    half = HEAD // 2
    frequency = np.float32(10000.0) ** (-np.arange(half, dtype=np.float32) / np.float32(half))
    angles = np.arange(TOKENS, dtype=np.float32)[:, None] * frequency[None, :].astype(np.float32)
    wide = angles.astype(np.float64)
    return np.stack([np.cos(wide), np.sin(wide)]).astype(np.float32)


def block_kernel(
    act,
    gain,
    seg,
    table,
    w_query,
    w_pairs,
    w_gate,
    w_up,
    w_out,
    w_down,
    out,
    w_in,
    w_back,
    w_kv,
    turn,
    stat,
    stat_in,
    stat_all,
    raw_all,
    rows_all,
    pair_part,
    pair_in,
    pair_sum,
    pair_all,
    kv_all,
    part,
    land1,
    last1,
    half_sum,
    land2,
    last2,
    mixed,
    total,
    sib_out,
    sib_in,
    ring_out,
    ring_in,
    w_sem,
    wb_sem,
    m_sem,
    small_s,
    small_r,
    zx_s,
    zx_r,
    zt_s,
    zt_r,
    rq_s,
    rq_r,
    zk_s,
    zk_r,
    rs_s,
    rs_r,
    ag_s,
    ag_r,
    zr_s,
    zr_r,
):
    hid = lax.axis_index("hid")
    ffn = lax.axis_index("ffn")
    x, y = hid // SIDE, hid % SIDE
    z, core = ffn // 2, ffn % 2

    def mod4(v):
        return (v + SIDE) % SIDE

    def mod8(v):
        return (v + RING) % RING

    ids_x = {d: mod4(x + d) * SIDE + y for d in (1, 2, 3)}
    ids_y = {d: x * SIDE + mod4(y + d) for d in (1, 2, 3)}
    ids_z = {d: mod8(z + d) * 2 + core for d in (1, -1)}

    def dev_x(d):
        return (ids_x[d % SIDE], ffn)

    def dev_y(d):
        return (ids_y[d % SIDE], ffn)

    def dev_z(d):
        return (hid, ids_z[d])

    sibling = (hid, z * 2 + 1 - core)
    dirs = (1, -1)
    devs = ((dev_x, dev_y), (dev_y, dev_x))

    barrier = pltpu.get_barrier_semaphore()
    partners = [dev_x(d) for d in (1, 2, 3)] + [dev_y(d) for d in (1, 2, 3)]
    partners += [dev_z(1), dev_z(-1), sibling]
    for dev in partners:
        pl.semaphore_signal(barrier, inc=1, device_id=dev, device_id_type=pl.DeviceIdType.MESH)

    def remote(src, dst, ssem, rsem, dev):
        return pltpu.make_async_remote_copy(
            src_ref=src,
            dst_ref=dst,
            send_sem=ssem,
            recv_sem=rsem,
            device_id=dev,
            device_id_type=pl.DeviceIdType.MESH,
        )

    def w_copy(s, o):
        if s == 0:
            src = w_query.at[:, pl.ds(o * WIDE, WIDE)]
        else:
            src = (w_gate, w_up)[o].at[:, pl.ds((s - 1) * WIDE, WIDE)]
        return pltpu.make_async_copy(src, w_in.at[s, :, pl.ds(o * WIDE, WIDE)], w_sem.at[s, o])

    def wb_copy(u):
        if u < 2:
            src = w_out.at[pl.ds(u * WIDE, WIDE)]
        else:
            src = w_down.at[pl.ds((u - 2) * WIDE, WIDE)]
        return pltpu.make_async_copy(src, w_back.at[u], wb_sem.at[u])

    def turn_copies(i):
        copies = [
            pltpu.make_async_copy(
                table.at[i, pl.ds(pl.multiple_of(ffn * ROWS, ROWS), ROWS)],
                turn.at[1, i],
                m_sem.at[1 + 5 * i],
            )
        ]
        for g in range(QUARTERS):
            first = pl.multiple_of(g * (TOKENS // QUARTERS) + hid * QUARTER, QUARTER)
            copies.append(
                pltpu.make_async_copy(
                    table.at[i, pl.ds(first, QUARTER)],
                    turn.at[0, i, pl.ds(g * QUARTER, QUARTER)],
                    m_sem.at[2 + 5 * i + g],
                )
            )
        return copies

    kv_copy = pltpu.make_async_copy(w_pairs, w_kv, m_sem.at[0])

    pl.semaphore_wait(barrier, len(partners))

    def stat_copy(a, d):
        return remote(
            stat.at[a], stat_in.at[a, d - 1], small_s.at[a, d - 1], small_r.at[a, d - 1],
            (dev_x, dev_y)[a](d),
        )

    def pair_copy(k, d):
        if k == 0:
            src, dst, dev = pair_part.at[mod4(x + d)], pair_in.at[0, d - 1], dev_x(d)
        elif k == 1:
            src, dst, dev = pair_sum, pair_in.at[1, d - 1], dev_y(d)
        else:
            src, dst, dev = pair_all.at[x], pair_all.at[x], dev_x(d)
        return remote(src, dst, small_s.at[2 + k, d - 1], small_r.at[2 + k, d - 1], dev)

    def each(fn, k, what):
        for d in (1, 2, 3):
            getattr(fn(k, d), what)()

    def z_copy(buf, sems, j, i):
        d = dirs[i]
        block = mod8(z - (j - 1) * d) * 2 + core
        ref = buf.at[block] if j < 4 else buf.at[block, pl.ds(i * HALF, HALF)]
        return remote(ref, ref, sems[0].at[j - 1, i], sems[1].at[j - 1, i], dev_z(d))

    def sib_copy(buf, sems, off):
        ref = buf.at[mod8(z + off) * 2 + core]
        row = 4 + (off + 3) // 2
        col = (off + 3) % 2
        return remote(ref, ref, sems[0].at[row, col], sems[1].at[row, col], sibling)

    def z_start(buf, sems):
        for i in range(2):
            z_copy(buf, sems, 1, i).start()
        sib_copy(buf, sems, 0).start()

    def z_step(buf, sems, j):
        if j < 4:
            for i in range(2):
                z_copy(buf, sems, j, i).wait()
                z_copy(buf, sems, j + 1, i).start()
                sib_copy(buf, sems, -j * dirs[i]).start()
        else:
            for i in range(2):
                z_copy(buf, sems, j, i).wait()
            sib_copy(buf, sems, 4).start()

    def sib_wait(buf, sems, *offs):
        for off in offs:
            sib_copy(buf, sems, off).wait()

    def stat_z(j, i):
        ref = stat_all.at[mod8(z - (j - 1) * dirs[i])]
        return remote(ref, ref, zt_s.at[j, i], zt_r.at[j, i], dev_z(dirs[i]))

    def stat_step(j):
        for i in range(2):
            if (j, i) == (4, 1):
                continue
            stat_z(j, i).wait()
            if j < 3 + (i == 0):
                stat_z(j + 1, i).start()

    def quarter_copy(s, j, g, o, i):
        at = o * 2 + i
        return remote(
            part.at[s, o, g, pl.ds((6, 10)[i], 4)],
            land1.at[s, o, i, g],
            rq_s.at[s * QUARTERS + j, at],
            rq_r.at[s * QUARTERS + j, at],
            devs[o][0](dirs[i]),
        )

    both = [(o, i) for o in range(2) for i in range(2)]
    rel_x = [mod4(k - x) for k in range(SIDE)]
    rel_y = [mod4(k - y) for k in range(SIDE)]
    places = (
        [rel_x[h // SIDE] * SIDE + rel_y[h % SIDE] for h in range(GROUP)],
        [rel_y[h % SIDE] * SIDE + rel_x[h // SIDE] for h in range(GROUP)],
    )

    def products(s, g):
        rows = rows_all[pl.ds(g * QUARTERS, QUARTERS)].reshape(QUARTERS * ROWS, FEATS)
        res = jnp.dot(rows, w_in[s], preferred_element_type=F32).astype(BF16)
        for h in range(GROUP):
            block = res[h * QUARTER : (h + 1) * QUARTER]
            for o in range(2):
                part[s, o, g, places[o][h]] = block[:, o * WIDE : (o + 1) * WIDE]

    eye = lax.broadcasted_iota(jnp.int32, (ROWS, 128), 0) == lax.broadcasted_iota(
        jnp.int32, (ROWS, 128), 1
    )
    line = lax.broadcasted_iota(jnp.int32, (8, 128), 0)

    def to_row(column):
        return jnp.sum(jnp.where(eye, column, 0.0), 0, keepdims=True)

    def to_column(row):
        return jnp.sum(jnp.where(eye, row, 0.0), 1, keepdims=True)

    def norm(rows, tile):
        mean, scale = to_column(tile[0:1]), to_column(tile[1:2])
        return ((rows.astype(F32) - mean) * scale * gain[...].reshape(1, FEATS)).astype(BF16)

    zx = (zx_s, zx_r)
    zk = (zk_s, zk_r)
    raw_all[ffn] = act[...]
    z_start(raw_all, zx)
    values = act[...].astype(F32)
    mean = jnp.mean(values, 1, keepdims=True)
    square = jnp.sum((values - mean) ** 2, 1, keepdims=True)
    mean, square = to_row(mean), to_row(square)
    for a, count in ((0, FEATS), (1, FEATS * SIDE)):
        stat[a] = jnp.where(line == 0, mean, square)
        each(stat_copy, a, "start")
        if a == 0:
            kv_copy.start()
            for s in range(EARLY):
                for o in range(2):
                    w_copy(s, o).start()
            total[...] = jnp.zeros_like(total)
        else:
            for s in range(EARLY, STEPS):
                for o in range(2):
                    w_copy(s, o).start()
            z_step(raw_all, zx, 1)
        each(stat_copy, a, "wait")
        means = [mean] + [stat_in[a, d, 0:1] for d in range(3)]
        squares = [square] + [stat_in[a, d, 1:2] for d in range(3)]
        mean = (means[0] + means[1] + means[2] + means[3]) * 0.25
        square = squares[0] + squares[1] + squares[2] + squares[3]
        for one in means:
            square += count * (one - mean) ** 2
    scale = lax.rsqrt(square * (1.0 / D) + EPSILON)
    stat_all[z, core] = jnp.where(line == 0, mean, scale)
    stat_sib = remote(
        stat_all.at[z, core], stat_all.at[z, core], zt_s.at[0, 0], zt_r.at[0, 0], sibling
    )
    stat_sib.start()
    normed = norm(act[...], stat_all[z, core])
    stat_sib.wait()
    for i in range(2):
        stat_z(1, i).start()
    kv_copy.wait()
    pairs = jnp.dot(normed, w_kv[...], preferred_element_type=F32).astype(BF16)
    for q in range(4):
        pair_part[q] = pairs[:, q * 128 : (q + 1) * 128]
    each(pair_copy, 0, "start")
    for i in range(2):
        for copy in turn_copies(i):
            copy.start()
    for u in range(UNITS):
        wb_copy(u).start()
    for s in range(EARLY):
        for o in range(2):
            w_copy(s, o).wait()

    pair = z // 2
    turned = 1 - 2 * (z % 2)
    order = (pair, mod4(pair - turned), mod4(pair + turned), mod4(pair + 2))

    def first_products(j):
        g = order[j]

        def one(k, carry):
            rows_all[g * 4 + k] = norm(raw_all[g * 4 + k], stat_all[g * 2 + k // 2, k % 2])
            return carry

        lax.fori_loop(0, QUARTERS, one, 0)
        for s in range(EARLY):
            products(s, g)
            for o, i in both:
                quarter_copy(s, j, g, o, i).start()

    z_step(raw_all, zx, 2)
    stat_step(1)
    sib_wait(raw_all, zx, 0, 1, -1)
    first_products(0)
    each(pair_copy, 0, "wait")
    pair_sum[...] = (
        pair_part[x].astype(F32)
        + pair_in[0, 0].astype(F32)
        + pair_in[0, 1].astype(F32)
        + pair_in[0, 2].astype(F32)
    ).astype(BF16)
    each(pair_copy, 1, "start")
    z_step(raw_all, zx, 3)
    stat_step(2)
    sib_wait(raw_all, zx, 2, -2)
    first_products(1)
    each(pair_copy, 1, "wait")
    pair_all[x] = (
        pair_sum[...].astype(F32)
        + pair_in[1, 0].astype(F32)
        + pair_in[1, 1].astype(F32)
        + pair_in[1, 2].astype(F32)
    ).astype(BF16)
    each(pair_copy, 2, "start")
    z_step(raw_all, zx, 4)
    stat_step(3)
    sib_wait(raw_all, zx, 3, -3)
    first_products(2)
    stat_step(4)
    sib_wait(raw_all, zx, 4)
    first_products(3)
    each(pair_copy, 2, "wait")
    for i in range(2):
        for copy in turn_copies(i):
            copy.wait()
    first, second = pair_all[0].astype(F32), pair_all[1].astype(F32)
    kv_all[ffn, :, 0:128] = (first * turn[1, 0] - second * turn[1, 1]).astype(BF16)
    kv_all[ffn, :, 128:256] = (first * turn[1, 1] + second * turn[1, 0]).astype(BF16)
    kv_all[ffn, :, 256:384] = pair_all[2]
    kv_all[ffn, :, 384:512] = pair_all[3]
    z_start(kv_all, zk)

    for s in range(EARLY, STEPS):
        for o in range(2):
            w_copy(s, o).wait()
    for u in range(UNITS):
        wb_copy(u).wait()

    far1 = ((6, 4), (10, 4))
    near1 = ((4, 2), (14, 2))
    far2 = ((3, 2), (5, 2))
    near2 = ((2, 1), (7, 1))

    def rs_copy(s, o, k, i):
        first, size = (far1, near1, far2, near2)[k][i]
        at = o * 8 + k * 2 + i
        if k < 2:
            src = part.at[s, o, :, pl.ds(first, size)]
        else:
            src = half_sum.at[s, o, pl.ds(first, size)]
        return remote(
            src,
            (land1, last1, land2, last2)[k].at[s, o, i],
            rs_s.at[s, at],
            rs_r.at[s, at],
            devs[o][k // 2](dirs[i]),
        )

    def phase0(s):
        def tile(g, carry):
            products(s, g)
            return carry

        lax.fori_loop(0, QUARTERS, tile, 0)
        for o, i in both:
            rs_copy(s, o, 0, i).start()

    def added(first, *rest):
        res = first.astype(F32)
        for one in rest:
            res += one.astype(F32)
        return res

    def phase1(s):
        @pl.when(s < EARLY)
        def _():
            for j in range(QUARTERS):
                for o, i in both:
                    quarter_copy(s, j, order[j], o, i).wait()

        @pl.when(s >= EARLY)
        def _():
            for o, i in both:
                rs_copy(s, o, 0, i).wait()

        for o, i in both:
            first, size = near1[i]
            part[s, o, :, first : first + size] = added(
                part[s, o, :, first : first + size], land1[s, o, i, :, 2 - 2 * i : 4 - 2 * i]
            ).astype(BF16)
            rs_copy(s, o, 1, i).start()

    def phase2(s):
        for o in range(2):
            for i in range(2):
                rs_copy(s, o, 1, i).wait()
            for i in range(2):
                cut = slice(2 - 2 * i, 4 - 2 * i)
                res = added(
                    part[s, o, :, 2 * i : 2 * i + 2],
                    last1[s, o, i],
                    land1[s, o, 1 - i, :, cut],
                ).astype(BF16)
                for b in range(2):
                    for r in range(2):
                        half_sum[s, o, (2 * i + b) * 2 + r] = res[2 * r : 2 * r + 2, b].reshape(
                            HALF, WIDE
                        )
            for i in range(2):
                rs_copy(s, o, 2, i).start()

    def phase3(s):
        for o, i in both:
            rs_copy(s, o, 2, i).wait()
            first = near2[i][0]
            half_sum[s, o, first] = added(half_sum[s, o, first], land2[s, o, i, 1 - i]).astype(BF16)
            rs_copy(s, o, 3, i).start()

    def attend(left, right):
        seg_row = seg[...].astype(F32)
        key_at = lax.broadcasted_iota(jnp.int32, (ROWS, TOKENS), 1)
        row_at = lax.broadcasted_iota(jnp.int32, (ROWS, TOKENS), 0)
        row_at = row_at + (TOKENS // QUARTERS - QUARTER) * (row_at // QUARTER) + hid * QUARTER
        own = jnp.sum(jnp.where(key_at == row_at, seg_row, 0.0), 1, keepdims=True)
        allowed = (key_at <= row_at) & (seg_row == own)
        keys = kv_all[:, :, 0:HEAD].reshape(TOKENS, HEAD)
        vals = kv_all[:, :, HEAD : 2 * HEAD].reshape(TOKENS, HEAD)
        cosine, sine = turn[0, 0] * HEAD**-0.5, turn[0, 1] * HEAD**-0.5
        groups = [v[:, k * 128 : (k + 1) * 128] for v in (left, right) for k in range(3)]
        query = []
        for h in range(3):
            a, b = groups[2 * h], groups[2 * h + 1]
            query.append(jnp.concatenate([a * cosine - b * sine, a * sine + b * cosine], 1))
        scores = lax.dot_general(
            jnp.concatenate(query, 0).astype(BF16),
            keys,
            (((1,), (1,)), ((), ())),
            preferred_element_type=F32,
        )
        probs = []
        for h in range(3):
            expos = jnp.where(allowed, jnp.exp(scores[h * ROWS : (h + 1) * ROWS]), 0.0)
            probs.append((expos / jnp.sum(expos, 1, keepdims=True)).astype(BF16))
        res = jnp.dot(jnp.concatenate(probs, 0), vals, preferred_element_type=F32).astype(BF16)
        pieces = [
            res[h * ROWS : (h + 1) * ROWS, k * 128 : (k + 1) * 128]
            for h in range(3)
            for k in range(2)
        ]
        return jnp.concatenate(pieces[:3], 1), jnp.concatenate(pieces[3:], 1)

    def put(u, block):
        mixed[u, 0, 0, 0] = block[0:HALF]
        mixed[u, 1, 0, 0] = block[HALF:ROWS]

    def gather_copy(u, o, k, i):
        d = dirs[i]
        away, near = (3, 1)[i], (3, 1)[i]
        dev = devs[o][k // 2](d)
        if k == 0:
            src, dst = mixed.at[u, o, 0, 0], mixed.at[u, o, 0, away]
        elif k == 1:
            rows = pl.ds(i * QUARTER, QUARTER)
            src, dst = mixed.at[u, o, 0, near, rows], mixed.at[u, o, 0, 2, rows]
        elif k == 2:
            src, dst = mixed.at[u, o, 0], mixed.at[u, o, away]
        else:
            cut = pl.ds(2 * i, 2)
            src, dst = mixed.at[u, o, near, cut], mixed.at[u, o, 2, cut]
        at = o * 8 + k * 2 + i
        return remote(src, dst, ag_s.at[u, at], ag_r.at[u, at], dev)

    def phase4(s):
        sums = []
        for o in range(2):
            for i in range(2):
                rs_copy(s, o, 3, i).wait()
            sums.append(
                jnp.concatenate(
                    [
                        half_sum[s, o, i].astype(F32)
                        + last2[s, o, i, 0].astype(F32)
                        + land2[s, o, 1 - i, 1 - i].astype(F32)
                        for i in range(2)
                    ],
                    0,
                )
            )

        @pl.when(s == 0)
        def _():
            left, right = attend(*sums)
            put(0, left)
            put(1, right)
            for u in range(2):
                for o, i in both:
                    gather_copy(u, o, 0, i).start()

        @pl.when(s > 0)
        def _():
            gate, up = sums
            put(s + 1, (gate / (1.0 + jnp.exp(-gate)) * up).astype(BF16))
            for o, i in both:
                gather_copy(s + 1, o, 0, i).start()

    def phase5(u):
        for o, i in both:
            gather_copy(u, o, 0, i).wait()
            gather_copy(u, o, 1, i).start()

    def phase6(u):
        for o in range(2):
            for i in range(2):
                gather_copy(u, o, 1, i).wait()
            for i in range(2):
                gather_copy(u, o, 2, i).start()

    def phase7(u):
        for o, i in both:
            gather_copy(u, o, 2, i).wait()
            gather_copy(u, o, 3, i).start()

    def phase8(u):
        for o in range(2):
            for i in range(2):
                gather_copy(u, o, 3, i).wait()
            for p in range(2):
                rows = mixed[u, o, 2 * p : 2 * p + 2].reshape(2 * SIDE * HALF, WIDE)
                total[o, p * 256 : (p + 1) * 256] += jnp.dot(
                    rows, w_back[u], preferred_element_type=F32
                )

    def slot(t, carry):
        pl.when((t >= EARLY) & (t < STEPS))(lambda: phase0(t))
        for k, fn in ((1, phase1), (3, phase2), (4, phase3)):
            s = t - k
            pl.when((s >= 0) & (s < STEPS))(lambda fn=fn, s=s: fn(s))

        for j in range(1, 5):

            @pl.when(t == j)
            def _(j=j):
                z_step(kv_all, zk, j)
                if j == 4:
                    sib_wait(kv_all, zk, 0, 1, -1, 2, -2, 3, -3, 4)

        s4 = t - 5
        pl.when((s4 >= 0) & (s4 < STEPS))(lambda: phase4(s4))

        for k, fn in ((6, phase5), (7, phase6), (8, phase7), (9, phase8)):
            s = t - k

            @pl.when((s >= 0) & (s < STEPS))
            def _(fn=fn, s=s):
                def unit(u, c):
                    fn(u)
                    return c

                lax.fori_loop(jnp.where(s == 0, 0, s + 1), s + 2, unit, 0)

        return carry

    lax.fori_loop(1, STEPS + 9, slot, 0)

    offsets = (4, 3, -3, 2, -2, 1, -1, 0)

    def half_rows(block, h):
        g = block // SIDE
        o = g // 2
        px = mod4(block % SIDE - x)
        pieces = []
        for k in (2 * h, 2 * h + 1):
            place = jnp.where(o == 0, rel_y[k] * SIDE + px, px * SIDE + rel_y[k])
            first = pl.multiple_of(place * HALF + (g % 2) * QUARTER, QUARTER)
            pieces.append(total[o, pl.ds(first, QUARTER)])
        return jnp.concatenate(pieces, 0)

    def sib_sum(k):
        at = mod8(z + offsets[k])
        return remote(sib_out.at[at], sib_in.at[at], zr_s.at[k], zr_r.at[k], sibling)

    for k in range(RING):
        at = mod8(z + offsets[k])
        for h in range(2):
            sib_out[at, h * HALF : (h + 1) * HALF] = half_rows(at * 2 + 1 - core, h).astype(BF16)
        sib_sum(k).start()

    def chip_sum(k, h):
        at = mod8(z + offsets[k])
        return half_rows(at * 2 + core, h) + sib_in[at, h * HALF : (h + 1) * HALF].astype(F32)

    def ring_copy(j, i, h):
        at = 8 + j * 4 + i * 2 + h
        return remote(
            ring_out.at[j, i, h], ring_in.at[j, i, h], zr_s.at[at], zr_r.at[at], dev_z(dirs[i])
        )

    sib_sum(0).wait()
    for i in range(2):
        ring_out[0, i, i] = chip_sum(0, i).astype(BF16)
        ring_copy(0, i, i).start()
    for j in (1, 2, 3):
        for i in range(2):
            sib_sum(2 * j - 1 + i).wait()
        for turn_of in range(2):
            for i in range(2):
                h = (1 - i, i)[turn_of]
                here = chip_sum(2 * j - 1 + i, h)
                if j > 1 or h == i:
                    ring_copy(j - 1, i, h).wait()
                    here += ring_in[j - 1, i, h].astype(F32)
                ring_out[j, i, h] = here.astype(BF16)
                ring_copy(j, i, h).start()
    sib_sum(7).wait()
    for h in range(2):
        here = chip_sum(7, h) + act[h * HALF : (h + 1) * HALF].astype(F32)
        for i in range(2):
            ring_copy(3, i, h).wait()
            here += ring_in[3, i, h].astype(F32)
        out[h * HALF : (h + 1) * HALF] = here.astype(BF16)


def per_device(activations, ln_gain, segments, w_query, w_key_value, w_gate, w_up, w_out, w_down):
    vmem = pl.BlockSpec(memory_space=pltpu.VMEM)
    anywhere = pl.BlockSpec(memory_space=pl.ANY)
    dma = pltpu.SemaphoreType.DMA
    scratch = [
        pltpu.VMEM((STEPS, FEATS, 2 * WIDE), BF16),
        pltpu.VMEM((UNITS, WIDE, FEATS), BF16),
        pltpu.VMEM((FEATS, 512), BF16),
        pltpu.VMEM((2, 2, ROWS, 128), F32),
        pltpu.VMEM((2, 8, 128), F32),
        pltpu.VMEM((2, 3, 8, 128), F32),
        pltpu.VMEM((RING, 2, 8, 128), F32),
        pltpu.VMEM((GROUP, ROWS, FEATS), BF16),
        pltpu.VMEM((GROUP, ROWS, FEATS), BF16),
        pltpu.VMEM((4, ROWS, 128), BF16),
        pltpu.VMEM((2, 3, ROWS, 128), BF16),
        pltpu.VMEM((ROWS, 128), BF16),
        pltpu.VMEM((4, ROWS, 128), BF16),
        pltpu.VMEM((GROUP, ROWS, 512), BF16),
        pltpu.VMEM((STEPS, 2, QUARTERS, GROUP, QUARTER, WIDE), BF16),
        pltpu.VMEM((STEPS, 2, 2, QUARTERS, 4, QUARTER, WIDE), BF16),
        pltpu.VMEM((STEPS, 2, 2, QUARTERS, 2, QUARTER, WIDE), BF16),
        pltpu.VMEM((STEPS, 2, 2 * SIDE, HALF, WIDE), BF16),
        pltpu.VMEM((STEPS, 2, 2, 2, HALF, WIDE), BF16),
        pltpu.VMEM((STEPS, 2, 2, 1, HALF, WIDE), BF16),
        pltpu.VMEM((UNITS, 2, SIDE, SIDE, HALF, WIDE), BF16),
        pltpu.VMEM((2, GROUP * HALF, FEATS), F32),
        pltpu.VMEM((RING, ROWS, FEATS), BF16),
        pltpu.VMEM((RING, ROWS, FEATS), BF16),
        pltpu.VMEM((4, 2, 2, HALF, FEATS), BF16),
        pltpu.VMEM((4, 2, 2, HALF, FEATS), BF16),
        dma((STEPS, 2)),
        dma((UNITS,)),
        dma((11,)),
        dma((5, 3)),
        dma((5, 3)),
        dma((8, 2)),
        dma((8, 2)),
        dma((5, 2)),
        dma((5, 2)),
        dma((EARLY * QUARTERS, 4)),
        dma((EARLY * QUARTERS, 4)),
        dma((8, 2)),
        dma((8, 2)),
        dma((STEPS, 16)),
        dma((STEPS, 16)),
        dma((UNITS, 16)),
        dma((UNITS, 16)),
        dma((24,)),
        dma((24,)),
    ]
    return pl.pallas_call(
        block_kernel,
        out_shape=jax.ShapeDtypeStruct((ROWS, FEATS), BF16),
        in_specs=[vmem, vmem, vmem] + [anywhere] * 7,
        out_specs=vmem,
        scratch_shapes=scratch,
        compiler_params=pltpu.CompilerParams(
            collective_id=0, has_side_effects=True, vmem_limit_bytes=60 * 1024 * 1024
        ),
    )(
        activations,
        ln_gain,
        segments.reshape(1, TOKENS),
        jnp.asarray(tables()),
        w_query,
        w_key_value,
        w_gate,
        w_up,
        w_out,
        w_down,
    )


def solution(mesh):
    placed = (
        P("ffn", "hid"),
        P("hid"),
        P(),
        P("hid", "ffn"),
        P("hid", None),
        P("hid", "ffn"),
        P("hid", "ffn"),
        P("ffn", "hid"),
        P("ffn", "hid"),
    )
    return jax.shard_map(
        per_device, mesh=mesh, in_specs=placed, out_specs=P("ffn", "hid"), check_vma=False
    )
```

```python
import jax
import jax.numpy as jnp
import numpy as np
from jax import lax
from jax.experimental import pallas as pl
from jax.experimental.pallas import tpu as pltpu
from jax.sharding import PartitionSpec as P

D = 10240
HEAD = 256
TOKENS = 1024
EPSILON = 1e-06

SIDE = 4
RING = 8
GROUP = SIDE * SIDE
ROWS = TOKENS // GROUP
FEATS = D // GROUP
WIDE = 384
STEPS = 7
EARLY = 3
UNITS = 8
HALF = ROWS // 2
QUARTERS = 4
QUARTER = ROWS // 4
F32 = jnp.float32
BF16 = jnp.bfloat16


def tables():
    half = HEAD // 2
    frequency = np.float32(10000.0) ** (-np.arange(half, dtype=np.float32) / np.float32(half))
    angles = np.arange(TOKENS, dtype=np.float32)[:, None] * frequency[None, :].astype(np.float32)
    wide = angles.astype(np.float64)
    return np.stack([np.cos(wide), np.sin(wide)]).astype(np.float32)


def block_kernel(
    act,
    gain,
    seg,
    table,
    w_query,
    w_pairs,
    w_gate,
    w_up,
    w_out,
    w_down,
    out,
    w_in,
    w_back,
    w_kv,
    turn,
    stat,
    stat_in,
    stat_other,
    stat_all,
    raw_all,
    rows_all,
    pair_part,
    pair_in,
    pair_sum,
    pair_all,
    kv_all,
    part,
    land1,
    last1,
    half_sum,
    land2,
    last2,
    mixed,
    total,
    sib_out,
    sib_in,
    ring_out,
    ring_in,
    w_sem,
    wb_sem,
    m_sem,
    small_s,
    small_r,
    zx_s,
    zx_r,
    zt_s,
    zt_r,
    rq_s,
    rq_r,
    zk_s,
    zk_r,
    rs_s,
    rs_r,
    ag_s,
    ag_r,
    zr_s,
    zr_r,
):
    hid = lax.axis_index("hid")
    ffn = lax.axis_index("ffn")
    x, y = hid // SIDE, hid % SIDE
    z, core = ffn // 2, ffn % 2

    def mod4(v):
        return (v + SIDE) % SIDE

    def mod8(v):
        return (v + RING) % RING

    ids_x = {d: mod4(x + d) * SIDE + y for d in (1, 2, 3)}
    ids_y = {d: x * SIDE + mod4(y + d) for d in (1, 2, 3)}
    ids_z = {d: mod8(z + d) * 2 + core for d in (1, -1)}

    def dev_x(d):
        return (ids_x[d % SIDE], ffn)

    def dev_y(d):
        return (ids_y[d % SIDE], ffn)

    def dev_z(d):
        return (hid, ids_z[d])

    other = z * 2 + 1 - core
    sibling = (hid, other)
    dirs = (1, -1)
    devs = ((dev_x, dev_y), (dev_y, dev_x))

    barrier = pltpu.get_barrier_semaphore()
    partners = [dev_x(d) for d in (1, 2, 3)] + [dev_y(d) for d in (1, 2, 3)]
    partners += [(ids_y[d], other) for d in (1, 2, 3)]
    partners += [dev_z(1), dev_z(-1), sibling]
    for dev in partners:
        pl.semaphore_signal(barrier, inc=1, device_id=dev, device_id_type=pl.DeviceIdType.MESH)

    def remote(src, dst, ssem, rsem, dev):
        return pltpu.make_async_remote_copy(
            src_ref=src,
            dst_ref=dst,
            send_sem=ssem,
            recv_sem=rsem,
            device_id=dev,
            device_id_type=pl.DeviceIdType.MESH,
        )

    def w_copy(s, o):
        if s == 0:
            src = w_query.at[:, pl.ds(o * WIDE, WIDE)]
        else:
            src = (w_gate, w_up)[o].at[:, pl.ds((s - 1) * WIDE, WIDE)]
        return pltpu.make_async_copy(src, w_in.at[s, :, pl.ds(o * WIDE, WIDE)], w_sem.at[s, o])

    def wb_copy(u):
        if u < 2:
            src = w_out.at[pl.ds(u * WIDE, WIDE)]
        else:
            src = w_down.at[pl.ds((u - 2) * WIDE, WIDE)]
        return pltpu.make_async_copy(src, w_back.at[u], wb_sem.at[u])

    def turn_copies(i):
        copies = [
            pltpu.make_async_copy(
                table.at[i, pl.ds(pl.multiple_of(ffn * ROWS, ROWS), ROWS)],
                turn.at[1, i],
                m_sem.at[1 + 5 * i],
            )
        ]
        for g in range(QUARTERS):
            first = pl.multiple_of(g * (TOKENS // QUARTERS) + hid * QUARTER, QUARTER)
            copies.append(
                pltpu.make_async_copy(
                    table.at[i, pl.ds(first, QUARTER)],
                    turn.at[0, i, pl.ds(g * QUARTER, QUARTER)],
                    m_sem.at[2 + 5 * i + g],
                )
            )
        return copies

    kv_copy = pltpu.make_async_copy(w_pairs, w_kv, m_sem.at[0])

    pl.semaphore_wait(barrier, len(partners))

    def stat_copy(a, d):
        return remote(
            stat.at[a], stat_in.at[a, d - 1], small_s.at[a, d - 1], small_r.at[a, d - 1],
            (dev_x, dev_y)[a](d),
        )

    def other_copy(d):
        return remote(
            stat.at[1], stat_other.at[d], small_s.at[5 + d // 3, d % 3], small_r.at[5 + d // 3, d % 3],
            (ids_y[d], other) if d else sibling,
        )

    def pair_copy(k, d):
        if k == 0:
            src, dst, dev = pair_part.at[mod4(x + d)], pair_in.at[0, d - 1], dev_x(d)
        elif k == 1:
            src, dst, dev = pair_sum, pair_in.at[1, d - 1], dev_y(d)
        else:
            src, dst, dev = pair_all.at[x], pair_all.at[x], dev_x(d)
        return remote(src, dst, small_s.at[2 + k, d - 1], small_r.at[2 + k, d - 1], dev)

    def each(fn, k, what):
        for d in (1, 2, 3):
            getattr(fn(k, d), what)()

    def z_copy(buf, sems, j, i):
        d = dirs[i]
        block = mod8(z - (j - 1) * d) * 2 + core
        ref = buf.at[block] if j < 4 else buf.at[block, pl.ds(i * HALF, HALF)]
        return remote(ref, ref, sems[0].at[j - 1, i], sems[1].at[j - 1, i], dev_z(d))

    def sib_copy(buf, sems, off):
        ref = buf.at[mod8(z + off) * 2 + core]
        row = 4 + (off + 3) // 2
        col = (off + 3) % 2
        return remote(ref, ref, sems[0].at[row, col], sems[1].at[row, col], sibling)

    def z_start(buf, sems):
        for i in range(2):
            z_copy(buf, sems, 1, i).start()
        sib_copy(buf, sems, 0).start()

    def z_step(buf, sems, j):
        if j < 4:
            for i in range(2):
                z_copy(buf, sems, j, i).wait()
                z_copy(buf, sems, j + 1, i).start()
                sib_copy(buf, sems, -j * dirs[i]).start()
        else:
            for i in range(2):
                z_copy(buf, sems, j, i).wait()
            sib_copy(buf, sems, 4).start()

    def sib_wait(buf, sems, *offs):
        for off in offs:
            sib_copy(buf, sems, off).wait()

    def stat_z(j, i):
        ref = stat_all.at[mod8(z - (j - 1) * dirs[i])]
        return remote(ref, ref, zt_s.at[j, i], zt_r.at[j, i], dev_z(dirs[i]))

    def stat_step(j):
        for i in range(2):
            if (j, i) == (4, 1):
                continue
            stat_z(j, i).wait()
            if j < 3 + (i == 0):
                stat_z(j + 1, i).start()

    def quarter_copy(s, j, g, o, i):
        at = o * 2 + i
        return remote(
            part.at[s, o, g, pl.ds((6, 10)[i], 4)],
            land1.at[s, o, i, g],
            rq_s.at[s * QUARTERS + j, at],
            rq_r.at[s * QUARTERS + j, at],
            devs[o][0](dirs[i]),
        )

    both = [(o, i) for o in range(2) for i in range(2)]
    rel_x = [mod4(k - x) for k in range(SIDE)]
    rel_y = [mod4(k - y) for k in range(SIDE)]
    places = (
        [rel_x[h // SIDE] * SIDE + rel_y[h % SIDE] for h in range(GROUP)],
        [rel_y[h % SIDE] * SIDE + rel_x[h // SIDE] for h in range(GROUP)],
    )

    def products(s, g):
        rows = rows_all[pl.ds(g * QUARTERS, QUARTERS)].reshape(QUARTERS * ROWS, FEATS)
        res = jnp.dot(rows, w_in[s], preferred_element_type=F32).astype(BF16)
        for h in range(GROUP):
            block = res[h * QUARTER : (h + 1) * QUARTER]
            for o in range(2):
                part[s, o, g, places[o][h]] = block[:, o * WIDE : (o + 1) * WIDE]

    eye = lax.broadcasted_iota(jnp.int32, (ROWS, 128), 0) == lax.broadcasted_iota(
        jnp.int32, (ROWS, 128), 1
    )
    line = lax.broadcasted_iota(jnp.int32, (8, 128), 0)

    def to_row(column):
        return jnp.sum(jnp.where(eye, column, 0.0), 0, keepdims=True)

    def to_column(row):
        return jnp.sum(jnp.where(eye, row, 0.0), 1, keepdims=True)

    def norm(rows, tile):
        mean, scale = to_column(tile[0:1]), to_column(tile[1:2])
        return ((rows.astype(F32) - mean) * scale * gain[...].reshape(1, FEATS)).astype(BF16)

    zx = (zx_s, zx_r)
    zk = (zk_s, zk_r)
    raw_all[ffn] = act[...]
    z_start(raw_all, zx)
    values = act[...].astype(F32)
    mean = jnp.mean(values, 1, keepdims=True)
    square = jnp.sum((values - mean) ** 2, 1, keepdims=True)
    mean, square = to_row(mean), to_row(square)
    def merge(count, tiles):
        means = [tile[0:1] for tile in tiles]
        squares = [tile[1:2] for tile in tiles]
        mean = (means[0] + means[1] + means[2] + means[3]) * 0.25
        square = squares[0] + squares[1] + squares[2] + squares[3]
        for one in means:
            square += count * (one - mean) ** 2
        return mean, square

    def finish(tiles):
        mean, square = merge(FEATS * SIDE, tiles)
        return jnp.where(line == 0, mean, lax.rsqrt(square * (1.0 / D) + EPSILON))

    stat[0] = jnp.where(line == 0, mean, square)
    each(stat_copy, 0, "start")
    kv_copy.start()
    for s in range(EARLY):
        for o in range(2):
            w_copy(s, o).start()
    total[...] = jnp.zeros_like(total)
    each(stat_copy, 0, "wait")
    mean, square = merge(FEATS, [stat[0]] + [stat_in[0, d] for d in range(3)])
    stat[1] = jnp.where(line == 0, mean, square)
    each(stat_copy, 1, "start")
    for d in range(SIDE):
        other_copy(d).start()
    z_step(raw_all, zx, 1)
    each(stat_copy, 1, "wait")
    for d in range(SIDE):
        other_copy(d).wait()
    stat_all[z, core] = finish([stat[1]] + [stat_in[1, d] for d in range(3)])
    stat_all[z, 1 - core] = finish([stat_other[d] for d in range(SIDE)])
    for i in range(2):
        stat_z(1, i).start()
    normed = norm(act[...], stat_all[z, core])
    kv_copy.wait()
    pairs = jnp.dot(normed, w_kv[...], preferred_element_type=F32).astype(BF16)
    for q in range(4):
        pair_part[q] = pairs[:, q * 128 : (q + 1) * 128]
    each(pair_copy, 0, "start")
    for s in range(EARLY):
        for o in range(2):
            w_copy(s, o).wait()

    pair = z // 2
    turned = 1 - 2 * (z % 2)
    order = (pair, mod4(pair - turned), mod4(pair + turned), mod4(pair + 2))

    def first_rows(j):
        g = order[j]

        def one(k, carry):
            rows_all[g * 4 + k] = norm(raw_all[g * 4 + k], stat_all[g * 2 + k // 2, k % 2])
            return carry

        lax.fori_loop(0, QUARTERS, one, 0)

    def first_products(j, steps):
        g = order[j]
        for s in steps:
            products(s, g)
            for o, i in both:
                quarter_copy(s, j, g, o, i).start()

    stat_step(1)
    sib_wait(raw_all, zx, 0, 1, -1)
    first_rows(0)
    first_products(0, (0,))
    z_step(raw_all, zx, 2)
    first_products(0, range(1, EARLY))
    for s in range(EARLY, STEPS):
        for o in range(2):
            w_copy(s, o).start()
    each(pair_copy, 0, "wait")
    pair_sum[...] = (
        pair_part[x].astype(F32)
        + pair_in[0, 0].astype(F32)
        + pair_in[0, 1].astype(F32)
        + pair_in[0, 2].astype(F32)
    ).astype(BF16)
    each(pair_copy, 1, "start")
    z_step(raw_all, zx, 3)
    stat_step(2)
    sib_wait(raw_all, zx, 2, -2)
    first_rows(1)
    first_products(1, range(EARLY))
    for i in range(2):
        for copy in turn_copies(i):
            copy.start()
    for u in range(UNITS):
        wb_copy(u).start()
    each(pair_copy, 1, "wait")
    pair_all[x] = (
        pair_sum[...].astype(F32)
        + pair_in[1, 0].astype(F32)
        + pair_in[1, 1].astype(F32)
        + pair_in[1, 2].astype(F32)
    ).astype(BF16)
    each(pair_copy, 2, "start")
    z_step(raw_all, zx, 4)
    stat_step(3)
    sib_wait(raw_all, zx, 3, -3)
    first_rows(2)
    first_products(2, range(EARLY))
    stat_step(4)
    sib_wait(raw_all, zx, 4)
    first_rows(3)
    first_products(3, range(EARLY))
    each(pair_copy, 2, "wait")
    for i in range(2):
        for copy in turn_copies(i):
            copy.wait()
    first, second = pair_all[0].astype(F32), pair_all[1].astype(F32)
    kv_all[ffn, :, 0:128] = (first * turn[1, 0] - second * turn[1, 1]).astype(BF16)
    kv_all[ffn, :, 128:256] = (first * turn[1, 1] + second * turn[1, 0]).astype(BF16)
    kv_all[ffn, :, 256:384] = pair_all[2]
    kv_all[ffn, :, 384:512] = pair_all[3]
    z_start(kv_all, zk)

    for s in range(EARLY, STEPS):
        for o in range(2):
            w_copy(s, o).wait()
    for u in range(UNITS):
        wb_copy(u).wait()

    far1 = ((6, 4), (10, 4))
    near1 = ((4, 2), (14, 2))
    far2 = ((3, 2), (5, 2))
    near2 = ((2, 1), (7, 1))

    def rs_copy(s, o, k, i):
        first, size = (far1, near1, far2, near2)[k][i]
        at = o * 8 + k * 2 + i
        if k < 2:
            src = part.at[s, o, :, pl.ds(first, size)]
        else:
            src = half_sum.at[s, o, pl.ds(first, size)]
        return remote(
            src,
            (land1, last1, land2, last2)[k].at[s, o, i],
            rs_s.at[s, at],
            rs_r.at[s, at],
            devs[o][k // 2](dirs[i]),
        )

    def phase0(s):
        def tile(g, carry):
            products(s, g)
            return carry

        lax.fori_loop(0, QUARTERS, tile, 0)
        for o, i in both:
            rs_copy(s, o, 0, i).start()

    def added(first, *rest):
        res = first.astype(F32)
        for one in rest:
            res += one.astype(F32)
        return res

    def phase1(s):
        @pl.when(s < EARLY)
        def _():
            for j in range(QUARTERS):
                for o, i in both:
                    quarter_copy(s, j, order[j], o, i).wait()

        @pl.when(s >= EARLY)
        def _():
            for o, i in both:
                rs_copy(s, o, 0, i).wait()

        for o, i in both:
            first, size = near1[i]
            part[s, o, :, first : first + size] = added(
                part[s, o, :, first : first + size], land1[s, o, i, :, 2 - 2 * i : 4 - 2 * i]
            ).astype(BF16)
            rs_copy(s, o, 1, i).start()

    def phase2(s):
        for o in range(2):
            for i in range(2):
                rs_copy(s, o, 1, i).wait()
            for i in range(2):
                cut = slice(2 - 2 * i, 4 - 2 * i)
                res = added(
                    part[s, o, :, 2 * i : 2 * i + 2],
                    last1[s, o, i],
                    land1[s, o, 1 - i, :, cut],
                ).astype(BF16)
                for b in range(2):
                    for r in range(2):
                        half_sum[s, o, (2 * i + b) * 2 + r] = res[2 * r : 2 * r + 2, b].reshape(
                            HALF, WIDE
                        )
            for i in range(2):
                rs_copy(s, o, 2, i).start()

    def phase3(s):
        for o, i in both:
            rs_copy(s, o, 2, i).wait()
            first = near2[i][0]
            half_sum[s, o, first] = added(half_sum[s, o, first], land2[s, o, i, 1 - i]).astype(BF16)
            rs_copy(s, o, 3, i).start()

    def attend(left, right):
        seg_row = seg[...].astype(F32)
        key_at = lax.broadcasted_iota(jnp.int32, (ROWS, TOKENS), 1)
        row_at = lax.broadcasted_iota(jnp.int32, (ROWS, TOKENS), 0)
        row_at = row_at + (TOKENS // QUARTERS - QUARTER) * (row_at // QUARTER) + hid * QUARTER
        own = jnp.sum(jnp.where(key_at == row_at, seg_row, 0.0), 1, keepdims=True)
        allowed = (key_at <= row_at) & (seg_row == own)
        keys = kv_all[:, :, 0:HEAD].reshape(TOKENS, HEAD)
        vals = kv_all[:, :, HEAD : 2 * HEAD].reshape(TOKENS, HEAD)
        cosine, sine = turn[0, 0] * HEAD**-0.5, turn[0, 1] * HEAD**-0.5
        groups = [v[:, k * 128 : (k + 1) * 128] for v in (left, right) for k in range(3)]
        query = []
        for h in range(3):
            a, b = groups[2 * h], groups[2 * h + 1]
            query.append(jnp.concatenate([a * cosine - b * sine, a * sine + b * cosine], 1))
        scores = lax.dot_general(
            jnp.concatenate(query, 0).astype(BF16),
            keys,
            (((1,), (1,)), ((), ())),
            preferred_element_type=F32,
        )
        probs = []
        for h in range(3):
            expos = jnp.where(allowed, jnp.exp(scores[h * ROWS : (h + 1) * ROWS]), 0.0)
            probs.append((expos / jnp.sum(expos, 1, keepdims=True)).astype(BF16))
        res = jnp.dot(jnp.concatenate(probs, 0), vals, preferred_element_type=F32).astype(BF16)
        pieces = [
            res[h * ROWS : (h + 1) * ROWS, k * 128 : (k + 1) * 128]
            for h in range(3)
            for k in range(2)
        ]
        return jnp.concatenate(pieces[:3], 1), jnp.concatenate(pieces[3:], 1)

    def put(u, block):
        mixed[u, 0, 0, 0] = block[0:HALF]
        mixed[u, 1, 0, 0] = block[HALF:ROWS]

    def gather_copy(u, o, k, i):
        d = dirs[i]
        away, near = (3, 1)[i], (3, 1)[i]
        dev = devs[o][k // 2](d)
        if k == 0:
            src, dst = mixed.at[u, o, 0, 0], mixed.at[u, o, 0, away]
        elif k == 1:
            rows = pl.ds(i * QUARTER, QUARTER)
            src, dst = mixed.at[u, o, 0, near, rows], mixed.at[u, o, 0, 2, rows]
        elif k == 2:
            src, dst = mixed.at[u, o, 0], mixed.at[u, o, away]
        else:
            cut = pl.ds(2 * i, 2)
            src, dst = mixed.at[u, o, near, cut], mixed.at[u, o, 2, cut]
        at = o * 8 + k * 2 + i
        return remote(src, dst, ag_s.at[u, at], ag_r.at[u, at], dev)

    def phase4(s):
        sums = []
        for o in range(2):
            for i in range(2):
                rs_copy(s, o, 3, i).wait()
            sums.append(
                jnp.concatenate(
                    [
                        half_sum[s, o, i].astype(F32)
                        + last2[s, o, i, 0].astype(F32)
                        + land2[s, o, 1 - i, 1 - i].astype(F32)
                        for i in range(2)
                    ],
                    0,
                )
            )

        @pl.when(s == 0)
        def _():
            left, right = attend(*sums)
            put(0, left)
            put(1, right)
            for u in range(2):
                for o, i in both:
                    gather_copy(u, o, 0, i).start()

        @pl.when(s > 0)
        def _():
            gate, up = sums
            put(s + 1, (gate / (1.0 + jnp.exp(-gate)) * up).astype(BF16))
            for o, i in both:
                gather_copy(s + 1, o, 0, i).start()

    def phase5(u):
        for o, i in both:
            gather_copy(u, o, 0, i).wait()
            gather_copy(u, o, 1, i).start()

    def phase6(u):
        for o in range(2):
            for i in range(2):
                gather_copy(u, o, 1, i).wait()
            for i in range(2):
                gather_copy(u, o, 2, i).start()

    def phase7(u):
        for o, i in both:
            gather_copy(u, o, 2, i).wait()
            gather_copy(u, o, 3, i).start()

    def phase8(u):
        for o in range(2):
            for i in range(2):
                gather_copy(u, o, 3, i).wait()
            for p in range(2):
                rows = mixed[u, o, 2 * p : 2 * p + 2].reshape(2 * SIDE * HALF, WIDE)
                total[o, p * 256 : (p + 1) * 256] += jnp.dot(
                    rows, w_back[u], preferred_element_type=F32
                )

    def slot(t, carry):
        pl.when((t >= EARLY) & (t < STEPS))(lambda: phase0(t))
        for k, fn in ((1, phase1), (3, phase2), (4, phase3)):
            s = t - k
            pl.when((s >= 0) & (s < STEPS))(lambda fn=fn, s=s: fn(s))

        for j in range(1, 5):

            @pl.when(t == j)
            def _(j=j):
                z_step(kv_all, zk, j)
                if j == 4:
                    sib_wait(kv_all, zk, 0, 1, -1, 2, -2, 3, -3, 4)

        s4 = t - 5
        pl.when((s4 >= 0) & (s4 < STEPS))(lambda: phase4(s4))

        for k, fn in ((6, phase5), (7, phase6), (8, phase7), (9, phase8)):
            s = t - k

            @pl.when((s >= 0) & (s < STEPS))
            def _(fn=fn, s=s):
                def unit(u, c):
                    fn(u)
                    return c

                lax.fori_loop(jnp.where(s == 0, 0, s + 1), s + 2, unit, 0)

        return carry

    lax.fori_loop(1, STEPS + 9, slot, 0)

    offsets = (4, 3, -3, 2, -2, 1, -1, 0)

    def half_rows(block, h):
        g = block // SIDE
        o = g // 2
        px = mod4(block % SIDE - x)
        pieces = []
        for k in (2 * h, 2 * h + 1):
            place = jnp.where(o == 0, rel_y[k] * SIDE + px, px * SIDE + rel_y[k])
            first = pl.multiple_of(place * HALF + (g % 2) * QUARTER, QUARTER)
            pieces.append(total[o, pl.ds(first, QUARTER)])
        return jnp.concatenate(pieces, 0)

    def sib_sum(k):
        at = mod8(z + offsets[k])
        return remote(sib_out.at[at], sib_in.at[at], zr_s.at[k], zr_r.at[k], sibling)

    def sib_send(*which):
        for k in which:
            at = mod8(z + offsets[k])
            for h in range(2):
                sib_out[at, h * HALF : (h + 1) * HALF] = half_rows(at * 2 + 1 - core, h).astype(BF16)
            sib_sum(k).start()

    sib_send(0, 1, 2)

    def chip_sum(k, h):
        at = mod8(z + offsets[k])
        return half_rows(at * 2 + core, h) + sib_in[at, h * HALF : (h + 1) * HALF].astype(F32)

    def ring_copy(j, i, h):
        at = 8 + j * 4 + i * 2 + h
        return remote(
            ring_out.at[j, i, h], ring_in.at[j, i, h], zr_s.at[at], zr_r.at[at], dev_z(dirs[i])
        )

    sib_sum(0).wait()
    for i in range(2):
        ring_out[0, i, i] = chip_sum(0, i).astype(BF16)
        ring_copy(0, i, i).start()
    sib_send(3, 4)
    for j in (1, 2, 3):
        for i in range(2):
            sib_sum(2 * j - 1 + i).wait()
        for turn_of in range(2):
            for i in range(2):
                h = (1 - i, i)[turn_of]
                here = chip_sum(2 * j - 1 + i, h)
                if j > 1 or h == i:
                    ring_copy(j - 1, i, h).wait()
                    here += ring_in[j - 1, i, h].astype(F32)
                ring_out[j, i, h] = here.astype(BF16)
                ring_copy(j, i, h).start()
        if j < 3:
            sib_send(*((5, 6), (7,))[j - 1])
    sib_sum(7).wait()
    for h in range(2):
        here = chip_sum(7, h) + act[h * HALF : (h + 1) * HALF].astype(F32)
        for i in range(2):
            ring_copy(3, i, h).wait()
            here += ring_in[3, i, h].astype(F32)
        out[h * HALF : (h + 1) * HALF] = here.astype(BF16)


def per_device(activations, ln_gain, segments, w_query, w_key_value, w_gate, w_up, w_out, w_down):
    vmem = pl.BlockSpec(memory_space=pltpu.VMEM)
    anywhere = pl.BlockSpec(memory_space=pl.ANY)
    dma = pltpu.SemaphoreType.DMA
    scratch = [
        pltpu.VMEM((STEPS, FEATS, 2 * WIDE), BF16),
        pltpu.VMEM((UNITS, WIDE, FEATS), BF16),
        pltpu.VMEM((FEATS, 512), BF16),
        pltpu.VMEM((2, 2, ROWS, 128), F32),
        pltpu.VMEM((2, 8, 128), F32),
        pltpu.VMEM((2, 3, 8, 128), F32),
        pltpu.VMEM((4, 8, 128), F32),
        pltpu.VMEM((RING, 2, 8, 128), F32),
        pltpu.VMEM((GROUP, ROWS, FEATS), BF16),
        pltpu.VMEM((GROUP, ROWS, FEATS), BF16),
        pltpu.VMEM((4, ROWS, 128), BF16),
        pltpu.VMEM((2, 3, ROWS, 128), BF16),
        pltpu.VMEM((ROWS, 128), BF16),
        pltpu.VMEM((4, ROWS, 128), BF16),
        pltpu.VMEM((GROUP, ROWS, 512), BF16),
        pltpu.VMEM((STEPS, 2, QUARTERS, GROUP, QUARTER, WIDE), BF16),
        pltpu.VMEM((STEPS, 2, 2, QUARTERS, 4, QUARTER, WIDE), BF16),
        pltpu.VMEM((STEPS, 2, 2, QUARTERS, 2, QUARTER, WIDE), BF16),
        pltpu.VMEM((STEPS, 2, 2 * SIDE, HALF, WIDE), BF16),
        pltpu.VMEM((STEPS, 2, 2, 2, HALF, WIDE), BF16),
        pltpu.VMEM((STEPS, 2, 2, 1, HALF, WIDE), BF16),
        pltpu.VMEM((UNITS, 2, SIDE, SIDE, HALF, WIDE), BF16),
        pltpu.VMEM((2, GROUP * HALF, FEATS), F32),
        pltpu.VMEM((RING, ROWS, FEATS), BF16),
        pltpu.VMEM((RING, ROWS, FEATS), BF16),
        pltpu.VMEM((4, 2, 2, HALF, FEATS), BF16),
        pltpu.VMEM((4, 2, 2, HALF, FEATS), BF16),
        dma((STEPS, 2)),
        dma((UNITS,)),
        dma((11,)),
        dma((7, 3)),
        dma((7, 3)),
        dma((8, 2)),
        dma((8, 2)),
        dma((5, 2)),
        dma((5, 2)),
        dma((EARLY * QUARTERS, 4)),
        dma((EARLY * QUARTERS, 4)),
        dma((8, 2)),
        dma((8, 2)),
        dma((STEPS, 16)),
        dma((STEPS, 16)),
        dma((UNITS, 16)),
        dma((UNITS, 16)),
        dma((24,)),
        dma((24,)),
    ]
    return pl.pallas_call(
        block_kernel,
        out_shape=jax.ShapeDtypeStruct((ROWS, FEATS), BF16),
        in_specs=[vmem, vmem, vmem] + [anywhere] * 7,
        out_specs=vmem,
        scratch_shapes=scratch,
        compiler_params=pltpu.CompilerParams(
            collective_id=0, has_side_effects=True, vmem_limit_bytes=60 * 1024 * 1024
        ),
    )(
        activations,
        ln_gain,
        segments.reshape(1, TOKENS),
        jnp.asarray(tables()),
        w_query,
        w_key_value,
        w_gate,
        w_up,
        w_out,
        w_down,
    )


def solution(mesh):
    placed = (
        P("ffn", "hid"),
        P("hid"),
        P(),
        P("hid", "ffn"),
        P("hid", None),
        P("hid", "ffn"),
        P("hid", "ffn"),
        P("ffn", "hid"),
        P("ffn", "hid"),
    )
    return jax.shard_map(
        per_device, mesh=mesh, in_specs=placed, out_specs=P("ffn", "hid"), check_vma=False
    )
```

```python
import jax
import jax.numpy as jnp
import numpy as np
from jax import lax
from jax.experimental import pallas as pl
from jax.experimental.pallas import tpu as pltpu
from jax.sharding import PartitionSpec as P

D = 10240
HEAD = 256
TOKENS = 1024
EPSILON = 1e-06

SIDE = 4
RING = 8
GROUP = SIDE * SIDE
ROWS = TOKENS // GROUP
FEATS = D // GROUP
WIDE = 384
STEPS = 7
EARLY = 3
UNITS = 8
HALF = ROWS // 2
QUARTERS = 4
QUARTER = ROWS // 4
F32 = jnp.float32
BF16 = jnp.bfloat16


def tables():
    half = HEAD // 2
    frequency = np.float32(10000.0) ** (-np.arange(half, dtype=np.float32) / np.float32(half))
    angles = np.arange(TOKENS, dtype=np.float32)[:, None] * frequency[None, :].astype(np.float32)
    wide = angles.astype(np.float64)
    return np.stack([np.cos(wide), np.sin(wide)]).astype(np.float32)


def block_kernel(
    act,
    gain,
    seg,
    table,
    w_query,
    w_pairs,
    w_gate,
    w_up,
    w_out,
    w_down,
    out,
    w_in,
    w_back,
    w_kv,
    turn,
    stat,
    stat_in,
    stat_other,
    stat_all,
    raw_all,
    rows_all,
    pair_part,
    pair_in,
    pair_sum,
    pair_all,
    kv_all,
    part,
    land1,
    last1,
    half_sum,
    land2,
    last2,
    mixed,
    total,
    sib_out,
    sib_in,
    ring_out,
    ring_in,
    w_sem,
    wb_sem,
    m_sem,
    small_s,
    small_r,
    zx_s,
    zx_r,
    zt_s,
    zt_r,
    rq_s,
    rq_r,
    zk_s,
    zk_r,
    rs_s,
    rs_r,
    ag_s,
    ag_r,
    zr_s,
    zr_r,
):
    hid = lax.axis_index("hid")
    ffn = lax.axis_index("ffn")
    x, y = hid // SIDE, hid % SIDE
    z, core = ffn // 2, ffn % 2

    def mod4(v):
        return (v + SIDE) % SIDE

    def mod8(v):
        return (v + RING) % RING

    ids_x = {d: mod4(x + d) * SIDE + y for d in (1, 2, 3)}
    ids_y = {d: x * SIDE + mod4(y + d) for d in (1, 2, 3)}
    ids_z = {d: mod8(z + d) * 2 + core for d in (1, -1)}

    def dev_x(d):
        return (ids_x[d % SIDE], ffn)

    def dev_y(d):
        return (ids_y[d % SIDE], ffn)

    def dev_z(d):
        return (hid, ids_z[d])

    other = z * 2 + 1 - core
    sibling = (hid, other)
    dirs = (1, -1)
    devs = ((dev_x, dev_y), (dev_y, dev_x))

    barrier = pltpu.get_barrier_semaphore()
    partners = [dev_x(d) for d in (1, 2, 3)] + [dev_y(d) for d in (1, 2, 3)]
    partners += [(ids_y[d], other) for d in (1, 2, 3)]
    partners += [dev_z(1), dev_z(-1), sibling]
    for dev in partners:
        pl.semaphore_signal(barrier, inc=1, device_id=dev, device_id_type=pl.DeviceIdType.MESH)

    def remote(src, dst, ssem, rsem, dev):
        return pltpu.make_async_remote_copy(
            src_ref=src,
            dst_ref=dst,
            send_sem=ssem,
            recv_sem=rsem,
            device_id=dev,
            device_id_type=pl.DeviceIdType.MESH,
        )

    def w_copy(s, o):
        if s == 0:
            src = w_query.at[:, pl.ds(o * WIDE, WIDE)]
        else:
            src = (w_gate, w_up)[o].at[:, pl.ds((s - 1) * WIDE, WIDE)]
        return pltpu.make_async_copy(src, w_in.at[s, :, pl.ds(o * WIDE, WIDE)], w_sem.at[s, o])

    def wb_copy(u):
        if u < 2:
            src = w_out.at[pl.ds(u * WIDE, WIDE)]
        else:
            src = w_down.at[pl.ds((u - 2) * WIDE, WIDE)]
        return pltpu.make_async_copy(src, w_back.at[u], wb_sem.at[u])

    def turn_copies(i):
        copies = [
            pltpu.make_async_copy(
                table.at[i, pl.ds(pl.multiple_of(ffn * ROWS, ROWS), ROWS)],
                turn.at[1, i],
                m_sem.at[1 + 5 * i],
            )
        ]
        for g in range(QUARTERS):
            first = pl.multiple_of(g * (TOKENS // QUARTERS) + hid * QUARTER, QUARTER)
            copies.append(
                pltpu.make_async_copy(
                    table.at[i, pl.ds(first, QUARTER)],
                    turn.at[0, i, pl.ds(g * QUARTER, QUARTER)],
                    m_sem.at[2 + 5 * i + g],
                )
            )
        return copies

    kv_copy = pltpu.make_async_copy(w_pairs, w_kv, m_sem.at[0])

    pl.semaphore_wait(barrier, len(partners))

    def stat_copy(a, d):
        return remote(
            stat.at[a], stat_in.at[a, d - 1], small_s.at[a, d - 1], small_r.at[a, d - 1],
            (dev_x, dev_y)[a](d),
        )

    def other_copy(d):
        return remote(
            stat.at[1], stat_other.at[d], small_s.at[5 + d // 3, d % 3], small_r.at[5 + d // 3, d % 3],
            (ids_y[d], other) if d else sibling,
        )

    def pair_copy(k, d):
        if k == 0:
            src, dst, dev = pair_part.at[mod4(x + d)], pair_in.at[0, d - 1], dev_x(d)
        elif k == 1:
            src, dst, dev = pair_sum, pair_in.at[1, d - 1], dev_y(d)
        else:
            src, dst, dev = pair_all.at[x], pair_all.at[x], dev_x(d)
        return remote(src, dst, small_s.at[2 + k, d - 1], small_r.at[2 + k, d - 1], dev)

    def each(fn, k, what):
        for d in (1, 2, 3):
            getattr(fn(k, d), what)()

    def z_copy(buf, sems, j, i):
        d = dirs[i]
        block = mod8(z - (j - 1) * d) * 2 + core
        ref = buf.at[block] if j < 4 else buf.at[block, pl.ds(i * HALF, HALF)]
        return remote(ref, ref, sems[0].at[j - 1, i], sems[1].at[j - 1, i], dev_z(d))

    def sib_copy(buf, sems, off):
        ref = buf.at[mod8(z + off) * 2 + core]
        row = 4 + (off + 3) // 2
        col = (off + 3) % 2
        return remote(ref, ref, sems[0].at[row, col], sems[1].at[row, col], sibling)

    def z_start(buf, sems):
        for i in range(2):
            z_copy(buf, sems, 1, i).start()
        sib_copy(buf, sems, 0).start()

    def z_step(buf, sems, j):
        if j < 4:
            for i in range(2):
                z_copy(buf, sems, j, i).wait()
                z_copy(buf, sems, j + 1, i).start()
                sib_copy(buf, sems, -j * dirs[i]).start()
        else:
            for i in range(2):
                z_copy(buf, sems, j, i).wait()
            sib_copy(buf, sems, 4).start()

    def sib_wait(buf, sems, *offs):
        for off in offs:
            sib_copy(buf, sems, off).wait()

    def stat_z(j, i):
        ref = stat_all.at[mod8(z - (j - 1) * dirs[i])]
        return remote(ref, ref, zt_s.at[j, i], zt_r.at[j, i], dev_z(dirs[i]))

    def stat_step(j):
        for i in range(2):
            if (j, i) == (4, 1):
                continue
            stat_z(j, i).wait()
            if j < 3 + (i == 0):
                stat_z(j + 1, i).start()

    def quarter_copy(s, j, g, o, i):
        at = o * 2 + i
        return remote(
            part.at[s, o, g, pl.ds((6, 10)[i], 4)],
            land1.at[s, o, i, g],
            rq_s.at[s * QUARTERS + j, at],
            rq_r.at[s * QUARTERS + j, at],
            devs[o][0](dirs[i]),
        )

    both = [(o, i) for o in range(2) for i in range(2)]
    rel_x = [mod4(k - x) for k in range(SIDE)]
    rel_y = [mod4(k - y) for k in range(SIDE)]
    places = (
        [rel_x[h // SIDE] * SIDE + rel_y[h % SIDE] for h in range(GROUP)],
        [rel_y[h % SIDE] * SIDE + rel_x[h // SIDE] for h in range(GROUP)],
    )

    def products(s, g):
        rows = rows_all[pl.ds(g * QUARTERS, QUARTERS)].reshape(QUARTERS * ROWS, FEATS)
        res = jnp.dot(rows, w_in[s], preferred_element_type=F32).astype(BF16)
        for h in range(GROUP):
            block = res[h * QUARTER : (h + 1) * QUARTER]
            for o in range(2):
                part[s, o, g, places[o][h]] = block[:, o * WIDE : (o + 1) * WIDE]

    eye = lax.broadcasted_iota(jnp.int32, (ROWS, 128), 0) == lax.broadcasted_iota(
        jnp.int32, (ROWS, 128), 1
    )
    line = lax.broadcasted_iota(jnp.int32, (8, 128), 0)

    def to_row(column):
        return jnp.sum(jnp.where(eye, column, 0.0), 0, keepdims=True)

    def to_column(row):
        return jnp.sum(jnp.where(eye, row, 0.0), 1, keepdims=True)

    def norm(rows, tile):
        mean, scale = to_column(tile[0:1]), to_column(tile[1:2])
        return ((rows.astype(F32) - mean) * scale * gain[...].reshape(1, FEATS)).astype(BF16)

    zx = (zx_s, zx_r)
    zk = (zk_s, zk_r)
    raw_all[ffn] = act[...]
    z_start(raw_all, zx)
    values = act[...].astype(F32)
    mean = jnp.mean(values, 1, keepdims=True)
    square = jnp.sum((values - mean) ** 2, 1, keepdims=True)
    mean, square = to_row(mean), to_row(square)
    def merge(count, tiles):
        means = [tile[0:1] for tile in tiles]
        squares = [tile[1:2] for tile in tiles]
        mean = (means[0] + means[1] + means[2] + means[3]) * 0.25
        square = squares[0] + squares[1] + squares[2] + squares[3]
        for one in means:
            square += count * (one - mean) ** 2
        return mean, square

    def finish(tiles):
        mean, square = merge(FEATS * SIDE, tiles)
        return jnp.where(line == 0, mean, lax.rsqrt(square * (1.0 / D) + EPSILON))

    stat[0] = jnp.where(line == 0, mean, square)
    each(stat_copy, 0, "start")
    kv_copy.start()
    for s in range(EARLY):
        for o in range(2):
            w_copy(s, o).start()
    total[...] = jnp.zeros_like(total)
    each(stat_copy, 0, "wait")
    mean, square = merge(FEATS, [stat[0]] + [stat_in[0, d] for d in range(3)])
    stat[1] = jnp.where(line == 0, mean, square)
    each(stat_copy, 1, "start")
    for d in range(SIDE):
        other_copy(d).start()
    z_step(raw_all, zx, 1)
    each(stat_copy, 1, "wait")
    for d in range(SIDE):
        other_copy(d).wait()
    stat_all[z, core] = finish([stat[1]] + [stat_in[1, d] for d in range(3)])
    stat_all[z, 1 - core] = finish([stat_other[d] for d in range(SIDE)])
    for i in range(2):
        stat_z(1, i).start()
    normed = norm(act[...], stat_all[z, core])
    kv_copy.wait()
    pairs = jnp.dot(normed, w_kv[...], preferred_element_type=F32).astype(BF16)
    for q in range(4):
        pair_part[q] = pairs[:, q * 128 : (q + 1) * 128]
    each(pair_copy, 0, "start")
    for s in range(EARLY):
        for o in range(2):
            w_copy(s, o).wait()

    pair = z // 2
    turned = 1 - 2 * (z % 2)
    order = (pair, mod4(pair - turned), mod4(pair + turned), mod4(pair + 2))

    def first_rows(j):
        g = order[j]

        def one(k, carry):
            rows_all[g * 4 + k] = norm(raw_all[g * 4 + k], stat_all[g * 2 + k // 2, k % 2])
            return carry

        lax.fori_loop(0, QUARTERS, one, 0)

    def first_products(j, steps):
        g = order[j]
        for s in steps:
            products(s, g)
            for o, i in both:
                quarter_copy(s, j, g, o, i).start()

    stat_step(1)
    sib_wait(raw_all, zx, 0, 1, -1)
    first_rows(0)
    first_products(0, (0,))
    z_step(raw_all, zx, 2)
    first_products(0, range(1, EARLY))
    for s in range(EARLY, STEPS):
        for o in range(2):
            w_copy(s, o).start()
    each(pair_copy, 0, "wait")
    pair_sum[...] = (
        pair_part[x].astype(F32)
        + pair_in[0, 0].astype(F32)
        + pair_in[0, 1].astype(F32)
        + pair_in[0, 2].astype(F32)
    ).astype(BF16)
    each(pair_copy, 1, "start")
    z_step(raw_all, zx, 3)
    stat_step(2)
    sib_wait(raw_all, zx, 2, -2)
    first_rows(1)
    first_products(1, range(EARLY))
    for i in range(2):
        for copy in turn_copies(i):
            copy.start()
    for u in range(UNITS):
        wb_copy(u).start()
    each(pair_copy, 1, "wait")
    pair_all[x] = (
        pair_sum[...].astype(F32)
        + pair_in[1, 0].astype(F32)
        + pair_in[1, 1].astype(F32)
        + pair_in[1, 2].astype(F32)
    ).astype(BF16)
    each(pair_copy, 2, "start")
    z_step(raw_all, zx, 4)
    stat_step(3)
    sib_wait(raw_all, zx, 3, -3)
    first_rows(2)
    first_products(2, range(EARLY))
    stat_step(4)
    sib_wait(raw_all, zx, 4)
    first_rows(3)
    first_products(3, range(EARLY))
    each(pair_copy, 2, "wait")
    for i in range(2):
        for copy in turn_copies(i):
            copy.wait()
    first, second = pair_all[0].astype(F32), pair_all[1].astype(F32)
    kv_all[ffn, :, 0:128] = (first * turn[1, 0] - second * turn[1, 1]).astype(BF16)
    kv_all[ffn, :, 128:256] = (first * turn[1, 1] + second * turn[1, 0]).astype(BF16)
    kv_all[ffn, :, 256:384] = pair_all[2]
    kv_all[ffn, :, 384:512] = pair_all[3]
    z_start(kv_all, zk)

    for s in range(EARLY, STEPS):
        for o in range(2):
            w_copy(s, o).wait()
    for u in range(UNITS):
        wb_copy(u).wait()

    far1 = ((6, 4), (10, 4))
    near1 = ((4, 2), (14, 2))
    far2 = ((3, 2), (5, 2))
    near2 = ((2, 1), (7, 1))

    def rs_copy(s, o, k, i):
        first, size = (far1, near1, far2, near2)[k][i]
        at = o * 8 + k * 2 + i
        if k < 2:
            src = part.at[s, o, :, pl.ds(first, size)]
        else:
            src = half_sum.at[s, o, pl.ds(first, size)]
        return remote(
            src,
            (land1, last1, land2, last2)[k].at[s, o, i],
            rs_s.at[s, at],
            rs_r.at[s, at],
            devs[o][k // 2](dirs[i]),
        )

    def phase0(s):
        def tile(g, carry):
            products(s, g)
            return carry

        lax.fori_loop(0, QUARTERS, tile, 0)
        for o, i in both:
            rs_copy(s, o, 0, i).start()

    def added(first, *rest):
        res = first.astype(F32)
        for one in rest:
            res += one.astype(F32)
        return res

    def phase1(s):
        @pl.when(s < EARLY)
        def _():
            for j in range(QUARTERS):
                for o, i in both:
                    quarter_copy(s, j, order[j], o, i).wait()

        @pl.when(s >= EARLY)
        def _():
            for o, i in both:
                rs_copy(s, o, 0, i).wait()

        for o, i in both:
            first, size = near1[i]
            part[s, o, :, first : first + size] += land1[s, o, i, :, 2 - 2 * i : 4 - 2 * i]
            rs_copy(s, o, 1, i).start()

    def phase2(s):
        for o in range(2):
            for i in range(2):
                rs_copy(s, o, 1, i).wait()
            for i in range(2):
                cut = slice(2 - 2 * i, 4 - 2 * i)
                res = added(
                    part[s, o, :, 2 * i : 2 * i + 2],
                    last1[s, o, i],
                    land1[s, o, 1 - i, :, cut],
                ).astype(BF16)
                for b in range(2):
                    for r in range(2):
                        half_sum[s, o, (2 * i + b) * 2 + r] = res[2 * r : 2 * r + 2, b].reshape(
                            HALF, WIDE
                        )
            for i in range(2):
                rs_copy(s, o, 2, i).start()

    def phase3(s):
        for o, i in both:
            rs_copy(s, o, 2, i).wait()
            first = near2[i][0]
            half_sum[s, o, first] += land2[s, o, i, 1 - i]
            rs_copy(s, o, 3, i).start()

    def attend(left, right):
        seg_row = seg[...].astype(F32)
        key_at = lax.broadcasted_iota(jnp.int32, (ROWS, TOKENS), 1)
        row_at = lax.broadcasted_iota(jnp.int32, (ROWS, TOKENS), 0)
        row_at = row_at + (TOKENS // QUARTERS - QUARTER) * (row_at // QUARTER) + hid * QUARTER
        own = jnp.sum(jnp.where(key_at == row_at, seg_row, 0.0), 1, keepdims=True)
        allowed = (key_at <= row_at) & (seg_row == own)
        keys = kv_all[:, :, 0:HEAD].reshape(TOKENS, HEAD)
        vals = kv_all[:, :, HEAD : 2 * HEAD].reshape(TOKENS, HEAD)
        cosine, sine = turn[0, 0] * HEAD**-0.5, turn[0, 1] * HEAD**-0.5
        groups = [v[:, k * 128 : (k + 1) * 128] for v in (left, right) for k in range(3)]
        query = []
        for h in range(3):
            a, b = groups[2 * h], groups[2 * h + 1]
            query.append(jnp.concatenate([a * cosine - b * sine, a * sine + b * cosine], 1))
        scores = lax.dot_general(
            jnp.concatenate(query, 0).astype(BF16),
            keys,
            (((1,), (1,)), ((), ())),
            preferred_element_type=F32,
        )
        probs = []
        for h in range(3):
            expos = jnp.where(allowed, jnp.exp(scores[h * ROWS : (h + 1) * ROWS]), 0.0)
            probs.append((expos / jnp.sum(expos, 1, keepdims=True)).astype(BF16))
        res = jnp.dot(jnp.concatenate(probs, 0), vals, preferred_element_type=F32).astype(BF16)
        pieces = [
            res[h * ROWS : (h + 1) * ROWS, k * 128 : (k + 1) * 128]
            for h in range(3)
            for k in range(2)
        ]
        return jnp.concatenate(pieces[:3], 1), jnp.concatenate(pieces[3:], 1)

    def put(u, block):
        mixed[u, 0, 0, 0] = block[0:HALF]
        mixed[u, 1, 0, 0] = block[HALF:ROWS]

    def gather_copy(u, o, k, i):
        d = dirs[i]
        away, near = (3, 1)[i], (3, 1)[i]
        dev = devs[o][k // 2](d)
        if k == 0:
            src, dst = mixed.at[u, o, 0, 0], mixed.at[u, o, 0, away]
        elif k == 1:
            rows = pl.ds(i * QUARTER, QUARTER)
            src, dst = mixed.at[u, o, 0, near, rows], mixed.at[u, o, 0, 2, rows]
        elif k == 2:
            src, dst = mixed.at[u, o, 0], mixed.at[u, o, away]
        else:
            cut = pl.ds(2 * i, 2)
            src, dst = mixed.at[u, o, near, cut], mixed.at[u, o, 2, cut]
        at = o * 8 + k * 2 + i
        return remote(src, dst, ag_s.at[u, at], ag_r.at[u, at], dev)

    def phase4(s):
        sums = []
        for o in range(2):
            for i in range(2):
                rs_copy(s, o, 3, i).wait()
            sums.append(
                jnp.concatenate(
                    [
                        half_sum[s, o, i].astype(F32)
                        + last2[s, o, i, 0].astype(F32)
                        + land2[s, o, 1 - i, 1 - i].astype(F32)
                        for i in range(2)
                    ],
                    0,
                )
            )

        @pl.when(s == 0)
        def _():
            left, right = attend(*sums)
            put(0, left)
            put(1, right)
            for u in range(2):
                for o, i in both:
                    gather_copy(u, o, 0, i).start()

        @pl.when(s > 0)
        def _():
            gate, up = sums
            put(s + 1, (gate / (1.0 + jnp.exp(-gate)) * up).astype(BF16))
            for o, i in both:
                gather_copy(s + 1, o, 0, i).start()

    def phase5(u):
        for o, i in both:
            gather_copy(u, o, 0, i).wait()
            gather_copy(u, o, 1, i).start()

    def phase6(u):
        for o in range(2):
            for i in range(2):
                gather_copy(u, o, 1, i).wait()
            for i in range(2):
                gather_copy(u, o, 2, i).start()

    def phase7(u):
        for o, i in both:
            gather_copy(u, o, 2, i).wait()
            gather_copy(u, o, 3, i).start()

    def accumulate(u, count):
        weights = w_back[pl.ds(u, count)].reshape(count * WIDE, FEATS)
        for o in range(2):
            for p in range(2):
                rows = [
                    mixed[u + k, o, 2 * p : 2 * p + 2].reshape(2 * SIDE * HALF, WIDE)
                    for k in range(count)
                ]
                total[o, p * 256 : (p + 1) * 256] += jnp.dot(
                    jnp.concatenate(rows, 1), weights, preferred_element_type=F32
                )

    def phase8(u):
        for o, i in both:
            gather_copy(u, o, 3, i).wait()
        pl.when((u % 2 == 1) & (u < 6))(lambda: accumulate(u - 1, 2))
        pl.when(u >= 6)(lambda: accumulate(u, 1))

    def slot(t, carry):
        pl.when((t >= EARLY) & (t < STEPS))(lambda: phase0(t))
        for k, fn in ((2, phase1), (4, phase2), (5, phase3)):
            s = t - k
            pl.when((s >= 0) & (s < STEPS))(lambda fn=fn, s=s: fn(s))

        for j in range(1, 5):

            @pl.when(t == j + 1)
            def _(j=j):
                z_step(kv_all, zk, j)
                if j == 4:
                    sib_wait(kv_all, zk, 0, 1, -1, 2, -2, 3, -3, 4)

        s4 = t - 6
        pl.when((s4 >= 0) & (s4 < STEPS))(lambda: phase4(s4))

        for k, fn in ((7, phase5), (8, phase6), (9, phase7), (10, phase8)):
            s = t - k

            @pl.when((s >= 0) & (s < STEPS))
            def _(fn=fn, s=s):
                def unit(u, c):
                    fn(u)
                    return c

                lax.fori_loop(jnp.where(s == 0, 0, s + 1), s + 2, unit, 0)

        return carry

    lax.fori_loop(2, STEPS + 10, slot, 0)

    offsets = (4, 3, -3, 2, -2, 1, -1, 0)

    def half_rows(block, h):
        g = block // SIDE
        o = g // 2
        px = mod4(block % SIDE - x)
        pieces = []
        for k in (2 * h, 2 * h + 1):
            place = jnp.where(o == 0, rel_y[k] * SIDE + px, px * SIDE + rel_y[k])
            first = pl.multiple_of(place * HALF + (g % 2) * QUARTER, QUARTER)
            pieces.append(total[o, pl.ds(first, QUARTER)])
        return jnp.concatenate(pieces, 0)

    def sib_sum(k):
        at = mod8(z + offsets[k])
        return remote(sib_out.at[at], sib_in.at[at], zr_s.at[k], zr_r.at[k], sibling)

    def sib_send(*which):
        for k in which:
            at = mod8(z + offsets[k])
            for h in range(2):
                sib_out[at, h * HALF : (h + 1) * HALF] = half_rows(at * 2 + 1 - core, h).astype(BF16)
            sib_sum(k).start()

    sib_send(0, 1, 2)

    def chip_sum(k, h):
        at = mod8(z + offsets[k])
        return half_rows(at * 2 + core, h) + sib_in[at, h * HALF : (h + 1) * HALF].astype(F32)

    def ring_copy(j, i, h):
        at = 8 + j * 4 + i * 2 + h
        return remote(
            ring_out.at[j, i, h], ring_in.at[j, i, h], zr_s.at[at], zr_r.at[at], dev_z(dirs[i])
        )

    sib_sum(0).wait()
    for i in range(2):
        ring_out[0, i, i] = chip_sum(0, i).astype(BF16)
        ring_copy(0, i, i).start()
    sib_send(3, 4)
    for j in (1, 2, 3):
        for i in range(2):
            sib_sum(2 * j - 1 + i).wait()
        for turn_of in range(2):
            for i in range(2):
                h = (1 - i, i)[turn_of]
                here = chip_sum(2 * j - 1 + i, h)
                if j > 1 or h == i:
                    ring_copy(j - 1, i, h).wait()
                    here += ring_in[j - 1, i, h].astype(F32)
                ring_out[j, i, h] = here.astype(BF16)
                ring_copy(j, i, h).start()
        if j < 3:
            sib_send(*((5, 6), (7,))[j - 1])
    sib_sum(7).wait()
    for h in range(2):
        here = chip_sum(7, h) + act[h * HALF : (h + 1) * HALF].astype(F32)
        for i in range(2):
            ring_copy(3, i, h).wait()
            here += ring_in[3, i, h].astype(F32)
        out[h * HALF : (h + 1) * HALF] = here.astype(BF16)


def per_device(activations, ln_gain, segments, w_query, w_key_value, w_gate, w_up, w_out, w_down):
    vmem = pl.BlockSpec(memory_space=pltpu.VMEM)
    anywhere = pl.BlockSpec(memory_space=pl.ANY)
    dma = pltpu.SemaphoreType.DMA
    scratch = [
        pltpu.VMEM((STEPS, FEATS, 2 * WIDE), BF16),
        pltpu.VMEM((UNITS, WIDE, FEATS), BF16),
        pltpu.VMEM((FEATS, 512), BF16),
        pltpu.VMEM((2, 2, ROWS, 128), F32),
        pltpu.VMEM((2, 8, 128), F32),
        pltpu.VMEM((2, 3, 8, 128), F32),
        pltpu.VMEM((4, 8, 128), F32),
        pltpu.VMEM((RING, 2, 8, 128), F32),
        pltpu.VMEM((GROUP, ROWS, FEATS), BF16),
        pltpu.VMEM((GROUP, ROWS, FEATS), BF16),
        pltpu.VMEM((4, ROWS, 128), BF16),
        pltpu.VMEM((2, 3, ROWS, 128), BF16),
        pltpu.VMEM((ROWS, 128), BF16),
        pltpu.VMEM((4, ROWS, 128), BF16),
        pltpu.VMEM((GROUP, ROWS, 512), BF16),
        pltpu.VMEM((STEPS, 2, QUARTERS, GROUP, QUARTER, WIDE), BF16),
        pltpu.VMEM((STEPS, 2, 2, QUARTERS, 4, QUARTER, WIDE), BF16),
        pltpu.VMEM((STEPS, 2, 2, QUARTERS, 2, QUARTER, WIDE), BF16),
        pltpu.VMEM((STEPS, 2, 2 * SIDE, HALF, WIDE), BF16),
        pltpu.VMEM((STEPS, 2, 2, 2, HALF, WIDE), BF16),
        pltpu.VMEM((STEPS, 2, 2, 1, HALF, WIDE), BF16),
        pltpu.VMEM((UNITS, 2, SIDE, SIDE, HALF, WIDE), BF16),
        pltpu.VMEM((2, GROUP * HALF, FEATS), F32),
        pltpu.VMEM((RING, ROWS, FEATS), BF16),
        pltpu.VMEM((RING, ROWS, FEATS), BF16),
        pltpu.VMEM((4, 2, 2, HALF, FEATS), BF16),
        pltpu.VMEM((4, 2, 2, HALF, FEATS), BF16),
        dma((STEPS, 2)),
        dma((UNITS,)),
        dma((11,)),
        dma((7, 3)),
        dma((7, 3)),
        dma((8, 2)),
        dma((8, 2)),
        dma((5, 2)),
        dma((5, 2)),
        dma((EARLY * QUARTERS, 4)),
        dma((EARLY * QUARTERS, 4)),
        dma((8, 2)),
        dma((8, 2)),
        dma((STEPS, 16)),
        dma((STEPS, 16)),
        dma((UNITS, 16)),
        dma((UNITS, 16)),
        dma((24,)),
        dma((24,)),
    ]
    return pl.pallas_call(
        block_kernel,
        out_shape=jax.ShapeDtypeStruct((ROWS, FEATS), BF16),
        in_specs=[vmem, vmem, vmem] + [anywhere] * 7,
        out_specs=vmem,
        scratch_shapes=scratch,
        compiler_params=pltpu.CompilerParams(
            collective_id=0, has_side_effects=True, vmem_limit_bytes=60 * 1024 * 1024
        ),
    )(
        activations,
        ln_gain,
        segments.reshape(1, TOKENS),
        jnp.asarray(tables()),
        w_query,
        w_key_value,
        w_gate,
        w_up,
        w_out,
        w_down,
    )


def solution(mesh):
    placed = (
        P("ffn", "hid"),
        P("hid"),
        P(),
        P("hid", "ffn"),
        P("hid", None),
        P("hid", "ffn"),
        P("hid", "ffn"),
        P("ffn", "hid"),
        P("ffn", "hid"),
    )
    return jax.shard_map(
        per_device, mesh=mesh, in_specs=placed, out_specs=P("ffn", "hid"), check_vma=False
    )
```

```python
import jax
import jax.numpy as jnp
import numpy as np
from jax import lax
from jax.experimental import pallas as pl
from jax.experimental.pallas import tpu as pltpu
from jax.sharding import PartitionSpec as P

D = 10240
HEAD = 256
TOKENS = 1024
EPSILON = 1e-06

SIDE = 4
RING = 8
GROUP = SIDE * SIDE
ROWS = TOKENS // GROUP
FEATS = D // GROUP
WIDE = 384
STEPS = 7
EARLY = 3
PAIRED = 6
UNITS = 8
HALF = ROWS // 2
QUARTERS = 4
QUARTER = ROWS // 4
F32 = jnp.float32
BF16 = jnp.bfloat16


def tables():
    half = HEAD // 2
    frequency = np.float32(10000.0) ** (-np.arange(half, dtype=np.float32) / np.float32(half))
    angles = np.arange(TOKENS, dtype=np.float32)[:, None] * frequency[None, :].astype(np.float32)
    wide = angles.astype(np.float64)
    return np.stack([np.cos(wide), np.sin(wide)]).astype(np.float32)


def block_kernel(
    act,
    gain,
    seg,
    table,
    w_query,
    w_pairs,
    w_gate,
    w_up,
    w_out,
    w_down,
    out,
    w_in,
    w_back,
    w_kv,
    turn,
    stat,
    stat_in,
    stat_other,
    stat_all,
    raw_all,
    rows_all,
    pair_part,
    pair_in,
    pair_sum,
    pair_all,
    kv_all,
    part,
    land1,
    last1,
    near_sum,
    land2,
    last2,
    mixed,
    total,
    sib_out,
    sib_in,
    ring_out,
    ring_in,
    w_sem,
    wb_sem,
    m_sem,
    small_s,
    small_r,
    zx_s,
    zx_r,
    zt_s,
    zt_r,
    rq_s,
    rq_r,
    zk_s,
    zk_r,
    rs_s,
    rs_r,
    ag_s,
    ag_r,
    zr_s,
    zr_r,
):
    hid = lax.axis_index("hid")
    ffn = lax.axis_index("ffn")
    x, y = hid // SIDE, hid % SIDE
    z, core = ffn // 2, ffn % 2

    def mod4(v):
        return (v + SIDE) % SIDE

    def mod8(v):
        return (v + RING) % RING

    ids_x = {d: mod4(x + d) * SIDE + y for d in (1, 2, 3)}
    ids_y = {d: x * SIDE + mod4(y + d) for d in (1, 2, 3)}
    ids_z = {d: mod8(z + d) * 2 + core for d in (1, -1)}

    def dev_x(d):
        return (ids_x[d % SIDE], ffn)

    def dev_y(d):
        return (ids_y[d % SIDE], ffn)

    def dev_z(d):
        return (hid, ids_z[d])

    other = z * 2 + 1 - core
    sibling = (hid, other)
    dirs = (1, -1)
    devs = ((dev_x, dev_y), (dev_y, dev_x))

    barrier = pltpu.get_barrier_semaphore()
    partners = [dev_x(d) for d in (1, 2, 3)] + [dev_y(d) for d in (1, 2, 3)]
    partners += [(ids_y[d], other) for d in (1, 2, 3)]
    partners += [dev_z(1), dev_z(-1), sibling]
    for dev in partners:
        pl.semaphore_signal(barrier, inc=1, device_id=dev, device_id_type=pl.DeviceIdType.MESH)

    def remote(src, dst, ssem, rsem, dev):
        return pltpu.make_async_remote_copy(
            src_ref=src,
            dst_ref=dst,
            send_sem=ssem,
            recv_sem=rsem,
            device_id=dev,
            device_id_type=pl.DeviceIdType.MESH,
        )

    def w_copy(s, o):
        if s == 0:
            src = w_query.at[:, pl.ds(o * WIDE, WIDE)]
        else:
            src = (w_gate, w_up)[o].at[:, pl.ds((s - 1) * WIDE, WIDE)]
        return pltpu.make_async_copy(src, w_in.at[s, :, pl.ds(o * WIDE, WIDE)], w_sem.at[s, o])

    def wb_copy(u):
        if u < 2:
            src = w_out.at[pl.ds(u * WIDE, WIDE)]
        else:
            src = w_down.at[pl.ds((u - 2) * WIDE, WIDE)]
        return pltpu.make_async_copy(src, w_back.at[u], wb_sem.at[u])

    def turn_copies(i):
        copies = [
            pltpu.make_async_copy(
                table.at[i, pl.ds(pl.multiple_of(ffn * ROWS, ROWS), ROWS)],
                turn.at[1, i],
                m_sem.at[1 + 5 * i],
            )
        ]
        for g in range(QUARTERS):
            first = pl.multiple_of(g * (TOKENS // QUARTERS) + hid * QUARTER, QUARTER)
            copies.append(
                pltpu.make_async_copy(
                    table.at[i, pl.ds(first, QUARTER)],
                    turn.at[0, i, pl.ds(g * QUARTER, QUARTER)],
                    m_sem.at[2 + 5 * i + g],
                )
            )
        return copies

    kv_copy = pltpu.make_async_copy(w_pairs, w_kv, m_sem.at[0])

    pl.semaphore_wait(barrier, len(partners))

    def stat_copy(a, d):
        return remote(
            stat.at[a], stat_in.at[a, d - 1], small_s.at[a, d - 1], small_r.at[a, d - 1],
            (dev_x, dev_y)[a](d),
        )

    def other_copy(d):
        return remote(
            stat.at[1], stat_other.at[d], small_s.at[5 + d // 3, d % 3], small_r.at[5 + d // 3, d % 3],
            (ids_y[d], other) if d else sibling,
        )

    def pair_copy(k, d):
        if k == 0:
            src, dst, dev = pair_part.at[mod4(x + d)], pair_in.at[0, d - 1], dev_x(d)
        elif k == 1:
            src, dst, dev = pair_sum, pair_in.at[1, d - 1], dev_y(d)
        else:
            src, dst, dev = pair_all.at[x], pair_all.at[x], dev_x(d)
        return remote(src, dst, small_s.at[2 + k, d - 1], small_r.at[2 + k, d - 1], dev)

    def each(fn, k, what):
        for d in (1, 2, 3):
            getattr(fn(k, d), what)()

    def z_copy(buf, sems, j, i):
        d = dirs[i]
        block = mod8(z - (j - 1) * d) * 2 + core
        ref = buf.at[block] if j < 4 else buf.at[block, pl.ds(i * HALF, HALF)]
        return remote(ref, ref, sems[0].at[j - 1, i], sems[1].at[j - 1, i], dev_z(d))

    def sib_copy(buf, sems, off):
        ref = buf.at[mod8(z + off) * 2 + core]
        row = 4 + (off + 3) // 2
        col = (off + 3) % 2
        return remote(ref, ref, sems[0].at[row, col], sems[1].at[row, col], sibling)

    def z_start(buf, sems):
        for i in range(2):
            z_copy(buf, sems, 1, i).start()
        sib_copy(buf, sems, 0).start()

    def z_step(buf, sems, j):
        if j < 4:
            for i in range(2):
                z_copy(buf, sems, j, i).wait()
                z_copy(buf, sems, j + 1, i).start()
                sib_copy(buf, sems, -j * dirs[i]).start()
        else:
            for i in range(2):
                z_copy(buf, sems, j, i).wait()
            sib_copy(buf, sems, 4).start()

    def sib_wait(buf, sems, *offs):
        for off in offs:
            sib_copy(buf, sems, off).wait()

    def stat_z(j, i):
        ref = stat_all.at[mod8(z - (j - 1) * dirs[i])]
        return remote(ref, ref, zt_s.at[j, i], zt_r.at[j, i], dev_z(dirs[i]))

    def stat_step(j):
        for i in range(2):
            if (j, i) == (4, 1):
                continue
            stat_z(j, i).wait()
            if j < 3 + (i == 0):
                stat_z(j + 1, i).start()

    def quarter_copy(s, j, g, o, i):
        at = o * 2 + i
        return remote(
            part.at[s, o, pl.ds((6, 10)[i], 4), g],
            land1.at[s, o, i, :, g],
            rq_s.at[s * QUARTERS + j, at],
            rq_r.at[s * QUARTERS + j, at],
            devs[o][0](dirs[i]),
        )

    both = [(o, i) for o in range(2) for i in range(2)]
    rel_x = [mod4(k - x) for k in range(SIDE)]
    rel_y = [mod4(k - y) for k in range(SIDE)]
    places = (
        [rel_x[h // SIDE] * SIDE + rel_y[h % SIDE] for h in range(GROUP)],
        [rel_y[h % SIDE] * SIDE + rel_x[h // SIDE] for h in range(GROUP)],
    )

    def products(s, g):
        rows = rows_all[pl.ds(g * QUARTERS, QUARTERS)].reshape(QUARTERS * ROWS, FEATS)
        res = jnp.dot(rows, w_in[s], preferred_element_type=F32).astype(BF16)
        for h in range(GROUP):
            block = res[h * QUARTER : (h + 1) * QUARTER]
            for o in range(2):
                part[s, o, places[o][h], g] = block[:, o * WIDE : (o + 1) * WIDE]

    eye = lax.broadcasted_iota(jnp.int32, (ROWS, 128), 0) == lax.broadcasted_iota(
        jnp.int32, (ROWS, 128), 1
    )
    line = lax.broadcasted_iota(jnp.int32, (8, 128), 0)

    def to_row(column):
        return jnp.sum(jnp.where(eye, column, 0.0), 0, keepdims=True)

    def to_column(row):
        return jnp.sum(jnp.where(eye, row, 0.0), 1, keepdims=True)

    def norm(rows, tile):
        mean, scale = to_column(tile[0:1]), to_column(tile[1:2])
        return ((rows.astype(F32) - mean) * scale * gain[...].reshape(1, FEATS)).astype(BF16)

    zx = (zx_s, zx_r)
    zk = (zk_s, zk_r)
    raw_all[ffn] = act[...]
    z_start(raw_all, zx)
    values = act[...].astype(F32)
    mean = jnp.mean(values, 1, keepdims=True)
    square = jnp.sum((values - mean) ** 2, 1, keepdims=True)
    mean, square = to_row(mean), to_row(square)
    def merge(count, tiles):
        means = [tile[0:1] for tile in tiles]
        squares = [tile[1:2] for tile in tiles]
        mean = (means[0] + means[1] + means[2] + means[3]) * 0.25
        square = squares[0] + squares[1] + squares[2] + squares[3]
        for one in means:
            square += count * (one - mean) ** 2
        return mean, square

    def finish(tiles):
        mean, square = merge(FEATS * SIDE, tiles)
        return jnp.where(line == 0, mean, lax.rsqrt(square * (1.0 / D) + EPSILON))

    stat[0] = jnp.where(line == 0, mean, square)
    each(stat_copy, 0, "start")
    kv_copy.start()
    for s in range(EARLY):
        for o in range(2):
            w_copy(s, o).start()
    total[...] = jnp.zeros_like(total)
    each(stat_copy, 0, "wait")
    mean, square = merge(FEATS, [stat[0]] + [stat_in[0, d] for d in range(3)])
    stat[1] = jnp.where(line == 0, mean, square)
    each(stat_copy, 1, "start")
    for d in range(SIDE):
        other_copy(d).start()
    z_step(raw_all, zx, 1)
    each(stat_copy, 1, "wait")
    for d in range(SIDE):
        other_copy(d).wait()
    stat_all[z, core] = finish([stat[1]] + [stat_in[1, d] for d in range(3)])
    stat_all[z, 1 - core] = finish([stat_other[d] for d in range(SIDE)])
    for i in range(2):
        stat_z(1, i).start()
    normed = norm(act[...], stat_all[z, core])
    kv_copy.wait()
    pairs = jnp.dot(normed, w_kv[...], preferred_element_type=F32).astype(BF16)
    for q in range(4):
        pair_part[q] = pairs[:, q * 128 : (q + 1) * 128]
    each(pair_copy, 0, "start")
    for s in range(EARLY):
        for o in range(2):
            w_copy(s, o).wait()

    pair = z // 2
    turned = 1 - 2 * (z % 2)
    order = (pair, mod4(pair - turned), mod4(pair + turned), mod4(pair + 2))

    def first_rows(j):
        g = order[j]

        def one(k, carry):
            rows_all[g * 4 + k] = norm(raw_all[g * 4 + k], stat_all[g * 2 + k // 2, k % 2])
            return carry

        lax.fori_loop(0, QUARTERS, one, 0)

    def first_products(j, steps):
        g = order[j]
        for s in steps:
            products(s, g)
            for o, i in both:
                quarter_copy(s, j, g, o, i).start()

    stat_step(1)
    sib_wait(raw_all, zx, 0, 1, -1)
    first_rows(0)
    first_products(0, (0,))
    z_step(raw_all, zx, 2)
    first_products(0, range(1, EARLY))
    for s in range(EARLY, STEPS):
        for o in range(2):
            w_copy(s, o).start()
    each(pair_copy, 0, "wait")
    pair_sum[...] = (
        pair_part[x].astype(F32)
        + pair_in[0, 0].astype(F32)
        + pair_in[0, 1].astype(F32)
        + pair_in[0, 2].astype(F32)
    ).astype(BF16)
    each(pair_copy, 1, "start")
    z_step(raw_all, zx, 3)
    stat_step(2)
    sib_wait(raw_all, zx, 2, -2)
    first_rows(1)
    first_products(1, range(EARLY))
    for i in range(2):
        for copy in turn_copies(i):
            copy.start()
    for u in range(UNITS):
        wb_copy(u).start()
    each(pair_copy, 1, "wait")
    pair_all[x] = (
        pair_sum[...].astype(F32)
        + pair_in[1, 0].astype(F32)
        + pair_in[1, 1].astype(F32)
        + pair_in[1, 2].astype(F32)
    ).astype(BF16)
    each(pair_copy, 2, "start")
    z_step(raw_all, zx, 4)
    stat_step(3)
    sib_wait(raw_all, zx, 3, -3)
    first_rows(2)
    first_products(2, range(EARLY))
    stat_step(4)
    sib_wait(raw_all, zx, 4)
    first_rows(3)
    first_products(3, range(EARLY))
    each(pair_copy, 2, "wait")
    for i in range(2):
        for copy in turn_copies(i):
            copy.wait()
    first, second = pair_all[0].astype(F32), pair_all[1].astype(F32)
    kv_all[ffn, :, 0:128] = (first * turn[1, 0] - second * turn[1, 1]).astype(BF16)
    kv_all[ffn, :, 128:256] = (first * turn[1, 1] + second * turn[1, 0]).astype(BF16)
    kv_all[ffn, :, 256:384] = pair_all[2]
    kv_all[ffn, :, 384:512] = pair_all[3]
    z_start(kv_all, zk)

    for s in range(EARLY, STEPS):
        for o in range(2):
            w_copy(s, o).wait()
    for u in range(UNITS):
        wb_copy(u).wait()

    far1 = ((6, 4), (10, 4))
    near1 = ((4, 2), (14, 2))

    def rs_copy(s, o, k, i):
        at = o * 8 + k * 2 + i
        if k < 2:
            first, size = (far1, near1)[k][i]
            src = part.at[s, o, pl.ds(first, size)]
        elif k == 2:
            src = near_sum.at[s, o, pl.ds((6, 10)[i], 4)]
        else:
            src = near_sum.at[s, o, pl.ds((4, 14)[i], 2)]
        return remote(
            src,
            (land1, last1, land2, last2)[k].at[s, o, i],
            rs_s.at[s, at],
            rs_r.at[s, at],
            devs[o][k // 2](dirs[i]),
        )

    def phase0(s):
        def tile(g, carry):
            products(s, g)
            return carry

        lax.fori_loop(0, QUARTERS, tile, 0)
        for o, i in both:
            rs_copy(s, o, 0, i).start()

    def added(first, *rest):
        res = first.astype(F32)
        for one in rest:
            res += one.astype(F32)
        return res

    def phase1(s):
        @pl.when(s < EARLY)
        def _():
            for j in range(QUARTERS):
                for o, i in both:
                    quarter_copy(s, j, order[j], o, i).wait()

        @pl.when(s >= EARLY)
        def _():
            for o, i in both:
                rs_copy(s, o, 0, i).wait()

        for o, i in both:
            first, size = near1[i]
            part[s, o, first : first + size] += land1[s, o, i, 2 - 2 * i : 4 - 2 * i]
            rs_copy(s, o, 1, i).start()

    def phase2(s):
        for o in range(2):
            for i in range(2):
                rs_copy(s, o, 1, i).wait()
            for i in range(2):
                res = added(
                    part[s, o, 2 * i : 2 * i + 2],
                    last1[s, o, i],
                    land1[s, o, 1 - i, 2 - 2 * i : 4 - 2 * i],
                ).astype(BF16)
                near_sum[s, o, 8 * i : 8 * i + 8] = res.reshape(2 * QUARTERS, QUARTER, WIDE)
            for i in range(2):
                rs_copy(s, o, 2, i).start()

    def phase3(s):
        for o, i in both:
            rs_copy(s, o, 2, i).wait()
            first = (4, 14)[i]
            near_sum[s, o, first : first + 2] += land2[s, o, i, 2 - 2 * i : 4 - 2 * i]
            rs_copy(s, o, 3, i).start()

    def attend(left, right):
        seg_row = seg[...].astype(F32)
        key_at = lax.broadcasted_iota(jnp.int32, (ROWS, TOKENS), 1)
        row_at = lax.broadcasted_iota(jnp.int32, (ROWS, TOKENS), 0)
        row_at = row_at + (TOKENS // QUARTERS - QUARTER) * (row_at // QUARTER) + hid * QUARTER
        own = jnp.sum(jnp.where(key_at == row_at, seg_row, 0.0), 1, keepdims=True)
        allowed = (key_at <= row_at) & (seg_row == own)
        keys = kv_all[:, :, 0:HEAD].reshape(TOKENS, HEAD)
        vals = kv_all[:, :, HEAD : 2 * HEAD].reshape(TOKENS, HEAD)
        cosine, sine = turn[0, 0] * HEAD**-0.5, turn[0, 1] * HEAD**-0.5
        groups = [v[:, k * 128 : (k + 1) * 128] for v in (left, right) for k in range(3)]
        query = []
        for h in range(3):
            a, b = groups[2 * h], groups[2 * h + 1]
            query.append(jnp.concatenate([a * cosine - b * sine, a * sine + b * cosine], 1))
        scores = lax.dot_general(
            jnp.concatenate(query, 0).astype(BF16),
            keys,
            (((1,), (1,)), ((), ())),
            preferred_element_type=F32,
        )
        probs = []
        for h in range(3):
            expos = jnp.where(allowed, jnp.exp(scores[h * ROWS : (h + 1) * ROWS]), 0.0)
            probs.append((expos / jnp.sum(expos, 1, keepdims=True)).astype(BF16))
        res = jnp.dot(jnp.concatenate(probs, 0), vals, preferred_element_type=F32).astype(BF16)
        pieces = [
            res[h * ROWS : (h + 1) * ROWS, k * 128 : (k + 1) * 128]
            for h in range(3)
            for k in range(2)
        ]
        return jnp.concatenate(pieces[:3], 1), jnp.concatenate(pieces[3:], 1)

    def put(u, block):
        for o in range(2):
            mixed[u // 2, o, 0, 0, u % 2] = block[o * HALF : (o + 1) * HALF]

    def gather_copy(u, n, o, k, i):
        d = dirs[i]
        away, near = (3, 1)[i], (3, 1)[i]
        dev = devs[o][k // 2](d)
        pair = mixed.at[u // 2, o]
        which = pl.ds(u % 2, 1) if n == 1 else pl.ds(0, 2)
        if k == 0:
            src, dst = pair.at[0, 0, which], pair.at[0, away, which]
        elif k == 1:
            rows = pl.ds(i * QUARTER, QUARTER)
            src, dst = pair.at[0, near, which, rows], pair.at[0, 2, which, rows]
        elif k == 2:
            src, dst = pair.at[0, :, which], pair.at[away, :, which]
        else:
            cut = pl.ds(2 * i, 2)
            src, dst = pair.at[near, cut, which], pair.at[2, cut, which]
        at = o * 8 + k * 2 + i
        return remote(src, dst, ag_s.at[u, at], ag_r.at[u, at], dev)

    def by_units(u, fn):
        pl.when((u % 2 == 1) & (u < PAIRED))(lambda: fn(u - 1, 2))
        pl.when(u >= PAIRED)(lambda: fn(u, 1))

    def gather_first(u, n):
        for o, i in both:
            gather_copy(u, n, o, 0, i).start()

    def phase4(s):
        sums = []
        for o in range(2):
            for i in range(2):
                rs_copy(s, o, 3, i).wait()
            sums.append(
                jnp.concatenate(
                    [
                        added(
                            near_sum[s, o, 2 * i : 2 * i + 2],
                            last2[s, o, i],
                            land2[s, o, 1 - i, 2 - 2 * i : 4 - 2 * i],
                        ).reshape(HALF, WIDE)
                        for i in range(2)
                    ],
                    0,
                )
            )

        @pl.when(s == 0)
        def _():
            left, right = attend(*sums)
            put(0, left)
            put(1, right)
            gather_first(0, 2)

        @pl.when(s > 0)
        def _():
            gate, up = sums
            put(s + 1, (gate / (1.0 + jnp.exp(-gate)) * up).astype(BF16))
            by_units(s + 1, gather_first)

    def phase5(u, n):
        for o, i in both:
            gather_copy(u, n, o, 0, i).wait()
            gather_copy(u, n, o, 1, i).start()

    def phase6(u, n):
        for o in range(2):
            for i in range(2):
                gather_copy(u, n, o, 1, i).wait()
            for i in range(2):
                gather_copy(u, n, o, 2, i).start()

    def phase7(u, n):
        for o, i in both:
            gather_copy(u, n, o, 2, i).wait()
            gather_copy(u, n, o, 3, i).start()

    def accumulate(u, count):
        weights = w_back[pl.ds(u, count)].reshape(count * WIDE, FEATS)
        for o in range(2):
            for p in range(2):
                rows = [
                    mixed[u // 2, o, 2 * p : 2 * p + 2, :, one].reshape(2 * SIDE * HALF, WIDE)
                    for one in (range(2) if count == 2 else (u % 2,))
                ]
                total[o, p * 256 : (p + 1) * 256] += jnp.dot(
                    jnp.concatenate(rows, 1), weights, preferred_element_type=F32
                )

    def phase8(u, n):
        for o, i in both:
            gather_copy(u, n, o, 3, i).wait()
        accumulate(u, n)

    def slot(t, carry):
        pl.when((t >= EARLY) & (t < STEPS))(lambda: phase0(t))
        for k, fn in ((2, phase1), (4, phase2), (5, phase3)):
            s = t - k
            pl.when((s >= 0) & (s < STEPS))(lambda fn=fn, s=s: fn(s))

        for j in range(1, 5):

            @pl.when(t == j + 1)
            def _(j=j):
                z_step(kv_all, zk, j)
                if j == 4:
                    sib_wait(kv_all, zk, 0, 1, -1, 2, -2, 3, -3, 4)

        s4 = t - 6
        pl.when((s4 >= 0) & (s4 < STEPS))(lambda: phase4(s4))

        for k, fn in ((7, phase5), (8, phase6), (9, phase7), (10, phase8)):
            s = t - k

            @pl.when((s >= 0) & (s < STEPS))
            def _(fn=fn, s=s):
                by_units(s + 1, fn)

        return carry

    lax.fori_loop(2, STEPS + 10, slot, 0)

    offsets = (4, 3, -3, 2, -2, 1, -1, 0)

    def half_rows(block, h):
        g = block // SIDE
        o = g // 2
        px = mod4(block % SIDE - x)
        pieces = []
        for k in (2 * h, 2 * h + 1):
            place = jnp.where(o == 0, rel_y[k] * SIDE + px, px * SIDE + rel_y[k])
            first = pl.multiple_of(place * HALF + (g % 2) * QUARTER, QUARTER)
            pieces.append(total[o, pl.ds(first, QUARTER)])
        return jnp.concatenate(pieces, 0)

    def sib_sum(k):
        at = mod8(z + offsets[k])
        return remote(sib_out.at[at], sib_in.at[at], zr_s.at[k], zr_r.at[k], sibling)

    def sib_send(*which):
        for k in which:
            at = mod8(z + offsets[k])
            for h in range(2):
                sib_out[at, h * HALF : (h + 1) * HALF] = half_rows(at * 2 + 1 - core, h).astype(BF16)
            sib_sum(k).start()

    sib_send(0, 1, 2)

    def chip_sum(k, h):
        at = mod8(z + offsets[k])
        return half_rows(at * 2 + core, h) + sib_in[at, h * HALF : (h + 1) * HALF].astype(F32)

    def ring_copy(j, i, h):
        at = 8 + j * 4 + i * 2 + h
        return remote(
            ring_out.at[j, i, h], ring_in.at[j, i, h], zr_s.at[at], zr_r.at[at], dev_z(dirs[i])
        )

    sib_sum(0).wait()
    for i in range(2):
        ring_out[0, i, i] = chip_sum(0, i).astype(BF16)
        ring_copy(0, i, i).start()
    sib_send(3, 4)
    for j in (1, 2, 3):
        for i in range(2):
            sib_sum(2 * j - 1 + i).wait()
        for turn_of in range(2):
            for i in range(2):
                h = (1 - i, i)[turn_of]
                here = chip_sum(2 * j - 1 + i, h)
                if j > 1 or h == i:
                    ring_copy(j - 1, i, h).wait()
                    here += ring_in[j - 1, i, h].astype(F32)
                ring_out[j, i, h] = here.astype(BF16)
                ring_copy(j, i, h).start()
        if j < 3:
            sib_send(*((5, 6), (7,))[j - 1])
    sib_sum(7).wait()
    for h in range(2):
        here = chip_sum(7, h) + act[h * HALF : (h + 1) * HALF].astype(F32)
        for i in range(2):
            ring_copy(3, i, h).wait()
            here += ring_in[3, i, h].astype(F32)
        out[h * HALF : (h + 1) * HALF] = here.astype(BF16)


def per_device(activations, ln_gain, segments, w_query, w_key_value, w_gate, w_up, w_out, w_down):
    vmem = pl.BlockSpec(memory_space=pltpu.VMEM)
    anywhere = pl.BlockSpec(memory_space=pl.ANY)
    dma = pltpu.SemaphoreType.DMA
    scratch = [
        pltpu.VMEM((STEPS, FEATS, 2 * WIDE), BF16),
        pltpu.VMEM((UNITS, WIDE, FEATS), BF16),
        pltpu.VMEM((FEATS, 512), BF16),
        pltpu.VMEM((2, 2, ROWS, 128), F32),
        pltpu.VMEM((2, 8, 128), F32),
        pltpu.VMEM((2, 3, 8, 128), F32),
        pltpu.VMEM((4, 8, 128), F32),
        pltpu.VMEM((RING, 2, 8, 128), F32),
        pltpu.VMEM((GROUP, ROWS, FEATS), BF16),
        pltpu.VMEM((GROUP, ROWS, FEATS), BF16),
        pltpu.VMEM((4, ROWS, 128), BF16),
        pltpu.VMEM((2, 3, ROWS, 128), BF16),
        pltpu.VMEM((ROWS, 128), BF16),
        pltpu.VMEM((4, ROWS, 128), BF16),
        pltpu.VMEM((GROUP, ROWS, 512), BF16),
        pltpu.VMEM((STEPS, 2, GROUP, QUARTERS, QUARTER, WIDE), BF16),
        pltpu.VMEM((STEPS, 2, 2, 4, QUARTERS, QUARTER, WIDE), BF16),
        pltpu.VMEM((STEPS, 2, 2, 2, QUARTERS, QUARTER, WIDE), BF16),
        pltpu.VMEM((STEPS, 2, SIDE * QUARTERS, QUARTER, WIDE), BF16),
        pltpu.VMEM((STEPS, 2, 2, QUARTERS, QUARTER, WIDE), BF16),
        pltpu.VMEM((STEPS, 2, 2, 2, QUARTER, WIDE), BF16),
        pltpu.VMEM((UNITS // 2, 2, SIDE, SIDE, 2, HALF, WIDE), BF16),
        pltpu.VMEM((2, GROUP * HALF, FEATS), F32),
        pltpu.VMEM((RING, ROWS, FEATS), BF16),
        pltpu.VMEM((RING, ROWS, FEATS), BF16),
        pltpu.VMEM((4, 2, 2, HALF, FEATS), BF16),
        pltpu.VMEM((4, 2, 2, HALF, FEATS), BF16),
        dma((STEPS, 2)),
        dma((UNITS,)),
        dma((11,)),
        dma((7, 3)),
        dma((7, 3)),
        dma((8, 2)),
        dma((8, 2)),
        dma((5, 2)),
        dma((5, 2)),
        dma((EARLY * QUARTERS, 4)),
        dma((EARLY * QUARTERS, 4)),
        dma((8, 2)),
        dma((8, 2)),
        dma((STEPS, 16)),
        dma((STEPS, 16)),
        dma((UNITS, 16)),
        dma((UNITS, 16)),
        dma((24,)),
        dma((24,)),
    ]
    return pl.pallas_call(
        block_kernel,
        out_shape=jax.ShapeDtypeStruct((ROWS, FEATS), BF16),
        in_specs=[vmem, vmem, vmem] + [anywhere] * 7,
        out_specs=vmem,
        scratch_shapes=scratch,
        compiler_params=pltpu.CompilerParams(
            collective_id=0, has_side_effects=True, vmem_limit_bytes=60 * 1024 * 1024
        ),
    )(
        activations,
        ln_gain,
        segments.reshape(1, TOKENS),
        jnp.asarray(tables()),
        w_query,
        w_key_value,
        w_gate,
        w_up,
        w_out,
        w_down,
    )


def solution(mesh):
    placed = (
        P("ffn", "hid"),
        P("hid"),
        P(),
        P("hid", "ffn"),
        P("hid", None),
        P("hid", "ffn"),
        P("hid", "ffn"),
        P("ffn", "hid"),
        P("ffn", "hid"),
    )
    return jax.shard_map(
        per_device, mesh=mesh, in_specs=placed, out_specs=P("ffn", "hid"), check_vma=False
    )
```

```python
import jax
import jax.numpy as jnp
import numpy as np
from jax import lax
from jax.experimental import pallas as pl
from jax.experimental.pallas import tpu as pltpu
from jax.sharding import PartitionSpec as P

D = 10240
HEAD = 256
TOKENS = 1024
EPSILON = 1e-06

SIDE = 4
RING = 8
GROUP = SIDE * SIDE
ROWS = TOKENS // GROUP
FEATS = D // GROUP
WIDE = 384
STEPS = 7
EARLY = 3
PAIRED = 2
UNITS = 8
HALF = ROWS // 2
QUARTERS = 4
QUARTER = ROWS // 4
F32 = jnp.float32
BF16 = jnp.bfloat16


def tables():
    half = HEAD // 2
    frequency = np.float32(10000.0) ** (-np.arange(half, dtype=np.float32) / np.float32(half))
    angles = np.arange(TOKENS, dtype=np.float32)[:, None] * frequency[None, :].astype(np.float32)
    wide = angles.astype(np.float64)
    return np.stack([np.cos(wide), np.sin(wide)]).astype(np.float32)


def block_kernel(
    act,
    gain,
    seg,
    table,
    w_query,
    w_pairs,
    w_gate,
    w_up,
    w_out,
    w_down,
    out,
    w_in,
    w_back,
    w_kv,
    turn,
    stat,
    stat_in,
    stat_other,
    stat_all,
    raw_all,
    rows_all,
    pair_part,
    pair_in,
    pair_sum,
    pair_all,
    kv_all,
    part,
    land1,
    last1,
    near_sum,
    land2,
    last2,
    mixed,
    total,
    sib_out,
    sib_in,
    ring_out,
    ring_in,
    w_sem,
    wb_sem,
    m_sem,
    small_s,
    small_r,
    zx_s,
    zx_r,
    zt_s,
    zt_r,
    rq_s,
    rq_r,
    zk_s,
    zk_r,
    rs_s,
    rs_r,
    ag_s,
    ag_r,
    zr_s,
    zr_r,
):
    hid = lax.axis_index("hid")
    ffn = lax.axis_index("ffn")
    x, y = hid // SIDE, hid % SIDE
    z, core = ffn // 2, ffn % 2

    def mod4(v):
        return (v + SIDE) % SIDE

    def mod8(v):
        return (v + RING) % RING

    ids_x = {d: mod4(x + d) * SIDE + y for d in (1, 2, 3)}
    ids_y = {d: x * SIDE + mod4(y + d) for d in (1, 2, 3)}
    ids_z = {d: mod8(z + d) * 2 + core for d in (1, -1)}

    def dev_x(d):
        return (ids_x[d % SIDE], ffn)

    def dev_y(d):
        return (ids_y[d % SIDE], ffn)

    def dev_z(d):
        return (hid, ids_z[d])

    other = z * 2 + 1 - core
    sibling = (hid, other)
    dirs = (1, -1)
    devs = ((dev_x, dev_y), (dev_y, dev_x))

    barrier = pltpu.get_barrier_semaphore()
    partners = [dev_x(d) for d in (1, 2, 3)] + [dev_y(d) for d in (1, 2, 3)]
    partners += [(ids_y[d], other) for d in (1, 2, 3)]
    partners += [dev_z(1), dev_z(-1), sibling]
    for dev in partners:
        pl.semaphore_signal(barrier, inc=1, device_id=dev, device_id_type=pl.DeviceIdType.MESH)

    def remote(src, dst, ssem, rsem, dev):
        return pltpu.make_async_remote_copy(
            src_ref=src,
            dst_ref=dst,
            send_sem=ssem,
            recv_sem=rsem,
            device_id=dev,
            device_id_type=pl.DeviceIdType.MESH,
        )

    def w_copy(s, o):
        if s == 0:
            src = w_query.at[:, pl.ds(o * WIDE, WIDE)]
        else:
            src = (w_gate, w_up)[o].at[:, pl.ds((s - 1) * WIDE, WIDE)]
        return pltpu.make_async_copy(src, w_in.at[s, :, pl.ds(o * WIDE, WIDE)], w_sem.at[s, o])

    def wb_copy(u):
        if u < 2:
            src = w_out.at[pl.ds(u * WIDE, WIDE)]
        else:
            src = w_down.at[pl.ds((u - 2) * WIDE, WIDE)]
        return pltpu.make_async_copy(src, w_back.at[u], wb_sem.at[u])

    def turn_copies(i):
        copies = [
            pltpu.make_async_copy(
                table.at[i, pl.ds(pl.multiple_of(ffn * ROWS, ROWS), ROWS)],
                turn.at[1, i],
                m_sem.at[1 + 5 * i],
            )
        ]
        for g in range(QUARTERS):
            first = pl.multiple_of(g * (TOKENS // QUARTERS) + hid * QUARTER, QUARTER)
            copies.append(
                pltpu.make_async_copy(
                    table.at[i, pl.ds(first, QUARTER)],
                    turn.at[0, i, pl.ds(g * QUARTER, QUARTER)],
                    m_sem.at[2 + 5 * i + g],
                )
            )
        return copies

    kv_copy = pltpu.make_async_copy(w_pairs, w_kv, m_sem.at[0])

    kv_copy.start(priority=1)
    for s in range(EARLY):
        for o in range(2):
            w_copy(s, o).start(priority=1)
    pl.semaphore_wait(barrier, len(partners))

    def stat_copy(a, d):
        return remote(
            stat.at[a], stat_in.at[a, d - 1], small_s.at[a, d - 1], small_r.at[a, d - 1],
            (dev_x, dev_y)[a](d),
        )

    def other_copy(d):
        return remote(
            stat.at[1], stat_other.at[d], small_s.at[5 + d // 3, d % 3], small_r.at[5 + d // 3, d % 3],
            (ids_y[d], other) if d else sibling,
        )

    def pair_copy(k, d):
        if k == 0:
            src, dst, dev = pair_part.at[mod4(x + d)], pair_in.at[0, d - 1], dev_x(d)
        elif k == 1:
            src, dst, dev = pair_sum, pair_in.at[1, d - 1], dev_y(d)
        else:
            src, dst, dev = pair_all.at[x], pair_all.at[x], dev_x(d)
        return remote(src, dst, small_s.at[2 + k, d - 1], small_r.at[2 + k, d - 1], dev)

    def each(fn, k, what):
        for d in (1, 2, 3):
            getattr(fn(k, d), what)()

    def z_copy(buf, sems, j, i):
        d = dirs[i]
        block = mod8(z - (j - 1) * d) * 2 + core
        ref = buf.at[block] if j < 4 else buf.at[block, pl.ds(i * HALF, HALF)]
        return remote(ref, ref, sems[0].at[j - 1, i], sems[1].at[j - 1, i], dev_z(d))

    def sib_copy(buf, sems, off):
        ref = buf.at[mod8(z + off) * 2 + core]
        row = 4 + (off + 3) // 2
        col = (off + 3) % 2
        return remote(ref, ref, sems[0].at[row, col], sems[1].at[row, col], sibling)

    def z_start(buf, sems):
        for i in range(2):
            z_copy(buf, sems, 1, i).start()
        sib_copy(buf, sems, 0).start()

    def z_step(buf, sems, j):
        if j < 4:
            for i in range(2):
                z_copy(buf, sems, j, i).wait()
                z_copy(buf, sems, j + 1, i).start()
                sib_copy(buf, sems, -j * dirs[i]).start()
        else:
            for i in range(2):
                z_copy(buf, sems, j, i).wait()
            sib_copy(buf, sems, 4).start()

    def sib_wait(buf, sems, *offs):
        for off in offs:
            sib_copy(buf, sems, off).wait()

    def stat_z(j, i):
        ref = stat_all.at[mod8(z - (j - 1) * dirs[i])]
        return remote(ref, ref, zt_s.at[j, i], zt_r.at[j, i], dev_z(dirs[i]))

    def stat_step(j):
        for i in range(2):
            if (j, i) == (4, 1):
                continue
            stat_z(j, i).wait()
            if j < 3 + (i == 0):
                stat_z(j + 1, i).start()

    def quarter_copy(s, j, g, o, i):
        at = o * 2 + i
        return remote(
            part.at[s, o, pl.ds((6, 10)[i], 4), g],
            land1.at[s, o, i, :, g],
            rq_s.at[s * QUARTERS + j, at],
            rq_r.at[s * QUARTERS + j, at],
            devs[o][0](dirs[i]),
        )

    both = [(o, i) for o in range(2) for i in range(2)]
    rel_x = [mod4(k - x) for k in range(SIDE)]
    rel_y = [mod4(k - y) for k in range(SIDE)]
    places = (
        [rel_x[h // SIDE] * SIDE + rel_y[h % SIDE] for h in range(GROUP)],
        [rel_y[h % SIDE] * SIDE + rel_x[h // SIDE] for h in range(GROUP)],
    )

    def products(s, g):
        rows = rows_all[pl.ds(g * QUARTERS, QUARTERS)].reshape(QUARTERS * ROWS, FEATS)
        res = jnp.dot(rows, w_in[s], preferred_element_type=F32).astype(BF16)
        for h in range(GROUP):
            block = res[h * QUARTER : (h + 1) * QUARTER]
            for o in range(2):
                part[s, o, places[o][h], g] = block[:, o * WIDE : (o + 1) * WIDE]

    eye = lax.broadcasted_iota(jnp.int32, (ROWS, 128), 0) == lax.broadcasted_iota(
        jnp.int32, (ROWS, 128), 1
    )
    line = lax.broadcasted_iota(jnp.int32, (8, 128), 0)

    def to_row(column):
        return jnp.sum(jnp.where(eye, column, 0.0), 0, keepdims=True)

    def to_column(row):
        return jnp.sum(jnp.where(eye, row, 0.0), 1, keepdims=True)

    def norm(rows, tile):
        mean, scale = to_column(tile[0:1]), to_column(tile[1:2])
        return ((rows.astype(F32) - mean) * scale * gain[...].reshape(1, FEATS)).astype(BF16)

    zx = (zx_s, zx_r)
    zk = (zk_s, zk_r)
    raw_all[ffn] = act[...]
    z_start(raw_all, zx)
    values = act[...].astype(F32)
    mean = jnp.mean(values, 1, keepdims=True)
    square = jnp.sum((values - mean) ** 2, 1, keepdims=True)
    mean, square = to_row(mean), to_row(square)
    def merge(count, tiles):
        means = [tile[0:1] for tile in tiles]
        squares = [tile[1:2] for tile in tiles]
        mean = (means[0] + means[1] + means[2] + means[3]) * 0.25
        square = squares[0] + squares[1] + squares[2] + squares[3]
        for one in means:
            square += count * (one - mean) ** 2
        return mean, square

    def finish(tiles):
        mean, square = merge(FEATS * SIDE, tiles)
        return jnp.where(line == 0, mean, lax.rsqrt(square * (1.0 / D) + EPSILON))

    stat[0] = jnp.where(line == 0, mean, square)
    each(stat_copy, 0, "start")
    total[...] = jnp.zeros_like(total)
    each(stat_copy, 0, "wait")
    mean, square = merge(FEATS, [stat[0]] + [stat_in[0, d] for d in range(3)])
    stat[1] = jnp.where(line == 0, mean, square)
    each(stat_copy, 1, "start")
    for d in range(SIDE):
        other_copy(d).start()
    z_step(raw_all, zx, 1)
    each(stat_copy, 1, "wait")
    for d in range(SIDE):
        other_copy(d).wait()
    stat_all[z, core] = finish([stat[1]] + [stat_in[1, d] for d in range(3)])
    stat_all[z, 1 - core] = finish([stat_other[d] for d in range(SIDE)])
    for i in range(2):
        stat_z(1, i).start()
    normed = norm(act[...], stat_all[z, core])
    kv_copy.wait()
    pairs = jnp.dot(normed, w_kv[...], preferred_element_type=F32).astype(BF16)
    for q in range(4):
        pair_part[q] = pairs[:, q * 128 : (q + 1) * 128]
    each(pair_copy, 0, "start")
    for s in range(EARLY):
        for o in range(2):
            w_copy(s, o).wait()

    pair = z // 2
    turned = 1 - 2 * (z % 2)
    order = (pair, mod4(pair - turned), mod4(pair + turned), mod4(pair + 2))

    def first_rows(j):
        g = order[j]

        def one(k, carry):
            rows_all[g * 4 + k] = norm(raw_all[g * 4 + k], stat_all[g * 2 + k // 2, k % 2])
            return carry

        lax.fori_loop(0, QUARTERS, one, 0)

    def first_products(j, steps):
        g = order[j]
        for s in steps:
            products(s, g)
            for o, i in both:
                quarter_copy(s, j, g, o, i).start()

    stat_step(1)
    sib_wait(raw_all, zx, 0, 1, -1)
    first_rows(0)
    first_products(0, (0,))
    z_step(raw_all, zx, 2)
    first_products(0, range(1, EARLY))
    for s in range(EARLY, STEPS):
        for o in range(2):
            w_copy(s, o).start(priority=1)
    each(pair_copy, 0, "wait")
    pair_sum[...] = (
        pair_part[x].astype(F32)
        + pair_in[0, 0].astype(F32)
        + pair_in[0, 1].astype(F32)
        + pair_in[0, 2].astype(F32)
    ).astype(BF16)
    each(pair_copy, 1, "start")
    z_step(raw_all, zx, 3)
    stat_step(2)
    sib_wait(raw_all, zx, 2, -2)
    first_rows(1)
    first_products(1, range(EARLY))
    for i in range(2):
        for copy in turn_copies(i):
            copy.start(priority=1)
    for u in range(UNITS):
        wb_copy(u).start(priority=1)
    each(pair_copy, 1, "wait")
    pair_all[x] = (
        pair_sum[...].astype(F32)
        + pair_in[1, 0].astype(F32)
        + pair_in[1, 1].astype(F32)
        + pair_in[1, 2].astype(F32)
    ).astype(BF16)
    each(pair_copy, 2, "start")
    z_step(raw_all, zx, 4)
    stat_step(3)
    sib_wait(raw_all, zx, 3, -3)
    first_rows(2)
    first_products(2, range(EARLY))
    stat_step(4)
    sib_wait(raw_all, zx, 4)
    first_rows(3)
    first_products(3, range(EARLY))
    each(pair_copy, 2, "wait")
    for i in range(2):
        for copy in turn_copies(i):
            copy.wait()
    first, second = pair_all[0].astype(F32), pair_all[1].astype(F32)
    kv_all[ffn, :, 0:128] = (first * turn[1, 0] - second * turn[1, 1]).astype(BF16)
    kv_all[ffn, :, 128:256] = (first * turn[1, 1] + second * turn[1, 0]).astype(BF16)
    kv_all[ffn, :, 256:384] = pair_all[2]
    kv_all[ffn, :, 384:512] = pair_all[3]
    z_start(kv_all, zk)

    for s in range(EARLY, STEPS):
        for o in range(2):
            w_copy(s, o).wait()
    for u in range(UNITS):
        wb_copy(u).wait()

    far1 = ((6, 4), (10, 4))
    near1 = ((4, 2), (14, 2))

    def rs_copy(s, o, k, i):
        at = o * 8 + k * 2 + i
        if k < 2:
            first, size = (far1, near1)[k][i]
            src = part.at[s, o, pl.ds(first, size)]
        elif k == 2:
            src = near_sum.at[s, o, pl.ds((6, 10)[i], 4)]
        else:
            src = near_sum.at[s, o, pl.ds((4, 14)[i], 2)]
        return remote(
            src,
            (land1, last1, land2, last2)[k].at[s, o, i],
            rs_s.at[s, at],
            rs_r.at[s, at],
            devs[o][k // 2](dirs[i]),
        )

    def phase0(s):
        def tile(g, carry):
            products(s, g)
            return carry

        lax.fori_loop(0, QUARTERS, tile, 0)
        for o, i in both:
            rs_copy(s, o, 0, i).start()

    def added(first, *rest):
        res = first.astype(F32)
        for one in rest:
            res += one.astype(F32)
        return res

    def phase1(s):
        @pl.when(s < EARLY)
        def _():
            for j in range(QUARTERS):
                for o, i in both:
                    quarter_copy(s, j, order[j], o, i).wait()

        @pl.when(s >= EARLY)
        def _():
            for o, i in both:
                rs_copy(s, o, 0, i).wait()

        for o, i in both:
            first, size = near1[i]
            part[s, o, first : first + size] += land1[s, o, i, 2 - 2 * i : 4 - 2 * i]
            rs_copy(s, o, 1, i).start()

    def phase2(s):
        for o in range(2):
            for i in range(2):
                rs_copy(s, o, 1, i).wait()
            for i in range(2):
                res = added(
                    part[s, o, 2 * i : 2 * i + 2],
                    last1[s, o, i],
                    land1[s, o, 1 - i, 2 - 2 * i : 4 - 2 * i],
                ).astype(BF16)
                near_sum[s, o, 8 * i : 8 * i + 8] = res.reshape(2 * QUARTERS, QUARTER, WIDE)
            for i in range(2):
                rs_copy(s, o, 2, i).start()

    def phase3(s):
        for o, i in both:
            rs_copy(s, o, 2, i).wait()
            first = (4, 14)[i]
            near_sum[s, o, first : first + 2] += land2[s, o, i, 2 - 2 * i : 4 - 2 * i]
            rs_copy(s, o, 3, i).start()

    def attend(left, right):
        seg_row = seg[...].astype(F32)
        key_at = lax.broadcasted_iota(jnp.int32, (ROWS, TOKENS), 1)
        row_at = lax.broadcasted_iota(jnp.int32, (ROWS, TOKENS), 0)
        row_at = row_at + (TOKENS // QUARTERS - QUARTER) * (row_at // QUARTER) + hid * QUARTER
        own = jnp.sum(jnp.where(key_at == row_at, seg_row, 0.0), 1, keepdims=True)
        allowed = (key_at <= row_at) & (seg_row == own)
        keys = kv_all[:, :, 0:HEAD].reshape(TOKENS, HEAD)
        vals = kv_all[:, :, HEAD : 2 * HEAD].reshape(TOKENS, HEAD)
        cosine, sine = turn[0, 0] * HEAD**-0.5, turn[0, 1] * HEAD**-0.5
        groups = [v[:, k * 128 : (k + 1) * 128] for v in (left, right) for k in range(3)]
        query = []
        for h in range(3):
            a, b = groups[2 * h], groups[2 * h + 1]
            query.append(jnp.concatenate([a * cosine - b * sine, a * sine + b * cosine], 1))
        scores = lax.dot_general(
            jnp.concatenate(query, 0).astype(BF16),
            keys,
            (((1,), (1,)), ((), ())),
            preferred_element_type=F32,
        )
        probs = []
        for h in range(3):
            expos = jnp.where(allowed, jnp.exp(scores[h * ROWS : (h + 1) * ROWS]), 0.0)
            probs.append((expos / jnp.sum(expos, 1, keepdims=True)).astype(BF16))
        res = jnp.dot(jnp.concatenate(probs, 0), vals, preferred_element_type=F32).astype(BF16)
        pieces = [
            res[h * ROWS : (h + 1) * ROWS, k * 128 : (k + 1) * 128]
            for h in range(3)
            for k in range(2)
        ]
        return jnp.concatenate(pieces[:3], 1), jnp.concatenate(pieces[3:], 1)

    def put(u, block):
        for o in range(2):
            mixed[u // 2, o, 0, 0, u % 2] = block[o * HALF : (o + 1) * HALF]

    def gather_copy(u, n, o, k, i):
        d = dirs[i]
        away, near = (3, 1)[i], (3, 1)[i]
        dev = devs[o][k // 2](d)
        pair = mixed.at[u // 2, o]
        which = pl.ds(u % 2, 1) if n == 1 else pl.ds(0, 2)
        if k == 0:
            src, dst = pair.at[0, 0, which], pair.at[0, away, which]
        elif k == 1:
            rows = pl.ds(i * QUARTER, QUARTER)
            src, dst = pair.at[0, near, which, rows], pair.at[0, 2, which, rows]
        elif k == 2:
            src, dst = pair.at[0, :, which], pair.at[away, :, which]
        else:
            cut = pl.ds(2 * i, 2)
            src, dst = pair.at[near, cut, which], pair.at[2, cut, which]
        at = o * 8 + k * 2 + i
        return remote(src, dst, ag_s.at[u, at], ag_r.at[u, at], dev)

    def by_units(u, fn):
        pl.when((u % 2 == 1) & (u < PAIRED))(lambda: fn(u - 1, 2))
        pl.when(u >= PAIRED)(lambda: fn(u, 1))

    def gather_first(u, n):
        for o, i in both:
            gather_copy(u, n, o, 0, i).start()

    def phase4(s):
        sums = []
        for o in range(2):
            for i in range(2):
                rs_copy(s, o, 3, i).wait()
            sums.append(
                jnp.concatenate(
                    [
                        added(
                            near_sum[s, o, 2 * i : 2 * i + 2],
                            last2[s, o, i],
                            land2[s, o, 1 - i, 2 - 2 * i : 4 - 2 * i],
                        ).reshape(HALF, WIDE)
                        for i in range(2)
                    ],
                    0,
                )
            )

        @pl.when(s == 0)
        def _():
            left, right = attend(*sums)
            put(0, left)
            put(1, right)
            gather_first(0, 2)

        @pl.when(s > 0)
        def _():
            gate, up = sums
            put(s + 1, (gate / (1.0 + jnp.exp(-gate)) * up).astype(BF16))
            by_units(s + 1, gather_first)

    def phase5(u, n):
        for o, i in both:
            gather_copy(u, n, o, 0, i).wait()
            gather_copy(u, n, o, 1, i).start()

    def phase6(u, n):
        for o in range(2):
            for i in range(2):
                gather_copy(u, n, o, 1, i).wait()
            for i in range(2):
                gather_copy(u, n, o, 2, i).start()

    def phase7(u, n):
        for o, i in both:
            gather_copy(u, n, o, 2, i).wait()
            gather_copy(u, n, o, 3, i).start()

    def accumulate(u, count):
        weights = w_back[pl.ds(u, count)].reshape(count * WIDE, FEATS)
        for o in range(2):
            for p in range(2):
                rows = [
                    mixed[u // 2, o, 2 * p : 2 * p + 2, :, one].reshape(2 * SIDE * HALF, WIDE)
                    for one in (range(2) if count == 2 else (u % 2,))
                ]
                total[o, p * 256 : (p + 1) * 256] += jnp.dot(
                    jnp.concatenate(rows, 1), weights, preferred_element_type=F32
                )

    def phase8(u, n):
        for o, i in both:
            gather_copy(u, n, o, 3, i).wait()
        accumulate(u, n)

    def slot(t, carry):
        pl.when((t >= EARLY) & (t < STEPS))(lambda: phase0(t))
        for k, fn in ((2, phase1), (4, phase2), (5, phase3)):
            s = t - k
            pl.when((s >= 0) & (s < STEPS))(lambda fn=fn, s=s: fn(s))

        for j in range(1, 5):

            @pl.when(t == j + 1)
            def _(j=j):
                z_step(kv_all, zk, j)
                if j == 4:
                    sib_wait(kv_all, zk, 0, 1, -1, 2, -2, 3, -3, 4)

        s4 = t - 6
        pl.when((s4 >= 0) & (s4 < STEPS))(lambda: phase4(s4))

        for k, fn in ((7, phase5), (8, phase6), (9, phase7), (10, phase8)):
            s = t - k

            @pl.when((s >= 0) & (s < STEPS))
            def _(fn=fn, s=s):
                by_units(s + 1, fn)

        return carry

    lax.fori_loop(2, STEPS + 10, slot, 0)

    offsets = (4, 3, -3, 2, -2, 1, -1, 0)

    def some_rows(block, k):
        g = block // SIDE
        o = g // 2
        px = mod4(block % SIDE - x)
        place = jnp.where(o == 0, rel_y[k] * SIDE + px, px * SIDE + rel_y[k])
        first = pl.multiple_of(place * HALF + (g % 2) * QUARTER, QUARTER)
        return total[o, pl.ds(first, QUARTER)]

    def span(k):
        return slice(k * QUARTER, (k + 1) * QUARTER)

    def sib_sum(k):
        at = mod8(z + offsets[k])
        return remote(sib_out.at[at], sib_in.at[at], zr_s.at[k], zr_r.at[k], sibling)

    def sib_send(*which):
        for k in which:
            at = mod8(z + offsets[k])
            for q in range(4):
                sib_out[at, span(q)] = some_rows(at * 2 + 1 - core, q).astype(BF16)
            sib_sum(k).start()

    sib_send(0, 1, 2)

    def chip_sum(k, q):
        at = mod8(z + offsets[k])
        return some_rows(at * 2 + core, q) + sib_in[at, span(q)].astype(F32)

    def ring_copy(j, i, q):
        at = 8 + (j * 2 + i) * 4 + q
        return remote(
            ring_out.at[j, i, q], ring_in.at[j, i, q], zr_s.at[at], zr_r.at[at], dev_z(dirs[i])
        )

    sib_sum(0).wait()
    for q in range(2):
        for i in range(2):
            ring_out[0, i, 2 * i + q] = chip_sum(0, 2 * i + q).astype(BF16)
            ring_copy(0, i, 2 * i + q).start()
    sib_send(3, 4)
    for j in (1, 2, 3):
        for i in range(2):
            sib_sum(2 * j - 1 + i).wait()
        for turn_of in range(4):
            for i in range(2):
                q = (2 * (1 - i) + turn_of) % 4
                here = chip_sum(2 * j - 1 + i, q)
                if j > 1 or q // 2 == i:
                    ring_copy(j - 1, i, q).wait()
                    here += ring_in[j - 1, i, q].astype(F32)
                ring_out[j, i, q] = here.astype(BF16)
                ring_copy(j, i, q).start()
        if j < 3:
            sib_send(*((5, 6), (7,))[j - 1])
    sib_sum(7).wait()
    for q in (2, 0, 3, 1):
        here = chip_sum(7, q) + act[span(q)].astype(F32)
        for i in range(2):
            ring_copy(3, i, q).wait()
            here += ring_in[3, i, q].astype(F32)
        out[span(q)] = here.astype(BF16)


def per_device(activations, ln_gain, segments, w_query, w_key_value, w_gate, w_up, w_out, w_down):
    vmem = pl.BlockSpec(memory_space=pltpu.VMEM)
    anywhere = pl.BlockSpec(memory_space=pl.ANY)
    dma = pltpu.SemaphoreType.DMA
    scratch = [
        pltpu.VMEM((STEPS, FEATS, 2 * WIDE), BF16),
        pltpu.VMEM((UNITS, WIDE, FEATS), BF16),
        pltpu.VMEM((FEATS, 512), BF16),
        pltpu.VMEM((2, 2, ROWS, 128), F32),
        pltpu.VMEM((2, 8, 128), F32),
        pltpu.VMEM((2, 3, 8, 128), F32),
        pltpu.VMEM((4, 8, 128), F32),
        pltpu.VMEM((RING, 2, 8, 128), F32),
        pltpu.VMEM((GROUP, ROWS, FEATS), BF16),
        pltpu.VMEM((GROUP, ROWS, FEATS), BF16),
        pltpu.VMEM((4, ROWS, 128), BF16),
        pltpu.VMEM((2, 3, ROWS, 128), BF16),
        pltpu.VMEM((ROWS, 128), BF16),
        pltpu.VMEM((4, ROWS, 128), BF16),
        pltpu.VMEM((GROUP, ROWS, 512), BF16),
        pltpu.VMEM((STEPS, 2, GROUP, QUARTERS, QUARTER, WIDE), BF16),
        pltpu.VMEM((STEPS, 2, 2, 4, QUARTERS, QUARTER, WIDE), BF16),
        pltpu.VMEM((STEPS, 2, 2, 2, QUARTERS, QUARTER, WIDE), BF16),
        pltpu.VMEM((STEPS, 2, SIDE * QUARTERS, QUARTER, WIDE), BF16),
        pltpu.VMEM((STEPS, 2, 2, QUARTERS, QUARTER, WIDE), BF16),
        pltpu.VMEM((STEPS, 2, 2, 2, QUARTER, WIDE), BF16),
        pltpu.VMEM((UNITS // 2, 2, SIDE, SIDE, 2, HALF, WIDE), BF16),
        pltpu.VMEM((2, GROUP * HALF, FEATS), F32),
        pltpu.VMEM((RING, ROWS, FEATS), BF16),
        pltpu.VMEM((RING, ROWS, FEATS), BF16),
        pltpu.VMEM((4, 2, 4, QUARTER, FEATS), BF16),
        pltpu.VMEM((4, 2, 4, QUARTER, FEATS), BF16),
        dma((STEPS, 2)),
        dma((UNITS,)),
        dma((11,)),
        dma((7, 3)),
        dma((7, 3)),
        dma((8, 2)),
        dma((8, 2)),
        dma((5, 2)),
        dma((5, 2)),
        dma((EARLY * QUARTERS, 4)),
        dma((EARLY * QUARTERS, 4)),
        dma((8, 2)),
        dma((8, 2)),
        dma((STEPS, 16)),
        dma((STEPS, 16)),
        dma((UNITS, 16)),
        dma((UNITS, 16)),
        dma((40,)),
        dma((40,)),
    ]
    return pl.pallas_call(
        block_kernel,
        out_shape=jax.ShapeDtypeStruct((ROWS, FEATS), BF16),
        in_specs=[vmem, vmem, vmem] + [anywhere] * 7,
        out_specs=vmem,
        scratch_shapes=scratch,
        compiler_params=pltpu.CompilerParams(
            collective_id=0, has_side_effects=True, vmem_limit_bytes=60 * 1024 * 1024
        ),
    )(
        activations,
        ln_gain,
        segments.reshape(1, TOKENS),
        jnp.asarray(tables()),
        w_query,
        w_key_value,
        w_gate,
        w_up,
        w_out,
        w_down,
    )


def solution(mesh):
    placed = (
        P("ffn", "hid"),
        P("hid"),
        P(),
        P("hid", "ffn"),
        P("hid", None),
        P("hid", "ffn"),
        P("hid", "ffn"),
        P("ffn", "hid"),
        P("ffn", "hid"),
    )
    return jax.shard_map(
        per_device, mesh=mesh, in_specs=placed, out_specs=P("ffn", "hid"), check_vma=False
    )
```

```python
import jax
import jax.numpy as jnp
import numpy as np
from jax import lax
from jax.experimental import pallas as pl
from jax.experimental.pallas import tpu as pltpu
from jax.sharding import PartitionSpec as P

D = 10240
HEAD = 256
TOKENS = 1024
EPSILON = 1e-06

SIDE = 4
RING = 8
GROUP = SIDE * SIDE
ROWS = TOKENS // GROUP
FEATS = D // GROUP
WIDE = 384
STEPS = 7
EARLY = 3
UNITS = 8
HALF = ROWS // 2
QUARTERS = 4
QUARTER = ROWS // 4
F32 = jnp.float32
BF16 = jnp.bfloat16


def tables():
    half = HEAD // 2
    frequency = np.float32(10000.0) ** (-np.arange(half, dtype=np.float32) / np.float32(half))
    angles = np.arange(TOKENS, dtype=np.float32)[:, None] * frequency[None, :].astype(np.float32)
    wide = angles.astype(np.float64)
    return np.stack([np.cos(wide), np.sin(wide)]).astype(np.float32)


def block_kernel(
    act,
    gain,
    seg,
    table,
    w_query,
    w_pairs,
    w_gate,
    w_up,
    w_out,
    w_down,
    out,
    w_in,
    w_back,
    w_kv,
    turn,
    stat,
    stat_in,
    stat_other,
    stat_all,
    raw_all,
    rows_all,
    pair_part,
    pair_in,
    pair_sum,
    pair_all,
    heads,
    kv_all,
    part,
    land1,
    last1,
    near_sum,
    land2,
    last2,
    mixed,
    total,
    sib_out,
    sib_in,
    ring_out,
    ring_in,
    w_sem,
    wb_sem,
    m_sem,
    small_s,
    small_r,
    zx_s,
    zx_r,
    zt_s,
    zt_r,
    rq_s,
    rq_r,
    zk_s,
    zk_r,
    rs_s,
    rs_r,
    ag_s,
    ag_r,
    zr_s,
    zr_r,
):
    hid = lax.axis_index("hid")
    ffn = lax.axis_index("ffn")
    x, y = hid // SIDE, hid % SIDE
    z, core = ffn // 2, ffn % 2

    def mod4(v):
        return (v + SIDE) % SIDE

    def mod8(v):
        return (v + RING) % RING

    ids_x = {d: mod4(x + d) * SIDE + y for d in (1, 2, 3)}
    ids_y = {d: x * SIDE + mod4(y + d) for d in (1, 2, 3)}
    ids_z = {d: mod8(z + d) * 2 + core for d in (1, -1)}

    def dev_x(d):
        return (ids_x[d % SIDE], ffn)

    def dev_y(d):
        return (ids_y[d % SIDE], ffn)

    def dev_z(d):
        return (hid, ids_z[d])

    other = z * 2 + 1 - core
    sibling = (hid, other)
    dirs = (1, -1)
    devs = ((dev_x, dev_y), (dev_y, dev_x))

    barrier = pltpu.get_barrier_semaphore()
    partners = [dev_x(d) for d in (1, 2, 3)] + [dev_y(d) for d in (1, 2, 3)]
    partners += [(ids_y[d], other) for d in (1, 2, 3)]
    partners += [dev_z(1), dev_z(-1), sibling]
    for dev in partners:
        pl.semaphore_signal(barrier, inc=1, device_id=dev, device_id_type=pl.DeviceIdType.MESH)

    def remote(src, dst, ssem, rsem, dev):
        return pltpu.make_async_remote_copy(
            src_ref=src,
            dst_ref=dst,
            send_sem=ssem,
            recv_sem=rsem,
            device_id=dev,
            device_id_type=pl.DeviceIdType.MESH,
        )

    def w_copy(s, o):
        if s == 0:
            src = w_query.at[:, pl.ds(o * WIDE, WIDE)]
        else:
            src = (w_gate, w_up)[o].at[:, pl.ds((s - 1) * WIDE, WIDE)]
        return pltpu.make_async_copy(src, w_in.at[s, :, pl.ds(o * WIDE, WIDE)], w_sem.at[s, o])

    def wb_copy(u):
        if u < 2:
            src = w_out.at[pl.ds(u * WIDE, WIDE)]
        else:
            src = w_down.at[pl.ds((u - 2) * WIDE, WIDE)]
        return pltpu.make_async_copy(src, w_back.at[u], wb_sem.at[u])

    def turn_copies(i):
        copies = [
            pltpu.make_async_copy(
                table.at[i, pl.ds(pl.multiple_of(ffn * ROWS, ROWS), ROWS)],
                turn.at[1, i],
                m_sem.at[1 + 5 * i],
            )
        ]
        for g in range(QUARTERS):
            first = pl.multiple_of(g * (TOKENS // QUARTERS) + hid * QUARTER, QUARTER)
            copies.append(
                pltpu.make_async_copy(
                    table.at[i, pl.ds(first, QUARTER)],
                    turn.at[0, i, pl.ds(g * QUARTER, QUARTER)],
                    m_sem.at[2 + 5 * i + g],
                )
            )
        return copies

    kv_copy = pltpu.make_async_copy(w_pairs, w_kv, m_sem.at[0])

    kv_copy.start(priority=1)
    for s in range(EARLY):
        for o in range(2):
            w_copy(s, o).start(priority=1)
    pl.semaphore_wait(barrier, len(partners))

    def stat_copy(a, d):
        return remote(
            stat.at[a], stat_in.at[a, d - 1], small_s.at[a, d - 1], small_r.at[a, d - 1],
            (dev_x, dev_y)[a](d),
        )

    def other_copy(d):
        return remote(
            stat.at[1], stat_other.at[d], small_s.at[5 + d // 3, d % 3], small_r.at[5 + d // 3, d % 3],
            (ids_y[d], other) if d else sibling,
        )

    def pair_copy(k, d):
        if k == 0:
            src, dst, dev = pair_part.at[mod4(x + d)], pair_in.at[0, d - 1], dev_x(d)
        elif k == 1:
            src, dst, dev = pair_sum, pair_in.at[1, d - 1], dev_y(d)
        else:
            src, dst, dev = pair_all.at[x], pair_all.at[x], dev_x(d)
        return remote(src, dst, small_s.at[2 + k, d - 1], small_r.at[2 + k, d - 1], dev)

    def each(fn, k, what):
        for d in (1, 2, 3):
            getattr(fn(k, d), what)()

    def z_copy(buf, sems, j, i):
        d = dirs[i]
        block = mod8(z - (j - 1) * d) * 2 + core
        ref = buf.at[block] if j < 4 else buf.at[block, pl.ds(i * HALF, HALF)]
        return remote(ref, ref, sems[0].at[j - 1, i], sems[1].at[j - 1, i], dev_z(d))

    def sib_copy(buf, sems, off):
        ref = buf.at[mod8(z + off) * 2 + core]
        row = 4 + (off + 3) // 2
        col = (off + 3) % 2
        return remote(ref, ref, sems[0].at[row, col], sems[1].at[row, col], sibling)

    def z_start(buf, sems):
        for i in range(2):
            z_copy(buf, sems, 1, i).start()
        sib_copy(buf, sems, 0).start()

    def z_step(buf, sems, j):
        if j < 4:
            for i in range(2):
                z_copy(buf, sems, j, i).wait()
                z_copy(buf, sems, j + 1, i).start()
                sib_copy(buf, sems, -j * dirs[i]).start()
        else:
            for i in range(2):
                z_copy(buf, sems, j, i).wait()
            sib_copy(buf, sems, 4).start()

    def sib_wait(buf, sems, *offs):
        for off in offs:
            sib_copy(buf, sems, off).wait()

    def stat_z(j, i):
        ref = stat_all.at[mod8(z - (j - 1) * dirs[i])]
        return remote(ref, ref, zt_s.at[j, i], zt_r.at[j, i], dev_z(dirs[i]))

    def stat_step(j):
        for i in range(2):
            if (j, i) == (4, 1):
                continue
            stat_z(j, i).wait()
            if j < 3 + (i == 0):
                stat_z(j + 1, i).start()

    def added(first, *rest):
        res = first.astype(F32)
        for one in rest:
            res += one.astype(F32)
        return res

    def quarter_copy(s, j, g, o, i):
        at = o * 2 + i
        return remote(
            part.at[s, o, pl.ds((6, 10)[i], 4), g],
            land1.at[s, o, i, :, g],
            rq_s.at[s * QUARTERS + j, at],
            rq_r.at[s * QUARTERS + j, at],
            devs[o][0](dirs[i]),
        )

    both = [(o, i) for o in range(2) for i in range(2)]
    rel_x = [mod4(k - x) for k in range(SIDE)]
    rel_y = [mod4(k - y) for k in range(SIDE)]
    places = (
        [rel_x[h // SIDE] * SIDE + rel_y[h % SIDE] for h in range(GROUP)],
        [rel_y[h % SIDE] * SIDE + rel_x[h // SIDE] for h in range(GROUP)],
    )

    def products(s, g):
        rows = rows_all[pl.ds(g * QUARTERS, QUARTERS)].reshape(QUARTERS * ROWS, FEATS)
        res = jnp.dot(rows, w_in[s], preferred_element_type=F32).astype(BF16)
        for h in range(GROUP):
            block = res[h * QUARTER : (h + 1) * QUARTER]
            for o in range(2):
                part[s, o, places[o][h], g] = block[:, o * WIDE : (o + 1) * WIDE]

    eye = lax.broadcasted_iota(jnp.int32, (ROWS, 128), 0) == lax.broadcasted_iota(
        jnp.int32, (ROWS, 128), 1
    )
    line = lax.broadcasted_iota(jnp.int32, (8, 128), 0)

    def to_row(column):
        return jnp.sum(jnp.where(eye, column, 0.0), 0, keepdims=True)

    def to_column(row):
        return jnp.sum(jnp.where(eye, row, 0.0), 1, keepdims=True)

    def norm(rows, tile):
        mean, scale = to_column(tile[0:1]), to_column(tile[1:2])
        return ((rows.astype(F32) - mean) * scale * gain[...].reshape(1, FEATS)).astype(BF16)

    zx = (zx_s, zx_r)
    zk = (zk_s, zk_r)
    raw_all[ffn] = act[...]
    z_start(raw_all, zx)
    values = act[...].astype(F32)
    mean = jnp.mean(values, 1, keepdims=True)
    square = jnp.sum((values - mean) ** 2, 1, keepdims=True)
    mean, square = to_row(mean), to_row(square)
    def merge(count, tiles):
        means = [tile[0:1] for tile in tiles]
        squares = [tile[1:2] for tile in tiles]
        mean = (means[0] + means[1] + means[2] + means[3]) * 0.25
        square = squares[0] + squares[1] + squares[2] + squares[3]
        for one in means:
            square += count * (one - mean) ** 2
        return mean, square

    def finish(tiles):
        mean, square = merge(FEATS * SIDE, tiles)
        return jnp.where(line == 0, mean, lax.rsqrt(square * (1.0 / D) + EPSILON))

    stat[0] = jnp.where(line == 0, mean, square)
    each(stat_copy, 0, "start")
    total[...] = jnp.zeros_like(total)
    each(stat_copy, 0, "wait")
    mean, square = merge(FEATS, [stat[0]] + [stat_in[0, d] for d in range(3)])
    stat[1] = jnp.where(line == 0, mean, square)
    each(stat_copy, 1, "start")
    for d in range(SIDE):
        other_copy(d).start()
    z_step(raw_all, zx, 1)
    each(stat_copy, 1, "wait")
    for d in range(SIDE):
        other_copy(d).wait()
    stat_all[z, core] = finish([stat[1]] + [stat_in[1, d] for d in range(3)])
    stat_all[z, 1 - core] = finish([stat_other[d] for d in range(SIDE)])
    for i in range(2):
        stat_z(1, i).start()
    normed = norm(act[...], stat_all[z, core])
    kv_copy.wait()
    pairs = jnp.dot(normed, w_kv[...], preferred_element_type=F32).astype(BF16)
    for q in range(4):
        pair_part[q] = pairs[:, q * 128 : (q + 1) * 128]
    each(pair_copy, 0, "start")
    for s in range(EARLY):
        for o in range(2):
            w_copy(s, o).wait()

    pair = z // 2
    turned = 1 - 2 * (z % 2)
    def order(j):
        step = jnp.where(j == 3, 2, jnp.where(j == 0, 0, jnp.where(j == 1, -turned, turned)))
        return mod4(pair + step)

    def pair_add(own, a):
        return added(own, pair_in[a, 0], pair_in[a, 1], pair_in[a, 2]).astype(BF16)

    def early(j, carry):
        @pl.when(j == 0)
        def _():
            stat_step(1)
            sib_wait(raw_all, zx, 0, 1, -1)

        @pl.when(j == 1)
        def _():
            for s in range(EARLY, STEPS):
                for o in range(2):
                    w_copy(s, o).start(priority=1)
            each(pair_copy, 0, "wait")
            pair_sum[...] = pair_add(pair_part[x], 0)
            each(pair_copy, 1, "start")
            z_step(raw_all, zx, 3)
            stat_step(2)
            sib_wait(raw_all, zx, 2, -2)

        @pl.when(j == 2)
        def _():
            for i in range(2):
                for copy in turn_copies(i):
                    copy.start(priority=1)
            for u in range(UNITS):
                wb_copy(u).start(priority=1)
            each(pair_copy, 1, "wait")
            pair_all[x] = pair_add(pair_sum[...], 1)
            each(pair_copy, 2, "start")
            z_step(raw_all, zx, 4)
            stat_step(3)
            sib_wait(raw_all, zx, 3, -3)

        @pl.when(j == 3)
        def _():
            stat_step(4)
            sib_wait(raw_all, zx, 4)

        g = order(j)

        def one(k, c):
            rows_all[g * 4 + k] = norm(raw_all[g * 4 + k], stat_all[g * 2 + k // 2, k % 2])
            return c

        lax.fori_loop(0, QUARTERS, one, 0)

        def step(s, c):
            products(s, g)
            for o, i in both:
                quarter_copy(s, j, g, o, i).start()
            pl.when((j == 0) & (s == 0))(lambda: z_step(raw_all, zx, 2))
            return c

        lax.fori_loop(0, EARLY, step, 0)
        return carry

    lax.fori_loop(0, QUARTERS, early, 0)
    each(pair_copy, 2, "wait")
    for i in range(2):
        for copy in turn_copies(i):
            copy.wait()
    first, second = pair_all[0].astype(F32), pair_all[1].astype(F32)
    kv_all[ffn, :, 0:128] = (first * turn[1, 0] - second * turn[1, 1]).astype(BF16)
    kv_all[ffn, :, 128:256] = (first * turn[1, 1] + second * turn[1, 0]).astype(BF16)
    kv_all[ffn, :, 256:384] = pair_all[2]
    kv_all[ffn, :, 384:512] = pair_all[3]
    z_start(kv_all, zk)

    for s in range(EARLY, STEPS):
        for o in range(2):
            w_copy(s, o).wait()
    for u in range(UNITS):
        wb_copy(u).wait()

    far1 = ((6, 4), (10, 4))
    near1 = ((4, 2), (14, 2))

    def rs_copy(s, o, k, i):
        at = o * 8 + k * 2 + i
        if k < 2:
            first, size = (far1, near1)[k][i]
            src = part.at[s, o, pl.ds(first, size)]
        elif k == 2:
            src = near_sum.at[s, o, pl.ds((6, 10)[i], 4)]
        else:
            src = near_sum.at[s, o, pl.ds((4, 14)[i], 2)]
        return remote(
            src,
            (land1, last1, land2, last2)[k].at[s, o, i],
            rs_s.at[s, at],
            rs_r.at[s, at],
            devs[o][k // 2](dirs[i]),
        )

    def phase0(s):
        def tile(g, carry):
            products(s, g)
            return carry

        lax.fori_loop(0, QUARTERS, tile, 0)
        for o, i in both:
            rs_copy(s, o, 0, i).start()

    def phase1(s):
        @pl.when(s < EARLY)
        def _():
            def arrived(j, carry):
                for o, i in both:
                    quarter_copy(s, j, order(j), o, i).wait()
                return carry

            lax.fori_loop(0, QUARTERS, arrived, 0)

        @pl.when(s >= EARLY)
        def _():
            for o, i in both:
                rs_copy(s, o, 0, i).wait()

        for o, i in both:
            first, size = near1[i]
            part[s, o, first : first + size] += land1[s, o, i, 2 - 2 * i : 4 - 2 * i]
            rs_copy(s, o, 1, i).start()

    def phase2(s):
        for o in range(2):
            for i in range(2):
                rs_copy(s, o, 1, i).wait()
            for i in range(2):
                res = added(
                    part[s, o, 2 * i : 2 * i + 2],
                    last1[s, o, i],
                    land1[s, o, 1 - i, 2 - 2 * i : 4 - 2 * i],
                ).astype(BF16)
                near_sum[s, o, 8 * i : 8 * i + 8] = res.reshape(2 * QUARTERS, QUARTER, WIDE)
            for i in range(2):
                rs_copy(s, o, 2, i).start()

    def phase3(s):
        for o, i in both:
            rs_copy(s, o, 2, i).wait()
            first = (4, 14)[i]
            near_sum[s, o, first : first + 2] += land2[s, o, i, 2 - 2 * i : 4 - 2 * i]
            rs_copy(s, o, 3, i).start()

    def attend(left, right):
        seg_row = seg[...].astype(F32)
        key_at = lax.broadcasted_iota(jnp.int32, (ROWS, TOKENS), 1)
        row_at = lax.broadcasted_iota(jnp.int32, (ROWS, TOKENS), 0)
        row_at = row_at + (TOKENS // QUARTERS - QUARTER) * (row_at // QUARTER) + hid * QUARTER
        own = jnp.sum(jnp.where(key_at == row_at, seg_row, 0.0), 1, keepdims=True)
        allowed = (key_at <= row_at) & (seg_row == own)
        keys = kv_all[:, :, 0:HEAD].reshape(TOKENS, HEAD)
        vals = kv_all[:, :, HEAD : 2 * HEAD].reshape(TOKENS, HEAD)
        cosine, sine = turn[0, 0] * HEAD**-0.5, turn[0, 1] * HEAD**-0.5
        groups = [v[:, k * 128 : (k + 1) * 128] for v in (left, right) for k in range(3)]
        for h in range(3):
            a, b = groups[2 * h], groups[2 * h + 1]
            heads[h, :, 0:128] = (a * cosine - b * sine).astype(BF16)
            heads[h, :, 128:256] = (a * sine + b * cosine).astype(BF16)

        def head(h, carry):
            scores = lax.dot_general(
                heads[h], keys, (((1,), (1,)), ((), ())), preferred_element_type=F32
            )
            expos = jnp.where(allowed, jnp.exp(scores), 0.0)
            probs = (expos / jnp.sum(expos, 1, keepdims=True)).astype(BF16)
            heads[h] = jnp.dot(probs, vals, preferred_element_type=F32).astype(BF16)
            return carry

        lax.fori_loop(0, 3, head, 0)
        left = jnp.concatenate([heads[0], heads[1, :, 0:128]], 1)
        right = jnp.concatenate([heads[1, :, 128:256], heads[2]], 1)
        return left, right

    def put(u, block):
        for o in range(2):
            mixed[u // 2, o, 0, 0, u % 2] = block[o * HALF : (o + 1) * HALF]

    def gather_copy(u, o, k, i):
        d = dirs[i]
        away, near = (3, 1)[i], (3, 1)[i]
        dev = devs[o][k // 2](d)
        pair = mixed.at[u // 2, o]
        which = u % 2
        if k == 0:
            src, dst = pair.at[0, 0, which], pair.at[0, away, which]
        elif k == 1:
            rows = pl.ds(i * QUARTER, QUARTER)
            src, dst = pair.at[0, near, which, rows], pair.at[0, 2, which, rows]
        elif k == 2:
            src, dst = pair.at[0, :, which], pair.at[away, :, which]
        else:
            cut = pl.ds(2 * i, 2)
            src, dst = pair.at[near, cut, which], pair.at[2, cut, which]
        at = o * 8 + k * 2 + i
        return remote(src, dst, ag_s.at[u, at], ag_r.at[u, at], dev)

    def by_units(s, fn):
        def unit(u, carry):
            fn(u)
            return carry

        lax.fori_loop(jnp.where(s == 0, 0, s + 1), s + 2, unit, 0)

    def gather_first(u):
        for o, i in both:
            gather_copy(u, o, 0, i).start()

    def phase4(s):
        sums = []
        for o in range(2):
            for i in range(2):
                rs_copy(s, o, 3, i).wait()
            sums.append(
                jnp.concatenate(
                    [
                        added(
                            near_sum[s, o, 2 * i : 2 * i + 2],
                            last2[s, o, i],
                            land2[s, o, 1 - i, 2 - 2 * i : 4 - 2 * i],
                        ).reshape(HALF, WIDE)
                        for i in range(2)
                    ],
                    0,
                )
            )

        @pl.when(s == 0)
        def _():
            left, right = attend(*sums)
            put(0, left)
            put(1, right)

        @pl.when(s > 0)
        def _():
            gate, up = sums
            put(s + 1, (gate / (1.0 + jnp.exp(-gate)) * up).astype(BF16))

        by_units(s, gather_first)

    def phase5(u):
        for o, i in both:
            gather_copy(u, o, 0, i).wait()
            gather_copy(u, o, 1, i).start()

    def phase6(u):
        for o in range(2):
            for i in range(2):
                gather_copy(u, o, 1, i).wait()
            for i in range(2):
                gather_copy(u, o, 2, i).start()

    def phase7(u):
        for o, i in both:
            gather_copy(u, o, 2, i).wait()
            gather_copy(u, o, 3, i).start()

    def accumulate(u):
        def tile(k, carry):
            o, p = k // 2, k % 2
            rows = mixed[u // 2, o, pl.ds(2 * p, 2), :, u % 2].reshape(2 * SIDE * HALF, WIDE)
            at = pl.ds(pl.multiple_of(p * 256, 256), 256)
            total[o, at] += jnp.dot(rows, w_back[u], preferred_element_type=F32)
            return carry

        lax.fori_loop(0, 4, tile, 0)

    def phase8(u):
        for o, i in both:
            gather_copy(u, o, 3, i).wait()
        accumulate(u)

    def slot(t, carry):
        pl.when((t >= EARLY) & (t < STEPS))(lambda: phase0(t))
        for k, fn in ((2, phase1), (4, phase2), (5, phase3)):
            s = t - k
            pl.when((s >= 0) & (s < STEPS))(lambda fn=fn, s=s: fn(s))

        for j in range(1, 5):

            @pl.when(t == j + 1)
            def _(j=j):
                z_step(kv_all, zk, j)
                if j == 4:
                    sib_wait(kv_all, zk, 0, 1, -1, 2, -2, 3, -3, 4)

        s4 = t - 6
        pl.when((s4 >= 0) & (s4 < STEPS))(lambda: phase4(s4))

        for k, fn in ((7, phase5), (8, phase6), (9, phase7), (10, phase8)):
            s = t - k

            @pl.when((s >= 0) & (s < STEPS))
            def _(fn=fn, s=s):
                by_units(s, fn)

        return carry

    lax.fori_loop(2, STEPS + 10, slot, 0)

    offsets = (4, 3, -3, 2, -2, 1, -1, 0)

    def some_rows(block, k):
        g = block // SIDE
        o = g // 2
        px = mod4(block % SIDE - x)
        place = jnp.where(o == 0, rel_y[k] * SIDE + px, px * SIDE + rel_y[k])
        first = pl.multiple_of(place * HALF + (g % 2) * QUARTER, QUARTER)
        return total[o, pl.ds(first, QUARTER)]

    def span(k):
        return slice(k * QUARTER, (k + 1) * QUARTER)

    def sib_sum(k):
        at = mod8(z + offsets[k])
        return remote(sib_out.at[at], sib_in.at[at], zr_s.at[k], zr_r.at[k], sibling)

    def sib_send(*which):
        for k in which:
            at = mod8(z + offsets[k])
            for q in range(4):
                sib_out[at, span(q)] = some_rows(at * 2 + 1 - core, q).astype(BF16)
            sib_sum(k).start()

    sib_send(0, 1, 2)

    def chip_sum(k, q):
        at = mod8(z + offsets[k])
        return some_rows(at * 2 + core, q) + sib_in[at, span(q)].astype(F32)

    def ring_copy(j, i, q):
        at = 8 + (j * 2 + i) * 4 + q
        return remote(
            ring_out.at[j, i, q], ring_in.at[j, i, q], zr_s.at[at], zr_r.at[at], dev_z(dirs[i])
        )

    sib_sum(0).wait()
    for q in range(2):
        for i in range(2):
            ring_out[0, i, 2 * i + q] = chip_sum(0, 2 * i + q).astype(BF16)
            ring_copy(0, i, 2 * i + q).start()
    sib_send(3, 4)
    for j in (1, 2, 3):
        for i in range(2):
            sib_sum(2 * j - 1 + i).wait()
        for turn_of in range(4):
            for i in range(2):
                q = (2 * (1 - i) + turn_of) % 4
                here = chip_sum(2 * j - 1 + i, q)
                if j > 1 or q // 2 == i:
                    ring_copy(j - 1, i, q).wait()
                    here += ring_in[j - 1, i, q].astype(F32)
                ring_out[j, i, q] = here.astype(BF16)
                ring_copy(j, i, q).start()
        if j < 3:
            sib_send(*((5, 6), (7,))[j - 1])
    sib_sum(7).wait()
    for q in (2, 0, 3, 1):
        here = chip_sum(7, q) + act[span(q)].astype(F32)
        for i in range(2):
            ring_copy(3, i, q).wait()
            here += ring_in[3, i, q].astype(F32)
        out[span(q)] = here.astype(BF16)


def per_device(activations, ln_gain, segments, w_query, w_key_value, w_gate, w_up, w_out, w_down):
    vmem = pl.BlockSpec(memory_space=pltpu.VMEM)
    anywhere = pl.BlockSpec(memory_space=pl.ANY)
    dma = pltpu.SemaphoreType.DMA
    scratch = [
        pltpu.VMEM((STEPS, FEATS, 2 * WIDE), BF16),
        pltpu.VMEM((UNITS, WIDE, FEATS), BF16),
        pltpu.VMEM((FEATS, 512), BF16),
        pltpu.VMEM((2, 2, ROWS, 128), F32),
        pltpu.VMEM((2, 8, 128), F32),
        pltpu.VMEM((2, 3, 8, 128), F32),
        pltpu.VMEM((4, 8, 128), F32),
        pltpu.VMEM((RING, 2, 8, 128), F32),
        pltpu.VMEM((GROUP, ROWS, FEATS), BF16),
        pltpu.VMEM((GROUP, ROWS, FEATS), BF16),
        pltpu.VMEM((4, ROWS, 128), BF16),
        pltpu.VMEM((2, 3, ROWS, 128), BF16),
        pltpu.VMEM((ROWS, 128), BF16),
        pltpu.VMEM((4, ROWS, 128), BF16),
        pltpu.VMEM((3, ROWS, HEAD), BF16),
        pltpu.VMEM((GROUP, ROWS, 512), BF16),
        pltpu.VMEM((STEPS, 2, GROUP, QUARTERS, QUARTER, WIDE), BF16),
        pltpu.VMEM((STEPS, 2, 2, 4, QUARTERS, QUARTER, WIDE), BF16),
        pltpu.VMEM((STEPS, 2, 2, 2, QUARTERS, QUARTER, WIDE), BF16),
        pltpu.VMEM((STEPS, 2, SIDE * QUARTERS, QUARTER, WIDE), BF16),
        pltpu.VMEM((STEPS, 2, 2, QUARTERS, QUARTER, WIDE), BF16),
        pltpu.VMEM((STEPS, 2, 2, 2, QUARTER, WIDE), BF16),
        pltpu.VMEM((UNITS // 2, 2, SIDE, SIDE, 2, HALF, WIDE), BF16),
        pltpu.VMEM((2, GROUP * HALF, FEATS), F32),
        pltpu.VMEM((RING, ROWS, FEATS), BF16),
        pltpu.VMEM((RING, ROWS, FEATS), BF16),
        pltpu.VMEM((4, 2, 4, QUARTER, FEATS), BF16),
        pltpu.VMEM((4, 2, 4, QUARTER, FEATS), BF16),
        dma((STEPS, 2)),
        dma((UNITS,)),
        dma((11,)),
        dma((7, 3)),
        dma((7, 3)),
        dma((8, 2)),
        dma((8, 2)),
        dma((5, 2)),
        dma((5, 2)),
        dma((EARLY * QUARTERS, 4)),
        dma((EARLY * QUARTERS, 4)),
        dma((8, 2)),
        dma((8, 2)),
        dma((STEPS, 16)),
        dma((STEPS, 16)),
        dma((UNITS, 16)),
        dma((UNITS, 16)),
        dma((40,)),
        dma((40,)),
    ]
    return pl.pallas_call(
        block_kernel,
        out_shape=jax.ShapeDtypeStruct((ROWS, FEATS), BF16),
        in_specs=[vmem, vmem, vmem] + [anywhere] * 7,
        out_specs=vmem,
        scratch_shapes=scratch,
        compiler_params=pltpu.CompilerParams(
            collective_id=0, has_side_effects=True, vmem_limit_bytes=60 * 1024 * 1024
        ),
    )(
        activations,
        ln_gain,
        segments.reshape(1, TOKENS),
        jnp.asarray(tables()),
        w_query,
        w_key_value,
        w_gate,
        w_up,
        w_out,
        w_down,
    )


def solution(mesh):
    placed = (
        P("ffn", "hid"),
        P("hid"),
        P(),
        P("hid", "ffn"),
        P("hid", None),
        P("hid", "ffn"),
        P("hid", "ffn"),
        P("ffn", "hid"),
        P("ffn", "hid"),
    )
    return jax.shard_map(
        per_device, mesh=mesh, in_specs=placed, out_specs=P("ffn", "hid"), check_vma=False
    )
```

```python
import jax
import jax.numpy as jnp
import numpy as np
from jax import lax
from jax.experimental import pallas as pl
from jax.experimental.pallas import tpu as pltpu
from jax.sharding import PartitionSpec as P

D = 10240
HEAD = 256
TOKENS = 1024
EPSILON = 1e-06

SIDE = 4
RING = 8
GROUP = SIDE * SIDE
ROWS = TOKENS // GROUP
FEATS = D // GROUP
WIDE = 384
STEPS = 7
EARLY = 3
UNITS = 8
HALF = ROWS // 2
QUARTERS = 4
QUARTER = ROWS // 4
F32 = jnp.float32
BF16 = jnp.bfloat16


def tables():
    half = HEAD // 2
    frequency = np.float32(10000.0) ** (-np.arange(half, dtype=np.float32) / np.float32(half))
    angles = np.arange(TOKENS, dtype=np.float32)[:, None] * frequency[None, :].astype(np.float32)
    wide = angles.astype(np.float64)
    return np.stack([np.cos(wide), np.sin(wide)]).astype(np.float32)


def block_kernel(
    act,
    gain,
    seg,
    table,
    w_query,
    w_pairs,
    w_gate,
    w_up,
    w_out,
    w_down,
    out,
    w_in,
    w_back,
    w_kv,
    turn,
    stat,
    stat_in,
    stat_other,
    stat_all,
    raw_all,
    rows_all,
    pair_part,
    pair_in,
    pair_sum,
    pair_all,
    heads,
    kv_all,
    part,
    land1,
    last1,
    near_sum,
    land2,
    last2,
    mixed,
    total,
    sib_out,
    sib_in,
    ring_out,
    ring_in,
    w_sem,
    wb_sem,
    m_sem,
    small_s,
    small_r,
    zx_s,
    zx_r,
    zt_s,
    zt_r,
    rq_s,
    rq_r,
    zk_s,
    zk_r,
    rs_s,
    rs_r,
    ag_s,
    ag_r,
    zr_s,
    zr_r,
):
    hid = lax.axis_index("hid")
    ffn = lax.axis_index("ffn")
    x, y = hid // SIDE, hid % SIDE
    z, core = ffn // 2, ffn % 2

    def mod4(v):
        return (v + SIDE) % SIDE

    def mod8(v):
        return (v + RING) % RING

    ids_x = {d: mod4(x + d) * SIDE + y for d in (1, 2, 3)}
    ids_y = {d: x * SIDE + mod4(y + d) for d in (1, 2, 3)}
    ids_z = {d: mod8(z + d) * 2 + core for d in (1, -1)}

    def dev_x(d):
        return (ids_x[d % SIDE], ffn)

    def dev_y(d):
        return (ids_y[d % SIDE], ffn)

    def dev_z(d):
        return (hid, ids_z[d])

    other = z * 2 + 1 - core
    sibling = (hid, other)
    dirs = (1, -1)

    ids_one = {d: jnp.where(core == 0, ids_x[d], ids_y[d]) for d in (1, 3)}
    ids_two = {d: jnp.where(core == 0, ids_y[d], ids_x[d]) for d in (1, 3)}

    def dev_one(d):
        return (ids_one[d % SIDE], ffn)

    def dev_two(d):
        return (ids_two[d % SIDE], ffn)

    devs = ((dev_one, dev_two), (dev_two, dev_one))

    barrier = pltpu.get_barrier_semaphore()
    partners = [dev_x(d) for d in (1, 2, 3)] + [dev_y(d) for d in (1, 2, 3)]
    partners += [(ids_y[d], other) for d in (1, 2, 3)]
    partners += [dev_z(1), dev_z(-1), sibling]
    for dev in partners:
        pl.semaphore_signal(barrier, inc=1, device_id=dev, device_id_type=pl.DeviceIdType.MESH)

    def remote(src, dst, ssem, rsem, dev):
        return pltpu.make_async_remote_copy(
            src_ref=src,
            dst_ref=dst,
            send_sem=ssem,
            recv_sem=rsem,
            device_id=dev,
            device_id_type=pl.DeviceIdType.MESH,
        )

    def w_copy(s, o):
        if s == 0:
            src = w_query.at[:, pl.ds(o * WIDE, WIDE)]
        else:
            src = (w_gate, w_up)[o].at[:, pl.ds((s - 1) * WIDE, WIDE)]
        return pltpu.make_async_copy(src, w_in.at[s, :, pl.ds(o * WIDE, WIDE)], w_sem.at[s, o])

    def wb_copy(u):
        if u < 2:
            src = w_out.at[pl.ds(u * WIDE, WIDE)]
        else:
            src = w_down.at[pl.ds((u - 2) * WIDE, WIDE)]
        return pltpu.make_async_copy(src, w_back.at[u], wb_sem.at[u])

    def turn_copies(i):
        copies = [
            pltpu.make_async_copy(
                table.at[i, pl.ds(pl.multiple_of(ffn * ROWS, ROWS), ROWS)],
                turn.at[1, i],
                m_sem.at[1 + 5 * i],
            )
        ]
        for g in range(QUARTERS):
            first = pl.multiple_of(g * (TOKENS // QUARTERS) + hid * QUARTER, QUARTER)
            copies.append(
                pltpu.make_async_copy(
                    table.at[i, pl.ds(first, QUARTER)],
                    turn.at[0, i, pl.ds(g * QUARTER, QUARTER)],
                    m_sem.at[2 + 5 * i + g],
                )
            )
        return copies

    kv_copy = pltpu.make_async_copy(w_pairs, w_kv, m_sem.at[0])

    kv_copy.start(priority=1)
    for s in range(EARLY):
        for o in range(2):
            w_copy(s, o).start(priority=1)
    pl.semaphore_wait(barrier, len(partners))

    def stat_copy(a, d):
        return remote(
            stat.at[a], stat_in.at[a, d - 1], small_s.at[a, d - 1], small_r.at[a, d - 1],
            (dev_x, dev_y)[a](d),
        )

    def other_copy(d):
        return remote(
            stat.at[1], stat_other.at[d], small_s.at[5 + d // 3, d % 3], small_r.at[5 + d // 3, d % 3],
            (ids_y[d], other) if d else sibling,
        )

    def pair_copy(k, d):
        if k == 0:
            src, dst, dev = pair_part.at[mod4(x + d)], pair_in.at[0, d - 1], dev_x(d)
        elif k == 1:
            src, dst, dev = pair_sum, pair_in.at[1, d - 1], dev_y(d)
        else:
            src, dst, dev = pair_all.at[x], pair_all.at[x], dev_x(d)
        return remote(src, dst, small_s.at[2 + k, d - 1], small_r.at[2 + k, d - 1], dev)

    def each(fn, k, what):
        for d in (1, 2, 3):
            getattr(fn(k, d), what)()

    def z_copy(buf, sems, j, i):
        d = dirs[i]
        block = mod8(z - (j - 1) * d) * 2 + core
        ref = buf.at[block] if j < 4 else buf.at[block, pl.ds(i * HALF, HALF)]
        return remote(ref, ref, sems[0].at[j - 1, i], sems[1].at[j - 1, i], dev_z(d))

    def sib_copy(buf, sems, off):
        ref = buf.at[mod8(z + off) * 2 + core]
        row = 4 + (off + 3) // 2
        col = (off + 3) % 2
        return remote(ref, ref, sems[0].at[row, col], sems[1].at[row, col], sibling)

    def z_start(buf, sems):
        for i in range(2):
            z_copy(buf, sems, 1, i).start()
        sib_copy(buf, sems, 0).start()

    def z_step(buf, sems, j):
        if j < 4:
            for i in range(2):
                z_copy(buf, sems, j, i).wait()
                z_copy(buf, sems, j + 1, i).start()
                sib_copy(buf, sems, -j * dirs[i]).start()
        else:
            for i in range(2):
                z_copy(buf, sems, j, i).wait()
            sib_copy(buf, sems, 4).start()

    def sib_wait(buf, sems, *offs):
        for off in offs:
            sib_copy(buf, sems, off).wait()

    def stat_z(j, i):
        ref = stat_all.at[mod8(z - (j - 1) * dirs[i])]
        return remote(ref, ref, zt_s.at[j, i], zt_r.at[j, i], dev_z(dirs[i]))

    def stat_step(j):
        for i in range(2):
            if (j, i) == (4, 1):
                continue
            stat_z(j, i).wait()
            if j < 3 + (i == 0):
                stat_z(j + 1, i).start()

    def added(first, *rest):
        res = first.astype(F32)
        for one in rest:
            res += one.astype(F32)
        return res

    def quarter_copy(s, j, g, o, i):
        at = o * 2 + i
        return remote(
            part.at[s, o, pl.ds((6, 10)[i], 4), g],
            land1.at[s, o, i, :, g],
            rq_s.at[s * QUARTERS + j, at],
            rq_r.at[s * QUARTERS + j, at],
            devs[o][0](dirs[i]),
        )

    both = [(o, i) for o in range(2) for i in range(2)]
    rel_x = [mod4(k - x) for k in range(SIDE)]
    rel_y = [mod4(k - y) for k in range(SIDE)]
    x_y = [rel_x[h // SIDE] * SIDE + rel_y[h % SIDE] for h in range(GROUP)]
    y_x = [rel_y[h % SIDE] * SIDE + rel_x[h // SIDE] for h in range(GROUP)]
    places = (
        [jnp.where(core == 0, a, b) for a, b in zip(x_y, y_x)],
        [jnp.where(core == 0, b, a) for a, b in zip(x_y, y_x)],
    )

    def products(s, g):
        rows = rows_all[pl.ds(g * QUARTERS, QUARTERS)].reshape(QUARTERS * ROWS, FEATS)
        res = jnp.dot(rows, w_in[s], preferred_element_type=F32).astype(BF16)
        for h in range(GROUP):
            block = res[h * QUARTER : (h + 1) * QUARTER]
            for o in range(2):
                part[s, o, places[o][h], g] = block[:, o * WIDE : (o + 1) * WIDE]

    eye = lax.broadcasted_iota(jnp.int32, (ROWS, 128), 0) == lax.broadcasted_iota(
        jnp.int32, (ROWS, 128), 1
    )
    line = lax.broadcasted_iota(jnp.int32, (8, 128), 0)

    def to_row(column):
        return jnp.sum(jnp.where(eye, column, 0.0), 0, keepdims=True)

    def to_column(row):
        return jnp.sum(jnp.where(eye, row, 0.0), 1, keepdims=True)

    def norm(rows, tile):
        mean, scale = to_column(tile[0:1]), to_column(tile[1:2])
        return ((rows.astype(F32) - mean) * scale * gain[...].reshape(1, FEATS)).astype(BF16)

    zx = (zx_s, zx_r)
    zk = (zk_s, zk_r)
    raw_all[ffn] = act[...]
    z_start(raw_all, zx)
    values = act[...].astype(F32)
    mean = jnp.mean(values, 1, keepdims=True)
    square = jnp.sum((values - mean) ** 2, 1, keepdims=True)
    mean, square = to_row(mean), to_row(square)
    def merge(count, tiles):
        means = [tile[0:1] for tile in tiles]
        squares = [tile[1:2] for tile in tiles]
        mean = (means[0] + means[1] + means[2] + means[3]) * 0.25
        square = squares[0] + squares[1] + squares[2] + squares[3]
        for one in means:
            square += count * (one - mean) ** 2
        return mean, square

    def finish(tiles):
        mean, square = merge(FEATS * SIDE, tiles)
        return jnp.where(line == 0, mean, lax.rsqrt(square * (1.0 / D) + EPSILON))

    stat[0] = jnp.where(line == 0, mean, square)
    each(stat_copy, 0, "start")
    total[...] = jnp.zeros_like(total)
    each(stat_copy, 0, "wait")
    mean, square = merge(FEATS, [stat[0]] + [stat_in[0, d] for d in range(3)])
    stat[1] = jnp.where(line == 0, mean, square)
    each(stat_copy, 1, "start")
    for d in range(SIDE):
        other_copy(d).start()
    z_step(raw_all, zx, 1)
    each(stat_copy, 1, "wait")
    for d in range(SIDE):
        other_copy(d).wait()
    stat_all[z, core] = finish([stat[1]] + [stat_in[1, d] for d in range(3)])
    stat_all[z, 1 - core] = finish([stat_other[d] for d in range(SIDE)])
    for i in range(2):
        stat_z(1, i).start()
    normed = norm(act[...], stat_all[z, core])
    kv_copy.wait()
    pairs = jnp.dot(normed, w_kv[...], preferred_element_type=F32).astype(BF16)
    for q in range(4):
        pair_part[q] = pairs[:, q * 128 : (q + 1) * 128]
    each(pair_copy, 0, "start")
    for s in range(EARLY):
        for o in range(2):
            w_copy(s, o).wait()

    pair = z // 2
    turned = 1 - 2 * (z % 2)
    def order(j):
        step = jnp.where(j == 3, 2, jnp.where(j == 0, 0, jnp.where(j == 1, -turned, turned)))
        return mod4(pair + step)

    def pair_add(own, a):
        return added(own, pair_in[a, 0], pair_in[a, 1], pair_in[a, 2]).astype(BF16)

    def early(j, carry):
        @pl.when(j == 0)
        def _():
            stat_step(1)
            sib_wait(raw_all, zx, 0, 1, -1)

        @pl.when(j == 1)
        def _():
            for s in range(EARLY, STEPS):
                for o in range(2):
                    w_copy(s, o).start(priority=1)
            each(pair_copy, 0, "wait")
            pair_sum[...] = pair_add(pair_part[x], 0)
            each(pair_copy, 1, "start")
            z_step(raw_all, zx, 3)
            stat_step(2)
            sib_wait(raw_all, zx, 2, -2)

        @pl.when(j == 2)
        def _():
            for i in range(2):
                for copy in turn_copies(i):
                    copy.start(priority=1)
            for u in range(UNITS):
                wb_copy(u).start(priority=1)
            each(pair_copy, 1, "wait")
            pair_all[x] = pair_add(pair_sum[...], 1)
            each(pair_copy, 2, "start")
            z_step(raw_all, zx, 4)
            stat_step(3)
            sib_wait(raw_all, zx, 3, -3)

        @pl.when(j == 3)
        def _():
            stat_step(4)
            sib_wait(raw_all, zx, 4)

        g = order(j)

        def one(k, c):
            rows_all[g * 4 + k] = norm(raw_all[g * 4 + k], stat_all[g * 2 + k // 2, k % 2])
            return c

        lax.fori_loop(0, QUARTERS, one, 0)

        def step(s, c):
            products(s, g)
            for o, i in both:
                quarter_copy(s, j, g, o, i).start()
            pl.when((j == 0) & (s == 0))(lambda: z_step(raw_all, zx, 2))
            return c

        lax.fori_loop(0, EARLY, step, 0)
        return carry

    lax.fori_loop(0, QUARTERS, early, 0)
    each(pair_copy, 2, "wait")
    for i in range(2):
        for copy in turn_copies(i):
            copy.wait()
    first, second = pair_all[0].astype(F32), pair_all[1].astype(F32)
    kv_all[ffn, :, 0:128] = (first * turn[1, 0] - second * turn[1, 1]).astype(BF16)
    kv_all[ffn, :, 128:256] = (first * turn[1, 1] + second * turn[1, 0]).astype(BF16)
    kv_all[ffn, :, 256:384] = pair_all[2]
    kv_all[ffn, :, 384:512] = pair_all[3]
    z_start(kv_all, zk)

    for s in range(EARLY, STEPS):
        for o in range(2):
            w_copy(s, o).wait()
    for u in range(UNITS):
        wb_copy(u).wait()

    far1 = ((6, 4), (10, 4))
    near1 = ((4, 2), (14, 2))

    def rs_copy(s, o, k, i):
        at = o * 8 + k * 2 + i
        if k < 2:
            first, size = (far1, near1)[k][i]
            src = part.at[s, o, pl.ds(first, size)]
        elif k == 2:
            src = near_sum.at[s, o, pl.ds((6, 10)[i], 4)]
        else:
            src = near_sum.at[s, o, pl.ds((4, 14)[i], 2)]
        return remote(
            src,
            (land1, last1, land2, last2)[k].at[s, o, i],
            rs_s.at[s, at],
            rs_r.at[s, at],
            devs[o][k // 2](dirs[i]),
        )

    def phase0(s):
        def tile(g, carry):
            products(s, g)
            return carry

        lax.fori_loop(0, QUARTERS, tile, 0)
        for o, i in both:
            rs_copy(s, o, 0, i).start()

    def phase1(s):
        @pl.when(s < EARLY)
        def _():
            def arrived(j, carry):
                for o, i in both:
                    quarter_copy(s, j, order(j), o, i).wait()
                return carry

            lax.fori_loop(0, QUARTERS, arrived, 0)

        @pl.when(s >= EARLY)
        def _():
            for o, i in both:
                rs_copy(s, o, 0, i).wait()

        for o, i in both:
            first, size = near1[i]
            part[s, o, first : first + size] += land1[s, o, i, 2 - 2 * i : 4 - 2 * i]
            rs_copy(s, o, 1, i).start()

    def phase2(s):
        for o in range(2):
            for i in range(2):
                rs_copy(s, o, 1, i).wait()
            for i in range(2):
                res = added(
                    part[s, o, 2 * i : 2 * i + 2],
                    last1[s, o, i],
                    land1[s, o, 1 - i, 2 - 2 * i : 4 - 2 * i],
                ).astype(BF16)
                near_sum[s, o, 8 * i : 8 * i + 8] = res.reshape(2 * QUARTERS, QUARTER, WIDE)
            for i in range(2):
                rs_copy(s, o, 2, i).start()

    def phase3(s):
        for o, i in both:
            rs_copy(s, o, 2, i).wait()
            first = (4, 14)[i]
            near_sum[s, o, first : first + 2] += land2[s, o, i, 2 - 2 * i : 4 - 2 * i]
            rs_copy(s, o, 3, i).start()

    def attend(left, right):
        seg_row = seg[...].astype(F32)
        key_at = lax.broadcasted_iota(jnp.int32, (ROWS, TOKENS), 1)
        row_at = lax.broadcasted_iota(jnp.int32, (ROWS, TOKENS), 0)
        row_at = row_at + (TOKENS // QUARTERS - QUARTER) * (row_at // QUARTER) + hid * QUARTER
        own = jnp.sum(jnp.where(key_at == row_at, seg_row, 0.0), 1, keepdims=True)
        allowed = (key_at <= row_at) & (seg_row == own)
        keys = kv_all[:, :, 0:HEAD].reshape(TOKENS, HEAD)
        vals = kv_all[:, :, HEAD : 2 * HEAD].reshape(TOKENS, HEAD)
        cosine, sine = turn[0, 0] * HEAD**-0.5, turn[0, 1] * HEAD**-0.5
        groups = [v[:, k * 128 : (k + 1) * 128] for v in (left, right) for k in range(3)]
        for h in range(3):
            a, b = groups[2 * h], groups[2 * h + 1]
            heads[h, :, 0:128] = (a * cosine - b * sine).astype(BF16)
            heads[h, :, 128:256] = (a * sine + b * cosine).astype(BF16)

        def head(h, carry):
            scores = lax.dot_general(
                heads[h], keys, (((1,), (1,)), ((), ())), preferred_element_type=F32
            )
            expos = jnp.where(allowed, jnp.exp(scores), 0.0)
            probs = (expos / jnp.sum(expos, 1, keepdims=True)).astype(BF16)
            heads[h] = jnp.dot(probs, vals, preferred_element_type=F32).astype(BF16)
            return carry

        lax.fori_loop(0, 3, head, 0)
        left = jnp.concatenate([heads[0], heads[1, :, 0:128]], 1)
        right = jnp.concatenate([heads[1, :, 128:256], heads[2]], 1)
        return left, right

    def put(u, block):
        for o in range(2):
            mixed[u // 2, o, 0, 0, u % 2] = block[o * HALF : (o + 1) * HALF]

    def gather_copy(u, o, k, i):
        d = dirs[i]
        away, near = (3, 1)[i], (3, 1)[i]
        dev = devs[o][k // 2](d)
        pair = mixed.at[u // 2, o]
        which = u % 2
        if k == 0:
            src, dst = pair.at[0, 0, which], pair.at[0, away, which]
        elif k == 1:
            rows = pl.ds(i * QUARTER, QUARTER)
            src, dst = pair.at[0, near, which, rows], pair.at[0, 2, which, rows]
        elif k == 2:
            src, dst = pair.at[0, :, which], pair.at[away, :, which]
        else:
            cut = pl.ds(2 * i, 2)
            src, dst = pair.at[near, cut, which], pair.at[2, cut, which]
        at = o * 8 + k * 2 + i
        return remote(src, dst, ag_s.at[u, at], ag_r.at[u, at], dev)

    def by_units(s, fn):
        def unit(u, carry):
            fn(u)
            return carry

        lax.fori_loop(jnp.where(s == 0, 0, s + 1), s + 2, unit, 0)

    def gather_first(u):
        for o, i in both:
            gather_copy(u, o, 0, i).start()

    def phase4(s):
        sums = []
        for o in range(2):
            for i in range(2):
                rs_copy(s, o, 3, i).wait()
            sums.append(
                jnp.concatenate(
                    [
                        added(
                            near_sum[s, o, 2 * i : 2 * i + 2],
                            last2[s, o, i],
                            land2[s, o, 1 - i, 2 - 2 * i : 4 - 2 * i],
                        ).reshape(HALF, WIDE)
                        for i in range(2)
                    ],
                    0,
                )
            )

        @pl.when(s == 0)
        def _():
            left, right = attend(*sums)
            put(0, left)
            put(1, right)

        @pl.when(s > 0)
        def _():
            gate, up = sums
            put(s + 1, (gate / (1.0 + jnp.exp(-gate)) * up).astype(BF16))

        by_units(s, gather_first)

    def phase5(u):
        for o, i in both:
            gather_copy(u, o, 0, i).wait()
            gather_copy(u, o, 1, i).start()

    def phase6(u):
        for o in range(2):
            for i in range(2):
                gather_copy(u, o, 1, i).wait()
            for i in range(2):
                gather_copy(u, o, 2, i).start()

    def phase7(u):
        for o, i in both:
            gather_copy(u, o, 2, i).wait()
            gather_copy(u, o, 3, i).start()

    def accumulate(u):
        def tile(k, carry):
            o, p = k // 2, k % 2
            rows = mixed[u // 2, o, pl.ds(2 * p, 2), :, u % 2].reshape(2 * SIDE * HALF, WIDE)
            at = pl.ds(pl.multiple_of(p * 256, 256), 256)
            total[o, at] += jnp.dot(rows, w_back[u], preferred_element_type=F32)
            return carry

        lax.fori_loop(0, 4, tile, 0)

    def phase8(u):
        for o, i in both:
            gather_copy(u, o, 3, i).wait()
        accumulate(u)

    def slot(t, carry):
        pl.when((t >= EARLY) & (t < STEPS))(lambda: phase0(t))
        for k, fn in ((2, phase1), (4, phase2), (5, phase3)):
            s = t - k
            pl.when((s >= 0) & (s < STEPS))(lambda fn=fn, s=s: fn(s))

        for j in range(1, 5):

            @pl.when(t == j + 1)
            def _(j=j):
                z_step(kv_all, zk, j)
                if j == 4:
                    sib_wait(kv_all, zk, 0, 1, -1, 2, -2, 3, -3, 4)

        s4 = t - 6
        pl.when((s4 >= 0) & (s4 < STEPS))(lambda: phase4(s4))

        for k, fn in ((7, phase5), (8, phase6), (9, phase7), (10, phase8)):
            s = t - k

            @pl.when((s >= 0) & (s < STEPS))
            def _(fn=fn, s=s):
                by_units(s, fn)

        return carry

    lax.fori_loop(2, STEPS + 10, slot, 0)

    offsets = (4, 3, -3, 2, -2, 1, -1, 0)

    def some_rows(block, k):
        g = block // SIDE
        o = g // 2
        px = mod4(block % SIDE - x)
        place = jnp.where(o == core, rel_y[k] * SIDE + px, px * SIDE + rel_y[k])
        first = pl.multiple_of(place * HALF + (g % 2) * QUARTER, QUARTER)
        return total[o, pl.ds(first, QUARTER)]

    def span(k):
        return slice(k * QUARTER, (k + 1) * QUARTER)

    def sib_sum(k):
        at = mod8(z + offsets[k])
        return remote(sib_out.at[at], sib_in.at[at], zr_s.at[k], zr_r.at[k], sibling)

    def sib_send(*which):
        for k in which:
            at = mod8(z + offsets[k])
            for q in range(4):
                sib_out[at, span(q)] = some_rows(at * 2 + 1 - core, q).astype(BF16)
            sib_sum(k).start()

    sib_send(0, 1, 2)

    def chip_sum(k, q):
        at = mod8(z + offsets[k])
        return some_rows(at * 2 + core, q) + sib_in[at, span(q)].astype(F32)

    def ring_copy(j, i, q):
        at = 8 + (j * 2 + i) * 4 + q
        return remote(
            ring_out.at[j, i, q], ring_in.at[j, i, q], zr_s.at[at], zr_r.at[at], dev_z(dirs[i])
        )

    sib_sum(0).wait()
    for q in range(2):
        for i in range(2):
            ring_out[0, i, 2 * i + q] = chip_sum(0, 2 * i + q).astype(BF16)
            ring_copy(0, i, 2 * i + q).start()
    sib_send(3, 4)
    for j in (1, 2, 3):
        for i in range(2):
            sib_sum(2 * j - 1 + i).wait()
        for turn_of in range(4):
            for i in range(2):
                q = (2 * (1 - i) + turn_of) % 4
                here = chip_sum(2 * j - 1 + i, q)
                if j > 1 or q // 2 == i:
                    ring_copy(j - 1, i, q).wait()
                    here += ring_in[j - 1, i, q].astype(F32)
                ring_out[j, i, q] = here.astype(BF16)
                ring_copy(j, i, q).start()
        if j < 3:
            sib_send(*((5, 6), (7,))[j - 1])
    sib_sum(7).wait()
    for q in (2, 0, 3, 1):
        here = chip_sum(7, q) + act[span(q)].astype(F32)
        for i in range(2):
            ring_copy(3, i, q).wait()
            here += ring_in[3, i, q].astype(F32)
        out[span(q)] = here.astype(BF16)


def per_device(activations, ln_gain, segments, w_query, w_key_value, w_gate, w_up, w_out, w_down):
    vmem = pl.BlockSpec(memory_space=pltpu.VMEM)
    anywhere = pl.BlockSpec(memory_space=pl.ANY)
    dma = pltpu.SemaphoreType.DMA
    scratch = [
        pltpu.VMEM((STEPS, FEATS, 2 * WIDE), BF16),
        pltpu.VMEM((UNITS, WIDE, FEATS), BF16),
        pltpu.VMEM((FEATS, 512), BF16),
        pltpu.VMEM((2, 2, ROWS, 128), F32),
        pltpu.VMEM((2, 8, 128), F32),
        pltpu.VMEM((2, 3, 8, 128), F32),
        pltpu.VMEM((4, 8, 128), F32),
        pltpu.VMEM((RING, 2, 8, 128), F32),
        pltpu.VMEM((GROUP, ROWS, FEATS), BF16),
        pltpu.VMEM((GROUP, ROWS, FEATS), BF16),
        pltpu.VMEM((4, ROWS, 128), BF16),
        pltpu.VMEM((2, 3, ROWS, 128), BF16),
        pltpu.VMEM((ROWS, 128), BF16),
        pltpu.VMEM((4, ROWS, 128), BF16),
        pltpu.VMEM((3, ROWS, HEAD), BF16),
        pltpu.VMEM((GROUP, ROWS, 512), BF16),
        pltpu.VMEM((STEPS, 2, GROUP, QUARTERS, QUARTER, WIDE), BF16),
        pltpu.VMEM((STEPS, 2, 2, 4, QUARTERS, QUARTER, WIDE), BF16),
        pltpu.VMEM((STEPS, 2, 2, 2, QUARTERS, QUARTER, WIDE), BF16),
        pltpu.VMEM((STEPS, 2, SIDE * QUARTERS, QUARTER, WIDE), BF16),
        pltpu.VMEM((STEPS, 2, 2, QUARTERS, QUARTER, WIDE), BF16),
        pltpu.VMEM((STEPS, 2, 2, 2, QUARTER, WIDE), BF16),
        pltpu.VMEM((UNITS // 2, 2, SIDE, SIDE, 2, HALF, WIDE), BF16),
        pltpu.VMEM((2, GROUP * HALF, FEATS), F32),
        pltpu.VMEM((RING, ROWS, FEATS), BF16),
        pltpu.VMEM((RING, ROWS, FEATS), BF16),
        pltpu.VMEM((4, 2, 4, QUARTER, FEATS), BF16),
        pltpu.VMEM((4, 2, 4, QUARTER, FEATS), BF16),
        dma((STEPS, 2)),
        dma((UNITS,)),
        dma((11,)),
        dma((7, 3)),
        dma((7, 3)),
        dma((8, 2)),
        dma((8, 2)),
        dma((5, 2)),
        dma((5, 2)),
        dma((EARLY * QUARTERS, 4)),
        dma((EARLY * QUARTERS, 4)),
        dma((8, 2)),
        dma((8, 2)),
        dma((STEPS, 16)),
        dma((STEPS, 16)),
        dma((UNITS, 16)),
        dma((UNITS, 16)),
        dma((40,)),
        dma((40,)),
    ]
    return pl.pallas_call(
        block_kernel,
        out_shape=jax.ShapeDtypeStruct((ROWS, FEATS), BF16),
        in_specs=[vmem, vmem, vmem] + [anywhere] * 7,
        out_specs=vmem,
        scratch_shapes=scratch,
        compiler_params=pltpu.CompilerParams(
            collective_id=0, has_side_effects=True, vmem_limit_bytes=54784 * 1024
        ),
    )(
        activations,
        ln_gain,
        segments.reshape(1, TOKENS),
        jnp.asarray(tables()),
        w_query,
        w_key_value,
        w_gate,
        w_up,
        w_out,
        w_down,
    )


def solution(mesh):
    placed = (
        P("ffn", "hid"),
        P("hid"),
        P(),
        P("hid", "ffn"),
        P("hid", None),
        P("hid", "ffn"),
        P("hid", "ffn"),
        P("ffn", "hid"),
        P("ffn", "hid"),
    )
    return jax.shard_map(
        per_device, mesh=mesh, in_specs=placed, out_specs=P("ffn", "hid"), check_vma=False
    )
```

```python
import jax
import jax.numpy as jnp
import numpy as np
from jax import lax
from jax.experimental import pallas as pl
from jax.experimental.pallas import tpu as pltpu
from jax.sharding import PartitionSpec as P

D = 10240
HEAD = 256
TOKENS = 1024
EPSILON = 1e-06

SIDE = 4
RING = 8
GROUP = SIDE * SIDE
ROWS = TOKENS // GROUP
FEATS = D // GROUP
WIDE = 384
STEPS = 7
EARLY = 3
UNITS = 8
HALF = ROWS // 2
QUARTERS = 4
QUARTER = ROWS // 4
F32 = jnp.float32
BF16 = jnp.bfloat16


def tables():
    half = HEAD // 2
    frequency = np.float32(10000.0) ** (-np.arange(half, dtype=np.float32) / np.float32(half))
    angles = np.arange(TOKENS, dtype=np.float32)[:, None] * frequency[None, :].astype(np.float32)
    wide = angles.astype(np.float64)
    return np.stack([np.cos(wide), np.sin(wide)]).astype(np.float32)


def block_kernel(
    act_far,
    gain_far,
    seg_far,
    table,
    w_query,
    w_pairs,
    w_gate,
    w_up,
    w_out,
    w_down,
    out,
    act,
    gain,
    seg,
    w_in,
    w_back,
    w_kv,
    turn,
    stat,
    stat_in,
    stat_other,
    stat_all,
    raw_all,
    rows_all,
    pair_part,
    pair_in,
    pair_sum,
    pair_all,
    heads,
    kv_all,
    part,
    land1,
    last1,
    near_sum,
    land2,
    last2,
    mixed,
    total,
    sib_out,
    sib_in,
    ring_out,
    ring_in,
    w_sem,
    wb_sem,
    m_sem,
    small_s,
    small_r,
    zx_s,
    zx_r,
    zt_s,
    zt_r,
    rq_s,
    rq_r,
    zk_s,
    zk_r,
    rs_s,
    rs_r,
    ag_s,
    ag_r,
    zr_s,
    zr_r,
):
    own_copies = [
        pltpu.make_async_copy(far, near, m_sem.at[11 + k])
        for k, (far, near) in enumerate(((act_far, act), (gain_far, gain), (seg_far, seg)))
    ]
    for copy in own_copies:
        copy.start(priority=1)
    hid = lax.axis_index("hid")
    ffn = lax.axis_index("ffn")
    x, y = hid // SIDE, hid % SIDE
    z, core = ffn // 2, ffn % 2

    def mod4(v):
        return (v + SIDE) % SIDE

    def mod8(v):
        return (v + RING) % RING

    ids_x = {d: mod4(x + d) * SIDE + y for d in (1, 2, 3)}
    ids_y = {d: x * SIDE + mod4(y + d) for d in (1, 2, 3)}
    ids_z = {d: mod8(z + d) * 2 + core for d in (1, -1)}

    def dev_x(d):
        return (ids_x[d % SIDE], ffn)

    def dev_y(d):
        return (ids_y[d % SIDE], ffn)

    def dev_z(d):
        return (hid, ids_z[d])

    other = z * 2 + 1 - core
    sibling = (hid, other)
    dirs = (1, -1)

    ids_one = {d: jnp.where(core == 0, ids_x[d], ids_y[d]) for d in (1, 3)}
    ids_two = {d: jnp.where(core == 0, ids_y[d], ids_x[d]) for d in (1, 3)}

    def dev_one(d):
        return (ids_one[d % SIDE], ffn)

    def dev_two(d):
        return (ids_two[d % SIDE], ffn)

    devs = ((dev_one, dev_two), (dev_two, dev_one))

    barrier = pltpu.get_barrier_semaphore()
    partners = [dev_x(d) for d in (1, 2, 3)] + [dev_y(d) for d in (1, 2, 3)]
    partners += [(ids_y[d], other) for d in (1, 2, 3)]
    partners += [dev_z(1), dev_z(-1), sibling]
    for dev in partners:
        pl.semaphore_signal(barrier, inc=1, device_id=dev, device_id_type=pl.DeviceIdType.MESH)

    def remote(src, dst, ssem, rsem, dev):
        return pltpu.make_async_remote_copy(
            src_ref=src,
            dst_ref=dst,
            send_sem=ssem,
            recv_sem=rsem,
            device_id=dev,
            device_id_type=pl.DeviceIdType.MESH,
        )

    def w_copy(s, o):
        if s == 0:
            src = w_query.at[:, pl.ds(o * WIDE, WIDE)]
        else:
            src = (w_gate, w_up)[o].at[:, pl.ds((s - 1) * WIDE, WIDE)]
        return pltpu.make_async_copy(src, w_in.at[s, :, pl.ds(o * WIDE, WIDE)], w_sem.at[s, o])

    def wb_copy(u):
        if u < 2:
            src = w_out.at[pl.ds(u * WIDE, WIDE)]
        else:
            src = w_down.at[pl.ds((u - 2) * WIDE, WIDE)]
        return pltpu.make_async_copy(src, w_back.at[u], wb_sem.at[u])

    def turn_copies(i):
        copies = [
            pltpu.make_async_copy(
                table.at[i, pl.ds(pl.multiple_of(ffn * ROWS, ROWS), ROWS)],
                turn.at[1, i],
                m_sem.at[1 + 5 * i],
            )
        ]
        for g in range(QUARTERS):
            first = pl.multiple_of(g * (TOKENS // QUARTERS) + hid * QUARTER, QUARTER)
            copies.append(
                pltpu.make_async_copy(
                    table.at[i, pl.ds(first, QUARTER)],
                    turn.at[0, i, pl.ds(g * QUARTER, QUARTER)],
                    m_sem.at[2 + 5 * i + g],
                )
            )
        return copies

    kv_copy = pltpu.make_async_copy(w_pairs, w_kv, m_sem.at[0])

    kv_copy.start(priority=1)
    for s in range(EARLY):
        for o in range(2):
            w_copy(s, o).start(priority=1)
    for copy in own_copies:
        copy.wait()
    pl.semaphore_wait(barrier, len(partners))

    def stat_copy(a, d):
        return remote(
            stat.at[a], stat_in.at[a, d - 1], small_s.at[a, d - 1], small_r.at[a, d - 1],
            (dev_x, dev_y)[a](d),
        )

    def other_copy(d):
        return remote(
            stat.at[1], stat_other.at[d], small_s.at[5 + d // 3, d % 3], small_r.at[5 + d // 3, d % 3],
            (ids_y[d], other) if d else sibling,
        )

    def pair_copy(k, d):
        if k == 0:
            src, dst, dev = pair_part.at[mod4(x + d)], pair_in.at[0, d - 1], dev_x(d)
        elif k == 1:
            src, dst, dev = pair_sum, pair_in.at[1, d - 1], dev_y(d)
        else:
            src, dst, dev = pair_all.at[x], pair_all.at[x], dev_x(d)
        return remote(src, dst, small_s.at[2 + k, d - 1], small_r.at[2 + k, d - 1], dev)

    def each(fn, k, what):
        for d in (1, 2, 3):
            getattr(fn(k, d), what)()

    def z_copy(buf, sems, j, i):
        d = dirs[i]
        block = mod8(z - (j - 1) * d) * 2 + core
        ref = buf.at[block] if j < 4 else buf.at[block, pl.ds(i * HALF, HALF)]
        return remote(ref, ref, sems[0].at[j - 1, i], sems[1].at[j - 1, i], dev_z(d))

    def sib_copy(buf, sems, off):
        ref = buf.at[mod8(z + off) * 2 + core]
        row = 4 + (off + 3) // 2
        col = (off + 3) % 2
        return remote(ref, ref, sems[0].at[row, col], sems[1].at[row, col], sibling)

    def z_start(buf, sems):
        for i in range(2):
            z_copy(buf, sems, 1, i).start()
        sib_copy(buf, sems, 0).start()

    def z_step(buf, sems, j):
        if j < 4:
            for i in range(2):
                z_copy(buf, sems, j, i).wait()
                z_copy(buf, sems, j + 1, i).start()
                sib_copy(buf, sems, -j * dirs[i]).start()
        else:
            for i in range(2):
                z_copy(buf, sems, j, i).wait()
            sib_copy(buf, sems, 4).start()

    def sib_wait(buf, sems, *offs):
        for off in offs:
            sib_copy(buf, sems, off).wait()

    def stat_z(j, i):
        ref = stat_all.at[mod8(z - (j - 1) * dirs[i])]
        return remote(ref, ref, zt_s.at[j, i], zt_r.at[j, i], dev_z(dirs[i]))

    def stat_step(j):
        for i in range(2):
            if (j, i) == (4, 1):
                continue
            stat_z(j, i).wait()
            if j < 3 + (i == 0):
                stat_z(j + 1, i).start()

    def added(first, *rest):
        res = first.astype(F32)
        for one in rest:
            res += one.astype(F32)
        return res

    def quarter_copy(s, j, g, o, i):
        at = o * 2 + i
        return remote(
            part.at[s, o, pl.ds((6, 10)[i], 4), g],
            land1.at[s, o, i, :, g],
            rq_s.at[s * QUARTERS + j, at],
            rq_r.at[s * QUARTERS + j, at],
            devs[o][0](dirs[i]),
        )

    both = [(o, i) for o in range(2) for i in range(2)]
    rel_x = [mod4(k - x) for k in range(SIDE)]
    rel_y = [mod4(k - y) for k in range(SIDE)]
    x_y = [rel_x[h // SIDE] * SIDE + rel_y[h % SIDE] for h in range(GROUP)]
    y_x = [rel_y[h % SIDE] * SIDE + rel_x[h // SIDE] for h in range(GROUP)]
    places = (
        [jnp.where(core == 0, a, b) for a, b in zip(x_y, y_x)],
        [jnp.where(core == 0, b, a) for a, b in zip(x_y, y_x)],
    )

    def products(s, g):
        rows = rows_all[pl.ds(g * QUARTERS, QUARTERS)].reshape(QUARTERS * ROWS, FEATS)
        res = jnp.dot(rows, w_in[s], preferred_element_type=F32).astype(BF16)
        for h in range(GROUP):
            block = res[h * QUARTER : (h + 1) * QUARTER]
            for o in range(2):
                part[s, o, places[o][h], g] = block[:, o * WIDE : (o + 1) * WIDE]

    eye = lax.broadcasted_iota(jnp.int32, (ROWS, 128), 0) == lax.broadcasted_iota(
        jnp.int32, (ROWS, 128), 1
    )
    line = lax.broadcasted_iota(jnp.int32, (8, 128), 0)

    def to_row(column):
        return jnp.sum(jnp.where(eye, column, 0.0), 0, keepdims=True)

    def to_column(row):
        return jnp.sum(jnp.where(eye, row, 0.0), 1, keepdims=True)

    def norm(rows, tile):
        mean, scale = to_column(tile[0:1]), to_column(tile[1:2])
        return ((rows.astype(F32) - mean) * scale * gain[...].reshape(1, FEATS)).astype(BF16)

    zx = (zx_s, zx_r)
    zk = (zk_s, zk_r)
    raw_all[ffn] = act[...]
    z_start(raw_all, zx)
    values = act[...].astype(F32)
    mean = jnp.mean(values, 1, keepdims=True)
    square = jnp.sum((values - mean) ** 2, 1, keepdims=True)
    mean, square = to_row(mean), to_row(square)
    def merge(count, tiles):
        means = [tile[0:1] for tile in tiles]
        squares = [tile[1:2] for tile in tiles]
        mean = (means[0] + means[1] + means[2] + means[3]) * 0.25
        square = squares[0] + squares[1] + squares[2] + squares[3]
        for one in means:
            square += count * (one - mean) ** 2
        return mean, square

    def finish(tiles):
        mean, square = merge(FEATS * SIDE, tiles)
        return jnp.where(line == 0, mean, lax.rsqrt(square * (1.0 / D) + EPSILON))

    stat[0] = jnp.where(line == 0, mean, square)
    each(stat_copy, 0, "start")
    total[...] = jnp.zeros_like(total)
    each(stat_copy, 0, "wait")
    mean, square = merge(FEATS, [stat[0]] + [stat_in[0, d] for d in range(3)])
    stat[1] = jnp.where(line == 0, mean, square)
    each(stat_copy, 1, "start")
    for d in range(SIDE):
        other_copy(d).start()
    z_step(raw_all, zx, 1)
    each(stat_copy, 1, "wait")
    for d in range(SIDE):
        other_copy(d).wait()
    stat_all[z, core] = finish([stat[1]] + [stat_in[1, d] for d in range(3)])
    stat_all[z, 1 - core] = finish([stat_other[d] for d in range(SIDE)])
    for i in range(2):
        stat_z(1, i).start()
    normed = norm(act[...], stat_all[z, core])
    kv_copy.wait()
    pairs = jnp.dot(normed, w_kv[...], preferred_element_type=F32).astype(BF16)
    for q in range(4):
        pair_part[q] = pairs[:, q * 128 : (q + 1) * 128]
    each(pair_copy, 0, "start")
    for s in range(EARLY):
        for o in range(2):
            w_copy(s, o).wait()

    pair = z // 2
    turned = 1 - 2 * (z % 2)
    def order(j):
        step = jnp.where(j == 3, 2, jnp.where(j == 0, 0, jnp.where(j == 1, -turned, turned)))
        return mod4(pair + step)

    def pair_add(own, a):
        return added(own, pair_in[a, 0], pair_in[a, 1], pair_in[a, 2]).astype(BF16)

    def early(j, carry):
        @pl.when(j == 0)
        def _():
            stat_step(1)
            sib_wait(raw_all, zx, 0, 1, -1)

        @pl.when(j == 1)
        def _():
            for s in range(EARLY, STEPS):
                for o in range(2):
                    w_copy(s, o).start(priority=1)
            each(pair_copy, 0, "wait")
            pair_sum[...] = pair_add(pair_part[x], 0)
            each(pair_copy, 1, "start")
            z_step(raw_all, zx, 3)
            stat_step(2)
            sib_wait(raw_all, zx, 2, -2)

        @pl.when(j == 2)
        def _():
            for i in range(2):
                for copy in turn_copies(i):
                    copy.start(priority=1)
            for u in range(UNITS):
                wb_copy(u).start(priority=1)
            each(pair_copy, 1, "wait")
            pair_all[x] = pair_add(pair_sum[...], 1)
            each(pair_copy, 2, "start")
            z_step(raw_all, zx, 4)
            stat_step(3)
            sib_wait(raw_all, zx, 3, -3)

        @pl.when(j == 3)
        def _():
            stat_step(4)
            sib_wait(raw_all, zx, 4)

        g = order(j)

        def one(k, c):
            rows_all[g * 4 + k] = norm(raw_all[g * 4 + k], stat_all[g * 2 + k // 2, k % 2])
            return c

        lax.fori_loop(0, QUARTERS, one, 0)

        def step(s, c):
            products(s, g)
            for o, i in both:
                quarter_copy(s, j, g, o, i).start()
            pl.when((j == 0) & (s == 0))(lambda: z_step(raw_all, zx, 2))
            return c

        lax.fori_loop(0, EARLY, step, 0)
        return carry

    lax.fori_loop(0, QUARTERS, early, 0)
    each(pair_copy, 2, "wait")
    for i in range(2):
        for copy in turn_copies(i):
            copy.wait()
    first, second = pair_all[0].astype(F32), pair_all[1].astype(F32)
    kv_all[ffn, :, 0:128] = (first * turn[1, 0] - second * turn[1, 1]).astype(BF16)
    kv_all[ffn, :, 128:256] = (first * turn[1, 1] + second * turn[1, 0]).astype(BF16)
    kv_all[ffn, :, 256:384] = pair_all[2]
    kv_all[ffn, :, 384:512] = pair_all[3]
    z_start(kv_all, zk)

    for s in range(EARLY, STEPS):
        for o in range(2):
            w_copy(s, o).wait()
    for u in range(UNITS):
        wb_copy(u).wait()

    far1 = ((6, 4), (10, 4))
    near1 = ((4, 2), (14, 2))

    def rs_copy(s, o, k, i):
        at = o * 8 + k * 2 + i
        if k < 2:
            first, size = (far1, near1)[k][i]
            src = part.at[s, o, pl.ds(first, size)]
        elif k == 2:
            src = near_sum.at[s, o, pl.ds((6, 10)[i], 4)]
        else:
            src = near_sum.at[s, o, pl.ds((4, 14)[i], 2)]
        return remote(
            src,
            (land1, last1, land2, last2)[k].at[s, o, i],
            rs_s.at[s, at],
            rs_r.at[s, at],
            devs[o][k // 2](dirs[i]),
        )

    def phase0(s):
        def tile(g, carry):
            products(s, g)
            return carry

        lax.fori_loop(0, QUARTERS, tile, 0)
        for o, i in both:
            rs_copy(s, o, 0, i).start()

    def phase1(s):
        @pl.when(s < EARLY)
        def _():
            def arrived(j, carry):
                for o, i in both:
                    quarter_copy(s, j, order(j), o, i).wait()
                return carry

            lax.fori_loop(0, QUARTERS, arrived, 0)

        @pl.when(s >= EARLY)
        def _():
            for o, i in both:
                rs_copy(s, o, 0, i).wait()

        for o, i in both:
            first, size = near1[i]
            part[s, o, first : first + size] += land1[s, o, i, 2 - 2 * i : 4 - 2 * i]
            rs_copy(s, o, 1, i).start()

    def phase2(s):
        for o in range(2):
            for i in range(2):
                rs_copy(s, o, 1, i).wait()
            for i in range(2):
                res = added(
                    part[s, o, 2 * i : 2 * i + 2],
                    last1[s, o, i],
                    land1[s, o, 1 - i, 2 - 2 * i : 4 - 2 * i],
                ).astype(BF16)
                near_sum[s, o, 8 * i : 8 * i + 8] = res.reshape(2 * QUARTERS, QUARTER, WIDE)
            for i in range(2):
                rs_copy(s, o, 2, i).start()

    def phase3(s):
        for o, i in both:
            rs_copy(s, o, 2, i).wait()
            first = (4, 14)[i]
            near_sum[s, o, first : first + 2] += land2[s, o, i, 2 - 2 * i : 4 - 2 * i]
            rs_copy(s, o, 3, i).start()

    def attend(left, right):
        seg_row = seg[...].astype(F32)
        key_at = lax.broadcasted_iota(jnp.int32, (ROWS, TOKENS), 1)
        row_at = lax.broadcasted_iota(jnp.int32, (ROWS, TOKENS), 0)
        row_at = row_at + (TOKENS // QUARTERS - QUARTER) * (row_at // QUARTER) + hid * QUARTER
        own = jnp.sum(jnp.where(key_at == row_at, seg_row, 0.0), 1, keepdims=True)
        allowed = (key_at <= row_at) & (seg_row == own)
        keys = kv_all[:, :, 0:HEAD].reshape(TOKENS, HEAD)
        vals = kv_all[:, :, HEAD : 2 * HEAD].reshape(TOKENS, HEAD)
        cosine, sine = turn[0, 0] * HEAD**-0.5, turn[0, 1] * HEAD**-0.5
        groups = [v[:, k * 128 : (k + 1) * 128] for v in (left, right) for k in range(3)]
        for h in range(3):
            a, b = groups[2 * h], groups[2 * h + 1]
            heads[h, :, 0:128] = (a * cosine - b * sine).astype(BF16)
            heads[h, :, 128:256] = (a * sine + b * cosine).astype(BF16)

        def head(h, carry):
            scores = lax.dot_general(
                heads[h], keys, (((1,), (1,)), ((), ())), preferred_element_type=F32
            )
            expos = jnp.where(allowed, jnp.exp(scores), 0.0)
            probs = (expos / jnp.sum(expos, 1, keepdims=True)).astype(BF16)
            heads[h] = jnp.dot(probs, vals, preferred_element_type=F32).astype(BF16)
            return carry

        lax.fori_loop(0, 3, head, 0)
        left = jnp.concatenate([heads[0], heads[1, :, 0:128]], 1)
        right = jnp.concatenate([heads[1, :, 128:256], heads[2]], 1)
        return left, right

    def put(u, block):
        for o in range(2):
            mixed[u // 2, o, 0, 0, u % 2] = block[o * HALF : (o + 1) * HALF]

    def gather_copy(u, o, k, i):
        d = dirs[i]
        away, near = (3, 1)[i], (3, 1)[i]
        dev = devs[o][k // 2](d)
        pair = mixed.at[u // 2, o]
        which = u % 2
        if k == 0:
            src, dst = pair.at[0, 0, which], pair.at[0, away, which]
        elif k == 1:
            rows = pl.ds(i * QUARTER, QUARTER)
            src, dst = pair.at[0, near, which, rows], pair.at[0, 2, which, rows]
        elif k == 2:
            src, dst = pair.at[0, :, which], pair.at[away, :, which]
        else:
            cut = pl.ds(2 * i, 2)
            src, dst = pair.at[near, cut, which], pair.at[2, cut, which]
        at = o * 8 + k * 2 + i
        return remote(src, dst, ag_s.at[u, at], ag_r.at[u, at], dev)

    def by_units(s, fn):
        def unit(u, carry):
            fn(u)
            return carry

        lax.fori_loop(jnp.where(s == 0, 0, s + 1), s + 2, unit, 0)

    def gather_first(u):
        for o, i in both:
            gather_copy(u, o, 0, i).start()

    def phase4(s):
        sums = []
        for o in range(2):
            for i in range(2):
                rs_copy(s, o, 3, i).wait()
            sums.append(
                jnp.concatenate(
                    [
                        added(
                            near_sum[s, o, 2 * i : 2 * i + 2],
                            last2[s, o, i],
                            land2[s, o, 1 - i, 2 - 2 * i : 4 - 2 * i],
                        ).reshape(HALF, WIDE)
                        for i in range(2)
                    ],
                    0,
                )
            )

        @pl.when(s == 0)
        def _():
            left, right = attend(*sums)
            put(0, left)
            put(1, right)

        @pl.when(s > 0)
        def _():
            gate, up = sums
            put(s + 1, (gate / (1.0 + jnp.exp(-gate)) * up).astype(BF16))

        by_units(s, gather_first)

    def phase5(u):
        for o, i in both:
            gather_copy(u, o, 0, i).wait()
            gather_copy(u, o, 1, i).start()

    def phase6(u):
        for o in range(2):
            for i in range(2):
                gather_copy(u, o, 1, i).wait()
            for i in range(2):
                gather_copy(u, o, 2, i).start()

    def phase7(u):
        for o, i in both:
            gather_copy(u, o, 2, i).wait()
            gather_copy(u, o, 3, i).start()

    def accumulate(u):
        def tile(k, carry):
            o, p = k // 2, k % 2
            rows = mixed[u // 2, o, pl.ds(2 * p, 2), :, u % 2].reshape(2 * SIDE * HALF, WIDE)
            at = pl.ds(pl.multiple_of(p * 256, 256), 256)
            total[o, at] += jnp.dot(rows, w_back[u], preferred_element_type=F32)
            return carry

        lax.fori_loop(0, 4, tile, 0)

    def phase8(u):
        for o, i in both:
            gather_copy(u, o, 3, i).wait()
        accumulate(u)

    def slot(t, carry):
        pl.when((t >= EARLY) & (t < STEPS))(lambda: phase0(t))
        for k, fn in ((2, phase1), (4, phase2), (5, phase3)):
            s = t - k
            pl.when((s >= 0) & (s < STEPS))(lambda fn=fn, s=s: fn(s))

        for j in range(1, 5):

            @pl.when(t == j + 1)
            def _(j=j):
                z_step(kv_all, zk, j)
                if j == 4:
                    sib_wait(kv_all, zk, 0, 1, -1, 2, -2, 3, -3, 4)

        s4 = t - 6
        pl.when((s4 >= 0) & (s4 < STEPS))(lambda: phase4(s4))

        for k, fn in ((7, phase5), (8, phase6), (9, phase7), (10, phase8)):
            s = t - k

            @pl.when((s >= 0) & (s < STEPS))
            def _(fn=fn, s=s):
                by_units(s, fn)

        return carry

    lax.fori_loop(2, STEPS + 10, slot, 0)

    offsets = (4, 3, -3, 2, -2, 1, -1, 0)

    def some_rows(block, k):
        g = block // SIDE
        o = g // 2
        px = mod4(block % SIDE - x)
        place = jnp.where(o == core, rel_y[k] * SIDE + px, px * SIDE + rel_y[k])
        first = pl.multiple_of(place * HALF + (g % 2) * QUARTER, QUARTER)
        return total[o, pl.ds(first, QUARTER)]

    def span(k):
        return slice(k * QUARTER, (k + 1) * QUARTER)

    def sib_sum(k):
        at = mod8(z + offsets[k])
        return remote(sib_out.at[at], sib_in.at[at], zr_s.at[k], zr_r.at[k], sibling)

    def sib_send(*which):
        for k in which:
            at = mod8(z + offsets[k])
            for q in range(4):
                sib_out[at, span(q)] = some_rows(at * 2 + 1 - core, q).astype(BF16)
            sib_sum(k).start()

    sib_send(0, 1, 2)

    def chip_sum(k, q):
        at = mod8(z + offsets[k])
        return some_rows(at * 2 + core, q) + sib_in[at, span(q)].astype(F32)

    def ring_copy(j, i, q):
        at = 8 + (j * 2 + i) * 4 + q
        return remote(
            ring_out.at[j, i, q], ring_in.at[j, i, q], zr_s.at[at], zr_r.at[at], dev_z(dirs[i])
        )

    sib_sum(0).wait()
    for q in range(2):
        for i in range(2):
            ring_out[0, i, 2 * i + q] = chip_sum(0, 2 * i + q).astype(BF16)
            ring_copy(0, i, 2 * i + q).start()
    sib_send(3, 4)
    for j in (1, 2, 3):
        for i in range(2):
            sib_sum(2 * j - 1 + i).wait()
        for turn_of in range(4):
            for i in range(2):
                q = (2 * (1 - i) + turn_of) % 4
                here = chip_sum(2 * j - 1 + i, q)
                if j > 1 or q // 2 == i:
                    ring_copy(j - 1, i, q).wait()
                    here += ring_in[j - 1, i, q].astype(F32)
                ring_out[j, i, q] = here.astype(BF16)
                ring_copy(j, i, q).start()
        if j < 3:
            sib_send(*((5, 6), (7,))[j - 1])
    sib_sum(7).wait()
    for q in (2, 0, 3, 1):
        here = chip_sum(7, q) + act[span(q)].astype(F32)
        for i in range(2):
            ring_copy(3, i, q).wait()
            here += ring_in[3, i, q].astype(F32)
        out[span(q)] = here.astype(BF16)


def per_device(activations, ln_gain, segments, w_query, w_key_value, w_gate, w_up, w_out, w_down):
    vmem = pl.BlockSpec(memory_space=pltpu.VMEM)
    far = pl.BlockSpec(memory_space=pltpu.HBM)
    dma = pltpu.SemaphoreType.DMA
    scratch = [
        pltpu.VMEM((ROWS, FEATS), BF16),
        pltpu.VMEM((FEATS,), F32),
        pltpu.VMEM((1, TOKENS), jnp.int32),
        pltpu.VMEM((STEPS, FEATS, 2 * WIDE), BF16),
        pltpu.VMEM((UNITS, WIDE, FEATS), BF16),
        pltpu.VMEM((FEATS, 512), BF16),
        pltpu.VMEM((2, 2, ROWS, 128), F32),
        pltpu.VMEM((2, 8, 128), F32),
        pltpu.VMEM((2, 3, 8, 128), F32),
        pltpu.VMEM((4, 8, 128), F32),
        pltpu.VMEM((RING, 2, 8, 128), F32),
        pltpu.VMEM((GROUP, ROWS, FEATS), BF16),
        pltpu.VMEM((GROUP, ROWS, FEATS), BF16),
        pltpu.VMEM((4, ROWS, 128), BF16),
        pltpu.VMEM((2, 3, ROWS, 128), BF16),
        pltpu.VMEM((ROWS, 128), BF16),
        pltpu.VMEM((4, ROWS, 128), BF16),
        pltpu.VMEM((3, ROWS, HEAD), BF16),
        pltpu.VMEM((GROUP, ROWS, 512), BF16),
        pltpu.VMEM((STEPS, 2, GROUP, QUARTERS, QUARTER, WIDE), BF16),
        pltpu.VMEM((STEPS, 2, 2, 4, QUARTERS, QUARTER, WIDE), BF16),
        pltpu.VMEM((STEPS, 2, 2, 2, QUARTERS, QUARTER, WIDE), BF16),
        pltpu.VMEM((STEPS, 2, SIDE * QUARTERS, QUARTER, WIDE), BF16),
        pltpu.VMEM((STEPS, 2, 2, QUARTERS, QUARTER, WIDE), BF16),
        pltpu.VMEM((STEPS, 2, 2, 2, QUARTER, WIDE), BF16),
        pltpu.VMEM((UNITS // 2, 2, SIDE, SIDE, 2, HALF, WIDE), BF16),
        pltpu.VMEM((2, GROUP * HALF, FEATS), F32),
        pltpu.VMEM((RING, ROWS, FEATS), BF16),
        pltpu.VMEM((RING, ROWS, FEATS), BF16),
        pltpu.VMEM((4, 2, 4, QUARTER, FEATS), BF16),
        pltpu.VMEM((4, 2, 4, QUARTER, FEATS), BF16),
        dma((STEPS, 2)),
        dma((UNITS,)),
        dma((14,)),
        dma((7, 3)),
        dma((7, 3)),
        dma((8, 2)),
        dma((8, 2)),
        dma((5, 2)),
        dma((5, 2)),
        dma((EARLY * QUARTERS, 4)),
        dma((EARLY * QUARTERS, 4)),
        dma((8, 2)),
        dma((8, 2)),
        dma((STEPS, 16)),
        dma((STEPS, 16)),
        dma((UNITS, 16)),
        dma((UNITS, 16)),
        dma((40,)),
        dma((40,)),
    ]
    return pl.pallas_call(
        block_kernel,
        out_shape=jax.ShapeDtypeStruct((ROWS, FEATS), BF16),
        in_specs=[far] * 10,
        out_specs=vmem,
        scratch_shapes=scratch,
        compiler_params=pltpu.CompilerParams(
            collective_id=0, has_side_effects=True, vmem_limit_bytes=54784 * 1024
        ),
    )(
        pltpu.with_memory_space_constraint(activations, pltpu.HBM),
        pltpu.with_memory_space_constraint(ln_gain, pltpu.HBM),
        pltpu.with_memory_space_constraint(segments.reshape(1, TOKENS), pltpu.HBM),
        jnp.asarray(tables()),
        w_query,
        w_key_value,
        w_gate,
        w_up,
        w_out,
        w_down,
    )


def solution(mesh):
    placed = (
        P("ffn", "hid"),
        P("hid"),
        P(),
        P("hid", "ffn"),
        P("hid", None),
        P("hid", "ffn"),
        P("hid", "ffn"),
        P("ffn", "hid"),
        P("ffn", "hid"),
    )
    return jax.shard_map(
        per_device, mesh=mesh, in_specs=placed, out_specs=P("ffn", "hid"), check_vma=False
    )
```

```python
import jax
import jax.numpy as jnp
import numpy as np
from jax import lax
from jax.experimental import pallas as pl
from jax.experimental.pallas import tpu as pltpu
from jax.sharding import PartitionSpec as P

D = 10240
HEAD = 256
TOKENS = 1024
EPSILON = 1e-06

SIDE = 4
RING = 8
GROUP = SIDE * SIDE
ROWS = TOKENS // GROUP
FEATS = D // GROUP
WIDE = 384
STEPS = 7
EARLY = 3
UNITS = 8
HALF = ROWS // 2
QUARTERS = 4
QUARTER = ROWS // 4
F32 = jnp.float32
BF16 = jnp.bfloat16


def tables():
    half = HEAD // 2
    frequency = np.float32(10000.0) ** (-np.arange(half, dtype=np.float32) / np.float32(half))
    angles = np.arange(TOKENS, dtype=np.float32)[:, None] * frequency[None, :].astype(np.float32)
    wide = angles.astype(np.float64)
    return np.stack([np.cos(wide), np.sin(wide)]).astype(np.float32)


def block_kernel(
    act_far,
    gain_far,
    seg_far,
    table,
    w_query,
    w_pairs,
    w_gate,
    w_up,
    w_out,
    w_down,
    out,
    act,
    gain,
    seg,
    w_in,
    w_back,
    w_kv,
    turn,
    stat,
    stat_in,
    stat_other,
    stat_all,
    raw_all,
    rows_all,
    pair_part,
    pair_in,
    pair_sum,
    pair_all,
    heads,
    kv_all,
    part,
    land1,
    last1,
    near_sum,
    land2,
    last2,
    mixed,
    total,
    sib_out,
    sib_in,
    ring_out,
    ring_in,
    w_sem,
    wb_sem,
    m_sem,
    small_s,
    small_r,
    zx_s,
    zx_r,
    zt_s,
    zt_r,
    rq_s,
    rq_r,
    zk_s,
    zk_r,
    rs_s,
    rs_r,
    ag_s,
    ag_r,
    zr_s,
    zr_r,
):
    own_copies = [
        pltpu.make_async_copy(far, near, m_sem.at[11 + k])
        for k, (far, near) in enumerate(((act_far, act), (gain_far, gain), (seg_far, seg)))
    ]
    for copy in own_copies:
        copy.start(priority=1)
    hid = lax.axis_index("hid")
    ffn = lax.axis_index("ffn")
    x, y = hid // SIDE, hid % SIDE
    z, core = ffn // 2, ffn % 2

    def mod4(v):
        return (v + SIDE) % SIDE

    def mod8(v):
        return (v + RING) % RING

    ids_x = {d: mod4(x + d) * SIDE + y for d in (1, 2, 3)}
    ids_y = {d: x * SIDE + mod4(y + d) for d in (1, 2, 3)}
    ids_z = {d: mod8(z + d) * 2 + core for d in (1, -1)}

    def dev_x(d):
        return (ids_x[d % SIDE], ffn)

    def dev_y(d):
        return (ids_y[d % SIDE], ffn)

    def dev_z(d):
        return (hid, ids_z[d])

    other = z * 2 + 1 - core
    sibling = (hid, other)
    dirs = (1, -1)

    ids_one = {d: jnp.where(core == 0, ids_x[d], ids_y[d]) for d in (1, 3)}
    ids_two = {d: jnp.where(core == 0, ids_y[d], ids_x[d]) for d in (1, 3)}

    def dev_one(d):
        return (ids_one[d % SIDE], ffn)

    def dev_two(d):
        return (ids_two[d % SIDE], ffn)

    devs = ((dev_one, dev_two), (dev_two, dev_one))

    barrier = pltpu.get_barrier_semaphore()
    partners = [dev_x(d) for d in (1, 2, 3)] + [dev_y(d) for d in (1, 2, 3)]
    partners += [(ids_y[d], other) for d in (1, 2, 3)]
    partners += [dev_z(1), dev_z(-1), sibling]
    for dev in partners:
        pl.semaphore_signal(barrier, inc=1, device_id=dev, device_id_type=pl.DeviceIdType.MESH)

    def remote(src, dst, ssem, rsem, dev):
        return pltpu.make_async_remote_copy(
            src_ref=src,
            dst_ref=dst,
            send_sem=ssem,
            recv_sem=rsem,
            device_id=dev,
            device_id_type=pl.DeviceIdType.MESH,
        )

    def w_copy(s, o):
        if s == 0:
            src = w_query.at[:, pl.ds(o * WIDE, WIDE)]
        else:
            src = (w_gate, w_up)[o].at[:, pl.ds((s - 1) * WIDE, WIDE)]
        return pltpu.make_async_copy(src, w_in.at[s, :, pl.ds(o * WIDE, WIDE)], w_sem.at[s, o])

    def wb_copy(u):
        if u < 2:
            src = w_out.at[pl.ds(u * WIDE, WIDE)]
        else:
            src = w_down.at[pl.ds((u - 2) * WIDE, WIDE)]
        return pltpu.make_async_copy(src, w_back.at[u], wb_sem.at[u])

    def turn_copies(i):
        copies = [
            pltpu.make_async_copy(
                table.at[i, pl.ds(pl.multiple_of(ffn * ROWS, ROWS), ROWS)],
                turn.at[1, i],
                m_sem.at[1 + 5 * i],
            )
        ]
        for g in range(QUARTERS):
            first = pl.multiple_of(g * (TOKENS // QUARTERS) + hid * QUARTER, QUARTER)
            copies.append(
                pltpu.make_async_copy(
                    table.at[i, pl.ds(first, QUARTER)],
                    turn.at[0, i, pl.ds(g * QUARTER, QUARTER)],
                    m_sem.at[2 + 5 * i + g],
                )
            )
        return copies

    kv_copy = pltpu.make_async_copy(w_pairs, w_kv, m_sem.at[0])

    kv_copy.start(priority=1)
    for s in range(EARLY):
        for o in range(2):
            w_copy(s, o).start(priority=1)
    for copy in own_copies:
        copy.wait()
    pl.semaphore_wait(barrier, len(partners))

    def stat_copy(a, d):
        return remote(
            stat.at[a], stat_in.at[a, d - 1], small_s.at[a, d - 1], small_r.at[a, d - 1],
            (dev_x, dev_y)[a](d),
        )

    def other_copy(d):
        return remote(
            stat.at[1], stat_other.at[d], small_s.at[5 + d // 3, d % 3], small_r.at[5 + d // 3, d % 3],
            (ids_y[d], other) if d else sibling,
        )

    def pair_copy(k, d):
        if k == 0:
            src, dst, dev = pair_part.at[mod4(x + d)], pair_in.at[0, d - 1], dev_x(d)
        elif k == 1:
            src, dst, dev = pair_sum, pair_in.at[1, d - 1], dev_y(d)
        else:
            src, dst, dev = pair_all.at[x], pair_all.at[x], dev_x(d)
        return remote(src, dst, small_s.at[2 + k, d - 1], small_r.at[2 + k, d - 1], dev)

    def each(fn, k, what):
        for d in (1, 2, 3):
            getattr(fn(k, d), what)()

    def z_copy(buf, sems, j, i):
        d = dirs[i]
        block = mod8(z - (j - 1) * d) * 2 + core
        ref = buf.at[block] if j < 4 else buf.at[block, pl.ds(i * HALF, HALF)]
        return remote(ref, ref, sems[0].at[j - 1, i], sems[1].at[j - 1, i], dev_z(d))

    def sib_copy(buf, sems, off):
        ref = buf.at[mod8(z + off) * 2 + core]
        row = 4 + (off + 3) // 2
        col = (off + 3) % 2
        return remote(ref, ref, sems[0].at[row, col], sems[1].at[row, col], sibling)

    def z_start(buf, sems):
        for i in range(2):
            z_copy(buf, sems, 1, i).start()
        sib_copy(buf, sems, 0).start()

    def z_step(buf, sems, j):
        if j < 4:
            for i in range(2):
                z_copy(buf, sems, j, i).wait()
                z_copy(buf, sems, j + 1, i).start()
                sib_copy(buf, sems, -j * dirs[i]).start()
        else:
            for i in range(2):
                z_copy(buf, sems, j, i).wait()
            sib_copy(buf, sems, 4).start()

    def sib_wait(buf, sems, *offs):
        for off in offs:
            sib_copy(buf, sems, off).wait()

    def stat_z(j, i):
        ref = stat_all.at[mod8(z - (j - 1) * dirs[i])]
        return remote(ref, ref, zt_s.at[j, i], zt_r.at[j, i], dev_z(dirs[i]))

    def stat_step(j):
        for i in range(2):
            if (j, i) == (4, 1):
                continue
            stat_z(j, i).wait()
            if j < 3 + (i == 0):
                stat_z(j + 1, i).start()

    def added(first, *rest):
        res = first.astype(F32)
        for one in rest:
            res += one.astype(F32)
        return res

    def quarter_copy(s, g, o, i):
        at = o * 2 + i
        return remote(
            part.at[s, o, pl.ds((6, 10)[i], 4), g],
            land1.at[s, o, i, :, g],
            rq_s.at[s * QUARTERS + g, at],
            rq_r.at[s * QUARTERS + g, at],
            devs[o][0](dirs[i]),
        )

    both = [(o, i) for o in range(2) for i in range(2)]
    rel_x = [mod4(k - x) for k in range(SIDE)]
    rel_y = [mod4(k - y) for k in range(SIDE)]
    x_y = [rel_x[h // SIDE] * SIDE + rel_y[h % SIDE] for h in range(GROUP)]
    y_x = [rel_y[h % SIDE] * SIDE + rel_x[h // SIDE] for h in range(GROUP)]
    places = (
        [jnp.where(core == 0, a, b) for a, b in zip(x_y, y_x)],
        [jnp.where(core == 0, b, a) for a, b in zip(x_y, y_x)],
    )

    def products(s, g):
        rows = rows_all[pl.ds(g * QUARTERS, QUARTERS)].reshape(QUARTERS * ROWS, FEATS)
        res = jnp.dot(rows, w_in[s], preferred_element_type=F32).astype(BF16)
        for h in range(GROUP):
            block = res[h * QUARTER : (h + 1) * QUARTER]
            for o in range(2):
                part[s, o, places[o][h], g] = block[:, o * WIDE : (o + 1) * WIDE]

    eye = lax.broadcasted_iota(jnp.int32, (ROWS, 128), 0) == lax.broadcasted_iota(
        jnp.int32, (ROWS, 128), 1
    )
    line = lax.broadcasted_iota(jnp.int32, (8, 128), 0)

    def to_row(column):
        return jnp.sum(jnp.where(eye, column, 0.0), 0, keepdims=True)

    def to_column(row):
        return jnp.sum(jnp.where(eye, row, 0.0), 1, keepdims=True)

    def norm(rows, tile):
        mean, scale = to_column(tile[0:1]), to_column(tile[1:2])
        return ((rows.astype(F32) - mean) * scale * gain[...].reshape(1, FEATS)).astype(BF16)

    zx = (zx_s, zx_r)
    zk = (zk_s, zk_r)
    raw_all[ffn] = act[...]
    z_start(raw_all, zx)
    values = act[...].astype(F32)
    mean = jnp.mean(values, 1, keepdims=True)
    square = jnp.sum((values - mean) ** 2, 1, keepdims=True)
    mean, square = to_row(mean), to_row(square)
    def merge(count, tiles):
        means = [tile[0:1] for tile in tiles]
        squares = [tile[1:2] for tile in tiles]
        mean = (means[0] + means[1] + means[2] + means[3]) * 0.25
        square = squares[0] + squares[1] + squares[2] + squares[3]
        for one in means:
            square += count * (one - mean) ** 2
        return mean, square

    def finish(tiles):
        mean, square = merge(FEATS * SIDE, tiles)
        return jnp.where(line == 0, mean, lax.rsqrt(square * (1.0 / D) + EPSILON))

    stat[0] = jnp.where(line == 0, mean, square)
    each(stat_copy, 0, "start")
    total[...] = jnp.zeros_like(total)
    each(stat_copy, 0, "wait")
    mean, square = merge(FEATS, [stat[0]] + [stat_in[0, d] for d in range(3)])
    stat[1] = jnp.where(line == 0, mean, square)
    each(stat_copy, 1, "start")
    for d in range(SIDE):
        other_copy(d).start()
    z_step(raw_all, zx, 1)
    each(stat_copy, 1, "wait")
    for d in range(SIDE):
        other_copy(d).wait()
    stat_all[z, core] = finish([stat[1]] + [stat_in[1, d] for d in range(3)])
    stat_all[z, 1 - core] = finish([stat_other[d] for d in range(SIDE)])
    for i in range(2):
        stat_z(1, i).start()
    normed = norm(act[...], stat_all[z, core])
    kv_copy.wait()
    pairs = jnp.dot(normed, w_kv[...], preferred_element_type=F32).astype(BF16)
    for q in range(4):
        pair_part[q] = pairs[:, q * 128 : (q + 1) * 128]
    each(pair_copy, 0, "start")
    for s in range(EARLY):
        for o in range(2):
            w_copy(s, o).wait()

    pair = z // 2
    turned = 1 - 2 * (z % 2)
    def order(j):
        step = jnp.where(j == 3, 2, jnp.where(j == 0, 0, jnp.where(j == 1, -turned, turned)))
        return mod4(pair + step)

    def pair_add(own, a):
        return added(own, pair_in[a, 0], pair_in[a, 1], pair_in[a, 2]).astype(BF16)

    def early(j, carry):
        @pl.when(j == 0)
        def _():
            stat_step(1)
            sib_wait(raw_all, zx, 0, 1, -1)

        @pl.when(j == 1)
        def _():
            for s in range(EARLY, STEPS):
                for o in range(2):
                    w_copy(s, o).start(priority=1)
            each(pair_copy, 0, "wait")
            pair_sum[...] = pair_add(pair_part[x], 0)
            each(pair_copy, 1, "start")
            z_step(raw_all, zx, 3)
            stat_step(2)
            sib_wait(raw_all, zx, 2, -2)

        @pl.when(j == 2)
        def _():
            for i in range(2):
                for copy in turn_copies(i):
                    copy.start(priority=1)
            for u in range(UNITS):
                wb_copy(u).start(priority=1)
            each(pair_copy, 1, "wait")
            pair_all[x] = pair_add(pair_sum[...], 1)
            each(pair_copy, 2, "start")
            z_step(raw_all, zx, 4)
            stat_step(3)
            sib_wait(raw_all, zx, 3, -3)

        @pl.when(j == 3)
        def _():
            stat_step(4)
            sib_wait(raw_all, zx, 4)

        g = order(j)

        def one(k, c):
            rows_all[g * 4 + k] = norm(raw_all[g * 4 + k], stat_all[g * 2 + k // 2, k % 2])
            return c

        lax.fori_loop(0, QUARTERS, one, 0)

        def step(s, c):
            products(s, g)
            for o, i in both:
                quarter_copy(s, g, o, i).start()
            pl.when((j == 0) & (s == 0))(lambda: z_step(raw_all, zx, 2))
            return c

        lax.fori_loop(0, EARLY, step, 0)
        return carry

    lax.fori_loop(0, QUARTERS, early, 0)
    each(pair_copy, 2, "wait")
    for i in range(2):
        for copy in turn_copies(i):
            copy.wait()
    first, second = pair_all[0].astype(F32), pair_all[1].astype(F32)
    kv_all[ffn, :, 0:128] = (first * turn[1, 0] - second * turn[1, 1]).astype(BF16)
    kv_all[ffn, :, 128:256] = (first * turn[1, 1] + second * turn[1, 0]).astype(BF16)
    kv_all[ffn, :, 256:384] = pair_all[2]
    kv_all[ffn, :, 384:512] = pair_all[3]
    z_start(kv_all, zk)

    for s in range(EARLY, STEPS):
        for o in range(2):
            w_copy(s, o).wait()
    for u in range(UNITS):
        wb_copy(u).wait()

    def rs_copy(s, o, k, i):
        at = o * 8 + k * 2 + i
        if k == 1:
            src = part.at[s, o, pl.ds((4, 14)[i], 2)]
        elif k == 2:
            src = near_sum.at[s, o, pl.ds((6, 10)[i], 4)]
        else:
            src = near_sum.at[s, o, pl.ds((4, 14)[i], 2)]
        return remote(
            src,
            (land1, last1, land2, last2)[k].at[s, o, i],
            rs_s.at[s, at],
            rs_r.at[s, at],
            devs[o][k // 2](dirs[i]),
        )

    def phase0(s):
        def tile(g, carry):
            products(s, g)
            for o, i in both:
                quarter_copy(s, g, o, i).start()
            return carry

        lax.fori_loop(0, QUARTERS, tile, 0)

    def phase1(s):
        def arrived(g, carry):
            for o, i in both:
                quarter_copy(s, g, o, i).wait()
            return carry

        lax.fori_loop(0, QUARTERS, arrived, 0)
        for o, i in both:
            first = (4, 14)[i]
            part[s, o, first : first + 2] += land1[s, o, i, 2 - 2 * i : 4 - 2 * i]
            rs_copy(s, o, 1, i).start()

    def phase2(s):
        for o in range(2):
            for i in range(2):
                rs_copy(s, o, 1, i).wait()
            for i in range(2):
                res = added(
                    part[s, o, 2 * i : 2 * i + 2],
                    last1[s, o, i],
                    land1[s, o, 1 - i, 2 - 2 * i : 4 - 2 * i],
                ).astype(BF16)
                near_sum[s, o, 8 * i : 8 * i + 8] = res.reshape(2 * QUARTERS, QUARTER, WIDE)
            for i in range(2):
                rs_copy(s, o, 2, i).start()

    def phase3(s):
        for o, i in both:
            rs_copy(s, o, 2, i).wait()
            first = (4, 14)[i]
            near_sum[s, o, first : first + 2] += land2[s, o, i, 2 - 2 * i : 4 - 2 * i]
            rs_copy(s, o, 3, i).start()

    def attend(left, right):
        seg_row = seg[...].astype(F32)
        key_at = lax.broadcasted_iota(jnp.int32, (ROWS, TOKENS), 1)
        row_at = lax.broadcasted_iota(jnp.int32, (ROWS, TOKENS), 0)
        row_at = row_at + (TOKENS // QUARTERS - QUARTER) * (row_at // QUARTER) + hid * QUARTER
        own = jnp.sum(jnp.where(key_at == row_at, seg_row, 0.0), 1, keepdims=True)
        allowed = (key_at <= row_at) & (seg_row == own)
        keys = kv_all[:, :, 0:HEAD].reshape(TOKENS, HEAD)
        vals = kv_all[:, :, HEAD : 2 * HEAD].reshape(TOKENS, HEAD)
        cosine, sine = turn[0, 0] * HEAD**-0.5, turn[0, 1] * HEAD**-0.5
        groups = [v[:, k * 128 : (k + 1) * 128] for v in (left, right) for k in range(3)]
        for h in range(3):
            a, b = groups[2 * h], groups[2 * h + 1]
            heads[h, :, 0:128] = (a * cosine - b * sine).astype(BF16)
            heads[h, :, 128:256] = (a * sine + b * cosine).astype(BF16)

        def head(h, carry):
            scores = lax.dot_general(
                heads[h], keys, (((1,), (1,)), ((), ())), preferred_element_type=F32
            )
            expos = jnp.where(allowed, jnp.exp(scores), 0.0)
            probs = (expos / jnp.sum(expos, 1, keepdims=True)).astype(BF16)
            heads[h] = jnp.dot(probs, vals, preferred_element_type=F32).astype(BF16)
            return carry

        lax.fori_loop(0, 3, head, 0)
        left = jnp.concatenate([heads[0], heads[1, :, 0:128]], 1)
        right = jnp.concatenate([heads[1, :, 128:256], heads[2]], 1)
        return left, right

    def put(u, block):
        for o in range(2):
            mixed[u // 2, o, 0, 0, u % 2] = block[o * HALF : (o + 1) * HALF]

    def gather_copy(u, o, k, i):
        d = dirs[i]
        away, near = (3, 1)[i], (3, 1)[i]
        dev = devs[o][k // 2](d)
        pair = mixed.at[u // 2, o]
        which = u % 2
        if k == 0:
            src, dst = pair.at[0, 0, which], pair.at[0, away, which]
        elif k == 1:
            rows = pl.ds(i * QUARTER, QUARTER)
            src, dst = pair.at[0, near, which, rows], pair.at[0, 2, which, rows]
        elif k == 2:
            src, dst = pair.at[0, :, which], pair.at[away, :, which]
        else:
            cut = pl.ds(2 * i, 2)
            src, dst = pair.at[near, cut, which], pair.at[2, cut, which]
        at = o * 8 + k * 2 + i
        return remote(src, dst, ag_s.at[u, at], ag_r.at[u, at], dev)

    def by_units(s, fn):
        def unit(u, carry):
            fn(u)
            return carry

        lax.fori_loop(jnp.where(s == 0, 0, s + 1), s + 2, unit, 0)

    def gather_first(u):
        for o, i in both:
            gather_copy(u, o, 0, i).start()

    def phase4(s):
        sums = []
        for o in range(2):
            for i in range(2):
                rs_copy(s, o, 3, i).wait()
            sums.append(
                jnp.concatenate(
                    [
                        added(
                            near_sum[s, o, 2 * i : 2 * i + 2],
                            last2[s, o, i],
                            land2[s, o, 1 - i, 2 - 2 * i : 4 - 2 * i],
                        ).reshape(HALF, WIDE)
                        for i in range(2)
                    ],
                    0,
                )
            )

        @pl.when(s == 0)
        def _():
            left, right = attend(*sums)
            put(0, left)
            put(1, right)

        @pl.when(s > 0)
        def _():
            gate, up = sums
            put(s + 1, (gate / (1.0 + jnp.exp(-gate)) * up).astype(BF16))

        by_units(s, gather_first)

    def phase5(u):
        for o, i in both:
            gather_copy(u, o, 0, i).wait()
            gather_copy(u, o, 1, i).start()

    def phase6(u):
        for o in range(2):
            for i in range(2):
                gather_copy(u, o, 1, i).wait()
            for i in range(2):
                gather_copy(u, o, 2, i).start()

    def phase7(u):
        for o, i in both:
            gather_copy(u, o, 2, i).wait()
            gather_copy(u, o, 3, i).start()

    def accumulate(u):
        def tile(k, carry):
            o, p = k // 2, k % 2
            rows = mixed[u // 2, o, pl.ds(2 * p, 2), :, u % 2].reshape(2 * SIDE * HALF, WIDE)
            at = pl.ds(pl.multiple_of(p * 256, 256), 256)
            total[o, at] += jnp.dot(rows, w_back[u], preferred_element_type=F32)
            return carry

        lax.fori_loop(0, 4, tile, 0)

    def phase8(u):
        for o, i in both:
            gather_copy(u, o, 3, i).wait()
        accumulate(u)

    def slot(t, carry):
        pl.when((t >= EARLY) & (t < STEPS))(lambda: phase0(t))
        for k, fn in ((2, phase1), (4, phase2), (5, phase3)):
            s = t - k
            pl.when((s >= 0) & (s < STEPS))(lambda fn=fn, s=s: fn(s))

        for j in range(1, 5):

            @pl.when(t == j + 1)
            def _(j=j):
                z_step(kv_all, zk, j)
                if j == 4:
                    sib_wait(kv_all, zk, 0, 1, -1, 2, -2, 3, -3, 4)

        s4 = t - 6
        pl.when((s4 >= 0) & (s4 < STEPS))(lambda: phase4(s4))

        for k, fn in ((7, phase5), (8, phase6), (9, phase7), (10, phase8)):
            s = t - k

            @pl.when((s >= 0) & (s < STEPS))
            def _(fn=fn, s=s):
                by_units(s, fn)

        return carry

    lax.fori_loop(2, STEPS + 10, slot, 0)

    offsets = (4, 3, -3, 2, -2, 1, -1, 0)

    def some_rows(block, k):
        g = block // SIDE
        o = g // 2
        px = mod4(block % SIDE - x)
        place = jnp.where(o == core, rel_y[k] * SIDE + px, px * SIDE + rel_y[k])
        first = pl.multiple_of(place * HALF + (g % 2) * QUARTER, QUARTER)
        return total[o, pl.ds(first, QUARTER)]

    def span(k):
        return slice(k * QUARTER, (k + 1) * QUARTER)

    def sib_sum(k):
        at = mod8(z + offsets[k])
        return remote(sib_out.at[at], sib_in.at[at], zr_s.at[k], zr_r.at[k], sibling)

    def sib_send(*which):
        for k in which:
            at = mod8(z + offsets[k])
            for q in range(4):
                sib_out[at, span(q)] = some_rows(at * 2 + 1 - core, q).astype(BF16)
            sib_sum(k).start()

    sib_send(0, 1, 2)

    def chip_sum(k, q):
        at = mod8(z + offsets[k])
        return some_rows(at * 2 + core, q) + sib_in[at, span(q)].astype(F32)

    def ring_copy(j, i, q):
        at = 8 + (j * 2 + i) * 4 + q
        return remote(
            ring_out.at[j, i, q], ring_in.at[j, i, q], zr_s.at[at], zr_r.at[at], dev_z(dirs[i])
        )

    sib_sum(0).wait()
    for q in range(2):
        for i in range(2):
            ring_out[0, i, 2 * i + q] = chip_sum(0, 2 * i + q).astype(BF16)
            ring_copy(0, i, 2 * i + q).start()
    sib_send(3, 4)
    for j in (1, 2, 3):
        for i in range(2):
            sib_sum(2 * j - 1 + i).wait()
        for turn_of in range(4):
            for i in range(2):
                q = (2 * (1 - i) + turn_of) % 4
                here = chip_sum(2 * j - 1 + i, q)
                if j > 1 or q // 2 == i:
                    ring_copy(j - 1, i, q).wait()
                    here += ring_in[j - 1, i, q].astype(F32)
                ring_out[j, i, q] = here.astype(BF16)
                ring_copy(j, i, q).start()
        if j < 3:
            sib_send(*((5, 6), (7,))[j - 1])
    sib_sum(7).wait()
    for q in (2, 0, 3, 1):
        here = chip_sum(7, q) + act[span(q)].astype(F32)
        for i in range(2):
            ring_copy(3, i, q).wait()
            here += ring_in[3, i, q].astype(F32)
        out[span(q)] = here.astype(BF16)


def per_device(activations, ln_gain, segments, w_query, w_key_value, w_gate, w_up, w_out, w_down):
    vmem = pl.BlockSpec(memory_space=pltpu.VMEM)
    far = pl.BlockSpec(memory_space=pltpu.HBM)
    dma = pltpu.SemaphoreType.DMA
    scratch = [
        pltpu.VMEM((ROWS, FEATS), BF16),
        pltpu.VMEM((FEATS,), F32),
        pltpu.VMEM((1, TOKENS), jnp.int32),
        pltpu.VMEM((STEPS, FEATS, 2 * WIDE), BF16),
        pltpu.VMEM((UNITS, WIDE, FEATS), BF16),
        pltpu.VMEM((FEATS, 512), BF16),
        pltpu.VMEM((2, 2, ROWS, 128), F32),
        pltpu.VMEM((2, 8, 128), F32),
        pltpu.VMEM((2, 3, 8, 128), F32),
        pltpu.VMEM((4, 8, 128), F32),
        pltpu.VMEM((RING, 2, 8, 128), F32),
        pltpu.VMEM((GROUP, ROWS, FEATS), BF16),
        pltpu.VMEM((GROUP, ROWS, FEATS), BF16),
        pltpu.VMEM((4, ROWS, 128), BF16),
        pltpu.VMEM((2, 3, ROWS, 128), BF16),
        pltpu.VMEM((ROWS, 128), BF16),
        pltpu.VMEM((4, ROWS, 128), BF16),
        pltpu.VMEM((3, ROWS, HEAD), BF16),
        pltpu.VMEM((GROUP, ROWS, 512), BF16),
        pltpu.VMEM((STEPS, 2, GROUP, QUARTERS, QUARTER, WIDE), BF16),
        pltpu.VMEM((STEPS, 2, 2, 4, QUARTERS, QUARTER, WIDE), BF16),
        pltpu.VMEM((STEPS, 2, 2, 2, QUARTERS, QUARTER, WIDE), BF16),
        pltpu.VMEM((STEPS, 2, SIDE * QUARTERS, QUARTER, WIDE), BF16),
        pltpu.VMEM((STEPS, 2, 2, QUARTERS, QUARTER, WIDE), BF16),
        pltpu.VMEM((STEPS, 2, 2, 2, QUARTER, WIDE), BF16),
        pltpu.VMEM((UNITS // 2, 2, SIDE, SIDE, 2, HALF, WIDE), BF16),
        pltpu.VMEM((2, GROUP * HALF, FEATS), F32),
        pltpu.VMEM((RING, ROWS, FEATS), BF16),
        pltpu.VMEM((RING, ROWS, FEATS), BF16),
        pltpu.VMEM((4, 2, 4, QUARTER, FEATS), BF16),
        pltpu.VMEM((4, 2, 4, QUARTER, FEATS), BF16),
        dma((STEPS, 2)),
        dma((UNITS,)),
        dma((14,)),
        dma((7, 3)),
        dma((7, 3)),
        dma((8, 2)),
        dma((8, 2)),
        dma((5, 2)),
        dma((5, 2)),
        dma((STEPS * QUARTERS, 4)),
        dma((STEPS * QUARTERS, 4)),
        dma((8, 2)),
        dma((8, 2)),
        dma((STEPS, 16)),
        dma((STEPS, 16)),
        dma((UNITS, 16)),
        dma((UNITS, 16)),
        dma((40,)),
        dma((40,)),
    ]
    return pl.pallas_call(
        block_kernel,
        out_shape=jax.ShapeDtypeStruct((ROWS, FEATS), BF16),
        in_specs=[far] * 10,
        out_specs=vmem,
        scratch_shapes=scratch,
        compiler_params=pltpu.CompilerParams(
            collective_id=0, has_side_effects=True, vmem_limit_bytes=54784 * 1024
        ),
    )(
        pltpu.with_memory_space_constraint(activations, pltpu.HBM),
        pltpu.with_memory_space_constraint(ln_gain, pltpu.HBM),
        pltpu.with_memory_space_constraint(segments.reshape(1, TOKENS), pltpu.HBM),
        jnp.asarray(tables()),
        w_query,
        w_key_value,
        w_gate,
        w_up,
        w_out,
        w_down,
    )


def solution(mesh):
    placed = (
        P("ffn", "hid"),
        P("hid"),
        P(),
        P("hid", "ffn"),
        P("hid", None),
        P("hid", "ffn"),
        P("hid", "ffn"),
        P("ffn", "hid"),
        P("ffn", "hid"),
    )
    return jax.shard_map(
        per_device, mesh=mesh, in_specs=placed, out_specs=P("ffn", "hid"), check_vma=False
    )
```

```python
import jax
import jax.numpy as jnp
import numpy as np
from jax import lax
from jax.experimental import pallas as pl
from jax.experimental.pallas import tpu as pltpu
from jax.sharding import PartitionSpec as P

D = 10240
HEAD = 256
TOKENS = 1024
EPSILON = 1e-06

SIDE = 4
RING = 8
GROUP = SIDE * SIDE
ROWS = TOKENS // GROUP
FEATS = D // GROUP
WIDE = 384
STEPS = 7
EARLY = 3
UNITS = 8
HALF = ROWS // 2
QUARTERS = 4
QUARTER = ROWS // 4
F32 = jnp.float32
BF16 = jnp.bfloat16


def tables():
    half = HEAD // 2
    frequency = np.float32(10000.0) ** (-np.arange(half, dtype=np.float32) / np.float32(half))
    angles = np.arange(TOKENS, dtype=np.float32)[:, None] * frequency[None, :].astype(np.float32)
    wide = angles.astype(np.float64)
    return np.stack([np.cos(wide), np.sin(wide)]).astype(np.float32)


def block_kernel(
    act_far,
    gain_far,
    seg_far,
    table,
    w_query,
    w_pairs,
    w_gate,
    w_up,
    w_out,
    w_down,
    out,
    act,
    gain,
    seg,
    w_in,
    w_back,
    w_kv,
    turn,
    stat,
    stat_in,
    stat_other,
    stat_all,
    raw_all,
    rows_all,
    pair_part,
    pair_in,
    pair_sum,
    pair_all,
    heads,
    kv_all,
    part,
    land1,
    last1,
    near_sum,
    land2,
    last2,
    mixed,
    total,
    sib_out,
    sib_in,
    ring_out,
    ring_in,
    w_sem,
    wb_sem,
    m_sem,
    small_s,
    small_r,
    zx_s,
    zx_r,
    zt_s,
    zt_r,
    rq_s,
    rq_r,
    zk_s,
    zk_r,
    rs_s,
    rs_r,
    ag_s,
    ag_r,
    zr_s,
    zr_r,
):
    own_copies = [
        pltpu.make_async_copy(far, near, m_sem.at[11 + k])
        for k, (far, near) in enumerate(((act_far, act), (gain_far, gain), (seg_far, seg)))
    ]
    for copy in own_copies:
        copy.start(priority=1)
    hid = lax.axis_index("hid")
    ffn = lax.axis_index("ffn")
    x, y = hid // SIDE, hid % SIDE
    z, core = ffn // 2, ffn % 2

    def mod4(v):
        return (v + SIDE) % SIDE

    def mod8(v):
        return (v + RING) % RING

    ids_x = {d: mod4(x + d) * SIDE + y for d in (1, 2, 3)}
    ids_y = {d: x * SIDE + mod4(y + d) for d in (1, 2, 3)}
    ids_z = {d: mod8(z + d) * 2 + core for d in (1, -1)}

    def dev_x(d):
        return (ids_x[d % SIDE], ffn)

    def dev_y(d):
        return (ids_y[d % SIDE], ffn)

    def dev_z(d):
        return (hid, ids_z[d])

    other = z * 2 + 1 - core
    sibling = (hid, other)
    dirs = (1, -1)

    ids_one = {d: jnp.where(core == 0, ids_x[d], ids_y[d]) for d in (1, 3)}
    ids_two = {d: jnp.where(core == 0, ids_y[d], ids_x[d]) for d in (1, 3)}

    def dev_one(d):
        return (ids_one[d % SIDE], ffn)

    def dev_two(d):
        return (ids_two[d % SIDE], ffn)

    devs = ((dev_one, dev_two), (dev_two, dev_one))

    barrier = pltpu.get_barrier_semaphore()
    partners = [dev_x(d) for d in (1, 2, 3)] + [dev_y(d) for d in (1, 2, 3)]
    partners += [(ids_y[d], other) for d in (1, 2, 3)]
    partners += [dev_z(1), dev_z(-1), sibling]
    for dev in partners:
        pl.semaphore_signal(barrier, inc=1, device_id=dev, device_id_type=pl.DeviceIdType.MESH)

    def remote(src, dst, ssem, rsem, dev):
        return pltpu.make_async_remote_copy(
            src_ref=src,
            dst_ref=dst,
            send_sem=ssem,
            recv_sem=rsem,
            device_id=dev,
            device_id_type=pl.DeviceIdType.MESH,
        )

    def w_copy(s, o):
        if s == 0:
            src = w_query.at[:, pl.ds(o * WIDE, WIDE)]
        else:
            src = (w_gate, w_up)[o].at[:, pl.ds((s - 1) * WIDE, WIDE)]
        return pltpu.make_async_copy(src, w_in.at[s, :, pl.ds(o * WIDE, WIDE)], w_sem.at[s, o])

    def wb_copy(u):
        if u < 2:
            src = w_out.at[pl.ds(u * WIDE, WIDE)]
        else:
            src = w_down.at[pl.ds((u - 2) * WIDE, WIDE)]
        return pltpu.make_async_copy(src, w_back.at[u], wb_sem.at[u])

    def turn_copies(i):
        copies = [
            pltpu.make_async_copy(
                table.at[i, pl.ds(pl.multiple_of(ffn * ROWS, ROWS), ROWS)],
                turn.at[1, i],
                m_sem.at[1 + 5 * i],
            )
        ]
        for g in range(QUARTERS):
            first = pl.multiple_of(g * (TOKENS // QUARTERS) + hid * QUARTER, QUARTER)
            copies.append(
                pltpu.make_async_copy(
                    table.at[i, pl.ds(first, QUARTER)],
                    turn.at[0, i, pl.ds(g * QUARTER, QUARTER)],
                    m_sem.at[2 + 5 * i + g],
                )
            )
        return copies

    kv_copy = pltpu.make_async_copy(w_pairs, w_kv, m_sem.at[0])

    kv_copy.start(priority=1)
    for s in range(EARLY):
        for o in range(2):
            w_copy(s, o).start(priority=1)
    for copy in own_copies:
        copy.wait()
    pl.semaphore_wait(barrier, len(partners))

    def stat_copy(a, d):
        return remote(
            stat.at[a], stat_in.at[a, d - 1], small_s.at[a, d - 1], small_r.at[a, d - 1],
            (dev_x, dev_y)[a](d),
        )

    def other_copy(d):
        return remote(
            stat.at[1], stat_other.at[d], small_s.at[5 + d // 3, d % 3], small_r.at[5 + d // 3, d % 3],
            (ids_y[d], other) if d else sibling,
        )

    def pair_copy(k, d):
        if k == 0:
            src, dst, dev = pair_part.at[mod4(x + d)], pair_in.at[0, d - 1], dev_x(d)
        elif k == 1:
            src, dst, dev = pair_sum, pair_in.at[1, d - 1], dev_y(d)
        else:
            src, dst, dev = pair_all.at[x], pair_all.at[x], dev_x(d)
        return remote(src, dst, small_s.at[2 + k, d - 1], small_r.at[2 + k, d - 1], dev)

    def each(fn, k, what):
        for d in (1, 2, 3):
            getattr(fn(k, d), what)()

    def z_copy(buf, sems, j, i):
        d = dirs[i]
        block = mod8(z - (j - 1) * d) * 2 + core
        ref = buf.at[block] if j < 4 else buf.at[block, pl.ds(i * HALF, HALF)]
        return remote(ref, ref, sems[0].at[j - 1, i], sems[1].at[j - 1, i], dev_z(d))

    def sib_copy(buf, sems, off):
        ref = buf.at[mod8(z + off) * 2 + core]
        row = 4 + (off + 3) // 2
        col = (off + 3) % 2
        return remote(ref, ref, sems[0].at[row, col], sems[1].at[row, col], sibling)

    def z_start(buf, sems):
        for i in range(2):
            z_copy(buf, sems, 1, i).start()
        sib_copy(buf, sems, 0).start()

    def z_step(buf, sems, j):
        if j < 4:
            for i in range(2):
                z_copy(buf, sems, j, i).wait()
                z_copy(buf, sems, j + 1, i).start()
                sib_copy(buf, sems, -j * dirs[i]).start()
        else:
            for i in range(2):
                z_copy(buf, sems, j, i).wait()
            sib_copy(buf, sems, 4).start()

    def sib_wait(buf, sems, *offs):
        for off in offs:
            sib_copy(buf, sems, off).wait()

    def stat_z(j, i):
        ref = stat_all.at[mod8(z - (j - 1) * dirs[i])]
        return remote(ref, ref, zt_s.at[j, i], zt_r.at[j, i], dev_z(dirs[i]))

    def stat_step(j):
        for i in range(2):
            if (j, i) == (4, 1):
                continue
            stat_z(j, i).wait()
            if j < 3 + (i == 0):
                stat_z(j + 1, i).start()

    def added(first, *rest):
        res = first.astype(F32)
        for one in rest:
            res += one.astype(F32)
        return res

    def quarter_copy(s, j, g, o, i):
        at = o * 2 + i
        return remote(
            part.at[s, o, pl.ds((6, 10)[i], 4), g],
            land1.at[s, o, i, :, g],
            rq_s.at[s * QUARTERS + j, at],
            rq_r.at[s * QUARTERS + j, at],
            devs[o][0](dirs[i]),
        )

    both = [(o, i) for o in range(2) for i in range(2)]
    rel_x = [mod4(k - x) for k in range(SIDE)]
    rel_y = [mod4(k - y) for k in range(SIDE)]
    x_y = [rel_x[h // SIDE] * SIDE + rel_y[h % SIDE] for h in range(GROUP)]
    y_x = [rel_y[h % SIDE] * SIDE + rel_x[h // SIDE] for h in range(GROUP)]
    places = (
        [jnp.where(core == 0, a, b) for a, b in zip(x_y, y_x)],
        [jnp.where(core == 0, b, a) for a, b in zip(x_y, y_x)],
    )

    def products(s, g):
        rows = rows_all[pl.ds(g * QUARTERS, QUARTERS)].reshape(QUARTERS * ROWS, FEATS)
        res = jnp.dot(rows, w_in[s], preferred_element_type=F32).astype(BF16)
        for h in range(GROUP):
            block = res[h * QUARTER : (h + 1) * QUARTER]
            for o in range(2):
                part[s, o, places[o][h], g] = block[:, o * WIDE : (o + 1) * WIDE]

    eye = lax.broadcasted_iota(jnp.int32, (ROWS, 128), 0) == lax.broadcasted_iota(
        jnp.int32, (ROWS, 128), 1
    )
    line = lax.broadcasted_iota(jnp.int32, (8, 128), 0)

    def to_row(column):
        return jnp.sum(jnp.where(eye, column, 0.0), 0, keepdims=True)

    def to_column(row):
        return jnp.sum(jnp.where(eye, row, 0.0), 1, keepdims=True)

    def norm(rows, tile):
        mean, scale = to_column(tile[0:1]), to_column(tile[1:2])
        return ((rows.astype(F32) - mean) * scale * gain[...].reshape(1, FEATS)).astype(BF16)

    zx = (zx_s, zx_r)
    zk = (zk_s, zk_r)
    raw_all[ffn] = act[...]
    z_start(raw_all, zx)
    values = act[...].astype(F32)
    mean = jnp.mean(values, 1, keepdims=True)
    square = jnp.sum((values - mean) ** 2, 1, keepdims=True)
    mean, square = to_row(mean), to_row(square)
    def merge(count, tiles):
        means = [tile[0:1] for tile in tiles]
        squares = [tile[1:2] for tile in tiles]
        mean = (means[0] + means[1] + means[2] + means[3]) * 0.25
        square = squares[0] + squares[1] + squares[2] + squares[3]
        for one in means:
            square += count * (one - mean) ** 2
        return mean, square

    def finish(tiles):
        mean, square = merge(FEATS * SIDE, tiles)
        return jnp.where(line == 0, mean, lax.rsqrt(square * (1.0 / D) + EPSILON))

    stat[0] = jnp.where(line == 0, mean, square)
    each(stat_copy, 0, "start")
    total[...] = jnp.zeros_like(total)
    each(stat_copy, 0, "wait")
    mean, square = merge(FEATS, [stat[0]] + [stat_in[0, d] for d in range(3)])
    stat[1] = jnp.where(line == 0, mean, square)
    each(stat_copy, 1, "start")
    for d in range(SIDE):
        other_copy(d).start()
    z_step(raw_all, zx, 1)
    each(stat_copy, 1, "wait")
    for d in range(SIDE):
        other_copy(d).wait()
    stat_all[z, core] = finish([stat[1]] + [stat_in[1, d] for d in range(3)])
    stat_all[z, 1 - core] = finish([stat_other[d] for d in range(SIDE)])
    for i in range(2):
        stat_z(1, i).start()
    normed = norm(act[...], stat_all[z, core])
    kv_copy.wait()
    pairs = jnp.dot(normed, w_kv[...], preferred_element_type=F32).astype(BF16)
    for q in range(4):
        pair_part[q] = pairs[:, q * 128 : (q + 1) * 128]
    each(pair_copy, 0, "start")
    for s in range(EARLY):
        for o in range(2):
            w_copy(s, o).wait()

    pair = z // 2
    turned = 1 - 2 * (z % 2)
    def order(j):
        step = jnp.where(j == 3, 2, jnp.where(j == 0, 0, jnp.where(j == 1, -turned, turned)))
        return mod4(pair + step)

    def pair_add(own, a):
        return added(own, pair_in[a, 0], pair_in[a, 1], pair_in[a, 2]).astype(BF16)

    def early(j, carry):
        @pl.when(j == 0)
        def _():
            stat_step(1)
            sib_wait(raw_all, zx, 0, 1, -1)

        @pl.when(j == 1)
        def _():
            for s in range(EARLY, STEPS):
                for o in range(2):
                    w_copy(s, o).start(priority=1)
            each(pair_copy, 0, "wait")
            pair_sum[...] = pair_add(pair_part[x], 0)
            each(pair_copy, 1, "start")
            z_step(raw_all, zx, 3)
            stat_step(2)
            sib_wait(raw_all, zx, 2, -2)

        @pl.when(j == 2)
        def _():
            for i in range(2):
                for copy in turn_copies(i):
                    copy.start(priority=1)
            for u in range(UNITS):
                wb_copy(u).start(priority=1)
            each(pair_copy, 1, "wait")
            pair_all[x] = pair_add(pair_sum[...], 1)
            each(pair_copy, 2, "start")
            z_step(raw_all, zx, 4)
            stat_step(3)
            sib_wait(raw_all, zx, 3, -3)

        @pl.when(j == 3)
        def _():
            stat_step(4)
            sib_wait(raw_all, zx, 4)

        g = order(j)

        def one(k, c):
            rows_all[g * 4 + k] = norm(raw_all[g * 4 + k], stat_all[g * 2 + k // 2, k % 2])
            return c

        lax.fori_loop(0, QUARTERS, one, 0)

        def step(s, c):
            products(s, g)
            for o, i in both:
                quarter_copy(s, j, g, o, i).start()
            pl.when((j == 0) & (s == 0))(lambda: z_step(raw_all, zx, 2))
            return c

        lax.fori_loop(0, EARLY, step, 0)
        return carry

    lax.fori_loop(0, QUARTERS, early, 0)
    each(pair_copy, 2, "wait")
    for i in range(2):
        for copy in turn_copies(i):
            copy.wait()
    first, second = pair_all[0].astype(F32), pair_all[1].astype(F32)
    kv_all[ffn, :, 0:128] = (first * turn[1, 0] - second * turn[1, 1]).astype(BF16)
    kv_all[ffn, :, 128:256] = (first * turn[1, 1] + second * turn[1, 0]).astype(BF16)
    kv_all[ffn, :, 256:384] = pair_all[2]
    kv_all[ffn, :, 384:512] = pair_all[3]
    z_start(kv_all, zk)

    for s in range(EARLY, STEPS):
        for o in range(2):
            w_copy(s, o).wait()
    for u in range(UNITS):
        wb_copy(u).wait()

    far1 = ((6, 4), (10, 4))
    near1 = ((4, 2), (14, 2))

    def rs_copy(s, o, k, i):
        at = o * 8 + k * 2 + i
        if k < 2:
            first, size = (far1, near1)[k][i]
            src = part.at[s, o, pl.ds(first, size)]
        elif k == 2:
            src = near_sum.at[s, o, pl.ds((6, 10)[i], 4)]
        else:
            src = near_sum.at[s, o, pl.ds((4, 14)[i], 2)]
        return remote(
            src,
            (land1, last1, land2, last2)[k].at[s, o, i],
            rs_s.at[s, at],
            rs_r.at[s, at],
            devs[o][k // 2](dirs[i]),
        )

    def phase0(s):
        def tile(g, carry):
            products(s, g)
            return carry

        lax.fori_loop(0, QUARTERS, tile, 0)
        for o, i in both:
            rs_copy(s, o, 0, i).start()

    def phase1(s):
        @pl.when(s < EARLY)
        def _():
            def arrived(j, carry):
                for o, i in both:
                    quarter_copy(s, j, order(j), o, i).wait()
                return carry

            lax.fori_loop(0, QUARTERS, arrived, 0)

        @pl.when(s >= EARLY)
        def _():
            for o, i in both:
                rs_copy(s, o, 0, i).wait()

        for o, i in both:
            first, size = near1[i]
            part[s, o, first : first + size] += land1[s, o, i, 2 - 2 * i : 4 - 2 * i]
            rs_copy(s, o, 1, i).start()

    def phase2(s):
        for o in range(2):
            for i in range(2):
                rs_copy(s, o, 1, i).wait()
            for i in range(2):
                res = added(
                    part[s, o, 2 * i : 2 * i + 2],
                    last1[s, o, i],
                    land1[s, o, 1 - i, 2 - 2 * i : 4 - 2 * i],
                ).astype(BF16)
                near_sum[s, o, 8 * i : 8 * i + 8] = res.reshape(2 * QUARTERS, QUARTER, WIDE)
            for i in range(2):
                rs_copy(s, o, 2, i).start()

    def phase3(s):
        for o, i in both:
            rs_copy(s, o, 2, i).wait()
            first = (4, 14)[i]
            near_sum[s, o, first : first + 2] += land2[s, o, i, 2 - 2 * i : 4 - 2 * i]
            rs_copy(s, o, 3, i).start()

    def attend(left, right):
        seg_row = seg[...].astype(F32)
        key_at = lax.broadcasted_iota(jnp.int32, (ROWS, TOKENS), 1)
        row_at = lax.broadcasted_iota(jnp.int32, (ROWS, TOKENS), 0)
        row_at = row_at + (TOKENS // QUARTERS - QUARTER) * (row_at // QUARTER) + hid * QUARTER
        own = jnp.sum(jnp.where(key_at == row_at, seg_row, 0.0), 1, keepdims=True)
        allowed = (key_at <= row_at) & (seg_row == own)
        keys = kv_all[:, :, 0:HEAD].reshape(TOKENS, HEAD)
        vals = kv_all[:, :, HEAD : 2 * HEAD].reshape(TOKENS, HEAD)
        cosine, sine = turn[0, 0] * HEAD**-0.5, turn[0, 1] * HEAD**-0.5
        groups = [v[:, k * 128 : (k + 1) * 128] for v in (left, right) for k in range(3)]
        for h in range(3):
            a, b = groups[2 * h], groups[2 * h + 1]
            heads[h, :, 0:128] = (a * cosine - b * sine).astype(BF16)
            heads[h, :, 128:256] = (a * sine + b * cosine).astype(BF16)

        def head(h, carry):
            scores = lax.dot_general(
                heads[h], keys, (((1,), (1,)), ((), ())), preferred_element_type=F32
            )
            expos = jnp.where(allowed, jnp.exp(scores), 0.0)
            probs = (expos / jnp.sum(expos, 1, keepdims=True)).astype(BF16)
            heads[h] = jnp.dot(probs, vals, preferred_element_type=F32).astype(BF16)
            return carry

        lax.fori_loop(0, 3, head, 0)
        left = jnp.concatenate([heads[0], heads[1, :, 0:128]], 1)
        right = jnp.concatenate([heads[1, :, 128:256], heads[2]], 1)
        return left, right

    def put(u, block):
        for o in range(2):
            mixed[u // 2, o, 0, 0, u % 2] = block[o * HALF : (o + 1) * HALF]

    def gather_copy(u, o, k, i):
        d = dirs[i]
        away, near = (3, 1)[i], (3, 1)[i]
        dev = devs[o][k // 2](d)
        pair = mixed.at[u // 2, o]
        which = u % 2
        if k == 0:
            src, dst = pair.at[0, 0, which], pair.at[0, away, which]
        elif k == 1:
            rows = pl.ds(i * QUARTER, QUARTER)
            src, dst = pair.at[0, near, which, rows], pair.at[0, 2, which, rows]
        elif k == 2:
            src, dst = pair.at[0, :, which], pair.at[away, :, which]
        else:
            cut = pl.ds(2 * i, 2)
            src, dst = pair.at[near, cut, which], pair.at[2, cut, which]
        at = o * 8 + k * 2 + i
        return remote(src, dst, ag_s.at[u, at], ag_r.at[u, at], dev)

    def by_units(s, fn):
        def unit(u, carry):
            fn(u)
            return carry

        lax.fori_loop(jnp.where(s == 0, 0, s + 1), s + 2, unit, 0)

    def gather_first(u):
        for o, i in both:
            gather_copy(u, o, 0, i).start()

    def phase4(s):
        sums = []
        for o in range(2):
            for i in range(2):
                rs_copy(s, o, 3, i).wait()
            sums.append(
                jnp.concatenate(
                    [
                        added(
                            near_sum[s, o, 2 * i : 2 * i + 2],
                            last2[s, o, i],
                            land2[s, o, 1 - i, 2 - 2 * i : 4 - 2 * i],
                        ).reshape(HALF, WIDE)
                        for i in range(2)
                    ],
                    0,
                )
            )

        @pl.when(s == 0)
        def _():
            left, right = attend(*sums)
            put(0, left)
            put(1, right)

        @pl.when(s > 0)
        def _():
            gate, up = sums
            put(s + 1, (gate / (1.0 + jnp.exp(-gate)) * up).astype(BF16))

        by_units(s, gather_first)

    def phase5(u):
        for o, i in both:
            gather_copy(u, o, 0, i).wait()
            gather_copy(u, o, 1, i).start()

    def phase6(u):
        for o in range(2):
            for i in range(2):
                gather_copy(u, o, 1, i).wait()
            for i in range(2):
                gather_copy(u, o, 2, i).start()

    def phase7(u):
        for o, i in both:
            gather_copy(u, o, 2, i).wait()
            gather_copy(u, o, 3, i).start()

    def accumulate(u):
        def tile(k, carry):
            o, p = k // 2, k % 2
            rows = mixed[u // 2, o, pl.ds(2 * p, 2), :, u % 2].reshape(2 * SIDE * HALF, WIDE)
            at = pl.ds(pl.multiple_of(p * 256, 256), 256)
            total[o, at] += jnp.dot(rows, w_back[u], preferred_element_type=F32)
            return carry

        lax.fori_loop(0, 4, tile, 0)

    def phase8(u):
        for o, i in both:
            gather_copy(u, o, 3, i).wait()
        accumulate(u)

    def slot(t, carry):
        pl.when((t >= EARLY) & (t < STEPS))(lambda: phase0(t))
        for k, fn in ((2, phase1), (3, phase2), (4, phase3)):
            s = t - k
            pl.when((s >= 0) & (s < STEPS))(lambda fn=fn, s=s: fn(s))

        for j in range(1, 5):

            @pl.when(t == j + 1)
            def _(j=j):
                z_step(kv_all, zk, j)
                if j == 4:
                    sib_wait(kv_all, zk, 0, 1, -1, 2, -2, 3, -3, 4)

        s4 = t - 5
        pl.when((s4 >= 0) & (s4 < STEPS))(lambda: phase4(s4))

        for k, fn in ((6, phase5), (7, phase6), (8, phase7), (9, phase8)):
            s = t - k

            @pl.when((s >= 0) & (s < STEPS))
            def _(fn=fn, s=s):
                by_units(s, fn)

        return carry

    lax.fori_loop(2, STEPS + 9, slot, 0)

    offsets = (4, 3, -3, 2, -2, 1, -1, 0)

    def some_rows(block, k):
        g = block // SIDE
        o = g // 2
        px = mod4(block % SIDE - x)
        place = jnp.where(o == core, rel_y[k] * SIDE + px, px * SIDE + rel_y[k])
        first = pl.multiple_of(place * HALF + (g % 2) * QUARTER, QUARTER)
        return total[o, pl.ds(first, QUARTER)]

    def span(k):
        return slice(k * QUARTER, (k + 1) * QUARTER)

    def sib_sum(k):
        at = mod8(z + offsets[k])
        return remote(sib_out.at[at], sib_in.at[at], zr_s.at[k], zr_r.at[k], sibling)

    def sib_send(*which):
        for k in which:
            at = mod8(z + offsets[k])
            for q in range(4):
                sib_out[at, span(q)] = some_rows(at * 2 + 1 - core, q).astype(BF16)
            sib_sum(k).start()

    sib_send(0, 1, 2)

    def chip_sum(k, q):
        at = mod8(z + offsets[k])
        return some_rows(at * 2 + core, q) + sib_in[at, span(q)].astype(F32)

    def ring_copy(j, i, q):
        at = 8 + (j * 2 + i) * 4 + q
        return remote(
            ring_out.at[j, i, q], ring_in.at[j, i, q], zr_s.at[at], zr_r.at[at], dev_z(dirs[i])
        )

    sib_sum(0).wait()
    for q in range(2):
        for i in range(2):
            ring_out[0, i, 2 * i + q] = chip_sum(0, 2 * i + q).astype(BF16)
            ring_copy(0, i, 2 * i + q).start()
    sib_send(3, 4)
    for j in (1, 2, 3):
        for i in range(2):
            sib_sum(2 * j - 1 + i).wait()
        for turn_of in range(4):
            for i in range(2):
                q = (2 * (1 - i) + turn_of) % 4
                here = chip_sum(2 * j - 1 + i, q)
                if j > 1 or q // 2 == i:
                    ring_copy(j - 1, i, q).wait()
                    here += ring_in[j - 1, i, q].astype(F32)
                ring_out[j, i, q] = here.astype(BF16)
                ring_copy(j, i, q).start()
        if j < 3:
            sib_send(*((5, 6), (7,))[j - 1])
    sib_sum(7).wait()
    for q in (2, 0, 3, 1):
        here = chip_sum(7, q) + act[span(q)].astype(F32)
        for i in range(2):
            ring_copy(3, i, q).wait()
            here += ring_in[3, i, q].astype(F32)
        out[span(q)] = here.astype(BF16)


def per_device(activations, ln_gain, segments, w_query, w_key_value, w_gate, w_up, w_out, w_down):
    vmem = pl.BlockSpec(memory_space=pltpu.VMEM)
    far = pl.BlockSpec(memory_space=pltpu.HBM)
    dma = pltpu.SemaphoreType.DMA
    scratch = [
        pltpu.VMEM((ROWS, FEATS), BF16),
        pltpu.VMEM((FEATS,), F32),
        pltpu.VMEM((1, TOKENS), jnp.int32),
        pltpu.VMEM((STEPS, FEATS, 2 * WIDE), BF16),
        pltpu.VMEM((UNITS, WIDE, FEATS), BF16),
        pltpu.VMEM((FEATS, 512), BF16),
        pltpu.VMEM((2, 2, ROWS, 128), F32),
        pltpu.VMEM((2, 8, 128), F32),
        pltpu.VMEM((2, 3, 8, 128), F32),
        pltpu.VMEM((4, 8, 128), F32),
        pltpu.VMEM((RING, 2, 8, 128), F32),
        pltpu.VMEM((GROUP, ROWS, FEATS), BF16),
        pltpu.VMEM((GROUP, ROWS, FEATS), BF16),
        pltpu.VMEM((4, ROWS, 128), BF16),
        pltpu.VMEM((2, 3, ROWS, 128), BF16),
        pltpu.VMEM((ROWS, 128), BF16),
        pltpu.VMEM((4, ROWS, 128), BF16),
        pltpu.VMEM((3, ROWS, HEAD), BF16),
        pltpu.VMEM((GROUP, ROWS, 512), BF16),
        pltpu.VMEM((STEPS, 2, GROUP, QUARTERS, QUARTER, WIDE), BF16),
        pltpu.VMEM((STEPS, 2, 2, 4, QUARTERS, QUARTER, WIDE), BF16),
        pltpu.VMEM((STEPS, 2, 2, 2, QUARTERS, QUARTER, WIDE), BF16),
        pltpu.VMEM((STEPS, 2, SIDE * QUARTERS, QUARTER, WIDE), BF16),
        pltpu.VMEM((STEPS, 2, 2, QUARTERS, QUARTER, WIDE), BF16),
        pltpu.VMEM((STEPS, 2, 2, 2, QUARTER, WIDE), BF16),
        pltpu.VMEM((UNITS // 2, 2, SIDE, SIDE, 2, HALF, WIDE), BF16),
        pltpu.VMEM((2, GROUP * HALF, FEATS), F32),
        pltpu.VMEM((RING, ROWS, FEATS), BF16),
        pltpu.VMEM((RING, ROWS, FEATS), BF16),
        pltpu.VMEM((4, 2, 4, QUARTER, FEATS), BF16),
        pltpu.VMEM((4, 2, 4, QUARTER, FEATS), BF16),
        dma((STEPS, 2)),
        dma((UNITS,)),
        dma((14,)),
        dma((7, 3)),
        dma((7, 3)),
        dma((8, 2)),
        dma((8, 2)),
        dma((5, 2)),
        dma((5, 2)),
        dma((EARLY * QUARTERS, 4)),
        dma((EARLY * QUARTERS, 4)),
        dma((8, 2)),
        dma((8, 2)),
        dma((STEPS, 16)),
        dma((STEPS, 16)),
        dma((UNITS, 16)),
        dma((UNITS, 16)),
        dma((40,)),
        dma((40,)),
    ]
    return pl.pallas_call(
        block_kernel,
        out_shape=jax.ShapeDtypeStruct((ROWS, FEATS), BF16),
        in_specs=[far] * 10,
        out_specs=vmem,
        scratch_shapes=scratch,
        compiler_params=pltpu.CompilerParams(
            collective_id=0, has_side_effects=True, vmem_limit_bytes=54784 * 1024
        ),
    )(
        pltpu.with_memory_space_constraint(activations, pltpu.HBM),
        pltpu.with_memory_space_constraint(ln_gain, pltpu.HBM),
        pltpu.with_memory_space_constraint(segments.reshape(1, TOKENS), pltpu.HBM),
        jnp.asarray(tables()),
        w_query,
        w_key_value,
        w_gate,
        w_up,
        w_out,
        w_down,
    )


def solution(mesh):
    placed = (
        P("ffn", "hid"),
        P("hid"),
        P(),
        P("hid", "ffn"),
        P("hid", None),
        P("hid", "ffn"),
        P("hid", "ffn"),
        P("ffn", "hid"),
        P("ffn", "hid"),
    )
    return jax.shard_map(
        per_device, mesh=mesh, in_specs=placed, out_specs=P("ffn", "hid"), check_vma=False
    )
```
